32 devices in a mesh: dp: 4 (over z), seq: 8 (over y, x, core).
Axes of the slice: x: 2, y: 2, z: 4, core: 2. Of those that a mesh axis runs over, the one named last changes fastest.
Arguments:
- tokens: bfloat16 [4, 3072, 512], P('dp', 'seq'), may hold values from -6 to 6
- doc_lengths: int32 [4, 8], P('dp'), may hold values from 3 to 3051, as said below
- cotangent: bfloat16 [4, 3072, 512], P('dp', 'seq'), may hold values from -6 to 6
- norm_gain: bfloat16 [3, 2, 512], replicated, may hold values from 0.099609375 to 1.8984375
- norm_shift: bfloat16 [3, 2, 512], replicated, may hold values from -1.75 to 1.75
- relative_bias: bfloat16 [3, 2, 512], replicated, may hold values from -3 to 3
- attention_in: bfloat16 [512, 3, 2048], replicated, may hold values from -0.25 to 0.25
- attention_out: bfloat16 [512, 3, 512], replicated, may hold values from -1 to 1
- expand_weight: bfloat16 [512, 3, 2048], replicated, may hold values from -0.25 to 0.25
- expand_bias: bfloat16 [3, 2048], replicated, may hold values from -1.75 to 1.75
- contract_weight: bfloat16 [2048, 3, 512], replicated, may hold values from -0.125 to 0.125
- contract_bias: bfloat16 [3, 512], replicated, may hold values from -1.75 to 1.75
- pool_weight: bfloat16 [1536, 512], replicated, may hold values from -0.15625 to 0.15625
- pool_bias: bfloat16 [512], replicated, may hold values from -1.75 to 1.75
- upsample_weight: bfloat16 [512, 1536], replicated, may hold values from -0.25 to 0.25
- upsample_bias: bfloat16 [1536], replicated, may hold values from -1.75 to 1.75
Outputs:
- output: bfloat16 [4, 3072, 512], P('dp', 'seq')
- tokens_grad: bfloat16 [4, 3072, 512], P('dp', 'seq')
- norm_gain_grad: float32 [3, 2, 512], replicated
- norm_shift_grad: float32 [3, 2, 512], replicated
- relative_bias_grad: float32 [3, 2, 512], replicated
- attention_in_grad: float32 [512, 3, 2048], P('seq')
- attention_out_grad: float32 [512, 3, 512], P('seq')
- expand_weight_grad: float32 [512, 3, 2048], P('seq')
- expand_bias_grad: float32 [3, 2048], replicated
- contract_weight_grad: float32 [2048, 3, 512], P('seq')
- contract_bias_grad: float32 [3, 512], replicated
- pool_weight_grad: float32 [1536, 512], P('seq')
- pool_bias_grad: float32 [512], replicated
- upsample_weight_grad: float32 [512, 1536], P('seq')
- upsample_bias_grad: float32 [1536], replicated
- rms: float32 [3], replicated
The draws below stay inside these ranges and needn't reach their ends.
Inputs may be any that keep to these rules, and one draw needn't show every extreme that they name: `doc_lengths`: in each row the 8 lengths are multiples of 3 that sum to 3072. One of them, neither the first nor the last and at a place drawn from the seed, starts among the first 384 places and ends among the last 384; every other one is at most 3 * (16) long. In one row, drawn from the seed, every other one is 3 long.
All inputs are finite; a program needn't handle non-finite values.
Results may differ from the reference program's by a relative error of at most 0.023.
Values may be sent and summed in bfloat16 or wider, within the bound.
No kernel may reach another device: no remote copies, remote signals or barrier semaphores. Data moves between devices by JAX's collectives and lax.ppermute only.
A program may use at most 320 MiB of HBM per device.

```python
import jax
import jax.numpy as jnp
from jax import lax

D = 512
FF = 2048
HEADS = 8
HD = 64
WIN = 256
QBLK = 384
DOCS = 8
TOK_DEV = 384
ROW = 3072
BATCH = 4


def draw_doc_lengths(key, part):
    key = jax.random.fold_in(key, 11)
    short_key, place_key, row_key = jax.random.split(key, 3)
    longest_short = TOK_DEV // (3 * DOCS)
    shorter = 3 * jax.random.randint(short_key, (BATCH, DOCS), 1, longest_short + 1)
    special_row = jax.random.randint(row_key, (), 0, BATCH)
    shorter = jnp.where(jnp.arange(BATCH)[:, None] == special_row, 3, shorter)
    chosen = jax.random.randint(place_key, (BATCH, 1), 1, DOCS - 1)
    column = jnp.arange(DOCS)[None, :]
    others = jnp.sum(jnp.where(column == chosen, 0, shorter), axis=1, keepdims=True)
    return jnp.where(column == chosen, ROW - others, shorter).astype(jnp.int32)


def block_levels(key, extent, cuts, low, top_value):
    def one(position, blocks):
        heights = jax.random.uniform(jax.random.fold_in(jax.random.fold_in(key, 6), position), (blocks,), jnp.float32, low / len(cuts), top_value / len(cuts))
        return jnp.repeat(jnp.exp(heights), extent[position] // blocks).reshape((-1,) + (1,) * (len(extent) - position - 1))

    level = one(*cuts[0])
    for cut in cuts[1:]:
        level = level * one(*cut)
    return level


def noise(rng, extent, width, limit, pieces=(), kind=jnp.bfloat16):
    gain = block_levels(rng, extent, pieces, -0.22, 0.18) if pieces else 1.0
    entries = jax.random.normal(rng, extent, jnp.float32) * width * gain
    return jnp.minimum(jnp.maximum(entries, -limit), limit).astype(kind)


def setup_inputs(seed: int = 0) -> dict:
    splits = jax.random.split(jax.random.key(seed), 17)
    return {
        "tokens": noise(splits[0], (BATCH, ROW, D), 1.0, 6.0, ((0, 4), (1, 8))),
        "doc_lengths": draw_doc_lengths(jax.random.fold_in(splits[16], 71), 0),
        "cotangent": noise(splits[2], (BATCH, ROW, D), 1.0, 6.0, ((0, 4), (1, 8))),
        "norm_gain": jnp.clip(1.0 + 0.18 * jax.random.normal(splits[3], (3, 2, D), jnp.float32), 0.099609375, 1.8984375).astype(jnp.bfloat16),
        "norm_shift": noise(splits[4], (3, 2, D), 0.3, 1.75),
        "relative_bias": noise(splits[5], (3, 2, D), 0.5, 3.0),
        "attention_in": noise(splits[6], (D, 3, 4 * D), D ** -0.5, 0.25),
        "attention_out": noise(splits[7], (D, 3, D), (D // 16) ** -0.5, 1.0),
        "expand_weight": noise(splits[8], (D, 3, FF), D ** -0.5, 0.25),
        "expand_bias": noise(splits[9], (3, FF), 0.3, 1.75),
        "contract_weight": noise(splits[10], (FF, 3, D), FF ** -0.5, 0.125),
        "contract_bias": noise(splits[11], (3, D), 0.3, 1.75),
        "pool_weight": noise(splits[12], (3 * D, D), (3 * D) ** -0.5, 0.15625),
        "pool_bias": noise(splits[13], (D,), 0.3, 1.75),
        "upsample_weight": noise(splits[14], (D, 3 * D), D ** -0.5, 0.25),
        "upsample_bias": noise(splits[15], (3 * D,), 0.3, 1.75),
    }


epsilon = 1e-05
masked_score = -1e+30

@jax.custom_vjp
def low(v):
    return lax.optimization_barrier(v.astype(jnp.bfloat16)).astype(jnp.float32)

@jax.custom_vjp
def low_back(v):
    return v

def low_keep(v):
    return (low(v), None)

def low_pass(kept, grad):
    return (grad,)

def back_keep(v):
    return (v, None)

def back_low(kept, grad):
    return (low(grad),)
low.defvjp(low_keep, low_pass)
low_back.defvjp(back_keep, back_low)

def matmul(first_matrix, second_matrix):
    return jnp.dot(first_matrix, second_matrix, precision=lax.Precision.HIGHEST, preferred_element_type=jnp.float32)

def layer_norm(values, scaling, offset):
    centre = values - lax.optimization_barrier(jnp.mean(values, axis=-1, keepdims=True))
    spread = lax.optimization_barrier(jnp.mean(centre * centre, axis=-1, keepdims=True))
    return centre * lax.rsqrt(spread + epsilon) * scaling + offset

def sinusoid(distance):
    halfway = D // 2
    frequency = jnp.power(10000.0, -2.0 * jnp.arange(halfway, dtype=jnp.float32) / D)
    phases = distance[:, None] * frequency[None, :]
    return jnp.concatenate([jnp.sin(phases), jnp.cos(phases)], axis=1)

def skewed(table_scores, key_count):
    head_count, query_count, table_length = table_scores.shape
    flattened = table_scores.reshape(head_count, query_count * table_length)
    flattened = flattened[:, query_count - 1:query_count - 1 + query_count * (table_length - 1)]
    return flattened.reshape(head_count, query_count, table_length - 1)[:, :, :key_count]

def split_into_heads(matrix):
    return matrix.reshape(matrix.shape[0], HEADS, matrix.shape[1] // HEADS)

def document_of(places, lengths):
    ending = jnp.cumsum(lengths)
    return lax.optimization_barrier(jnp.sum((places[:, None] >= ending[None, :]).astype(jnp.int32), axis=1))

def window_visible(query_place, key_place, lengths):
    behind = query_place[:, None] - key_place[None, :]
    same_document = document_of(query_place, lengths)[:, None] == document_of(key_place, lengths)[None, :]
    return (key_place[None, :] >= 0) & (behind >= 0) & (behind <= WIN) & same_document

def pooled_visible(query_place, key_place, lengths):
    same_document = document_of(3 * query_place, lengths)[:, None] == document_of(3 * key_place, lengths)[None, :]
    return (key_place[None, :] <= query_place[:, None]) & same_document

def softmax_attend(query_content, query_token_position, key_row_matrix, value_rows, lookup_table_rows, visible):
    content = jnp.einsum('qhd,khd->hqk', split_into_heads(query_content), split_into_heads(key_row_matrix), precision=lax.Precision.HIGHEST)
    token_position = jnp.einsum('eay,cay->aec', split_into_heads(query_token_position), split_into_heads(lookup_table_rows), precision=lax.Precision.HIGHEST)
    scores = low_back((content + skewed(token_position, key_row_matrix.shape[0])) * HD ** (-0.5))
    scores = jnp.where(visible[None], scores, masked_score)
    weights = low(jax.nn.softmax(scores, axis=-1))
    mixed_rows = jnp.einsum('hqk,khd->qhd', weights, split_into_heads(value_rows), precision=lax.Precision.HIGHEST)
    return mixed_rows.reshape(mixed_rows.shape[0], D)

def window_attention(lengths):

    def attention(query_content, query_token_position, key_row_matrix, value_rows, position_weight):
        row_total = key_row_matrix.shape[0]
        padded_keys = jnp.concatenate([jnp.zeros((WIN, D), jnp.float32), key_row_matrix], axis=0)
        padded_values = jnp.concatenate([jnp.zeros((WIN, D), jnp.float32), value_rows], axis=0)
        distance = (QBLK - 1 + WIN - jnp.arange(2 * QBLK + WIN - 1, dtype=jnp.int32)).astype(jnp.float32)
        embed_rows = low(sinusoid(distance))

        def one_block(block_index):
            first_row = (block_index * QBLK).astype(jnp.int32)
            lookup_table_rows = low(low_back(matmul(embed_rows, position_weight)))
            content = lax.dynamic_slice_in_dim(query_content, first_row, QBLK, 0)
            token_position = lax.dynamic_slice_in_dim(query_token_position, first_row, QBLK, 0)
            keyset = lax.dynamic_slice_in_dim(padded_keys, first_row, QBLK + WIN, 0)
            valueset = lax.dynamic_slice_in_dim(padded_values, first_row, QBLK + WIN, 0)
            query_place = first_row + jnp.arange(QBLK, dtype=jnp.int32)
            key_place = first_row - WIN + jnp.arange(QBLK + WIN, dtype=jnp.int32)
            visible = window_visible(query_place, key_place, lengths)
            return softmax_attend(content, token_position, keyset, valueset, lookup_table_rows, visible)
        blocks = lax.map(jax.checkpoint(one_block), jnp.arange(row_total // QBLK, dtype=jnp.int32))
        return blocks.reshape(row_total, D)
    return attention

def pooled_attention(lengths):

    def attention(query_content, query_token_position, key_row_matrix, value_rows, position_weight):
        pooled_total = key_row_matrix.shape[0]
        per_block = TOK_DEV // 3
        key_place = jnp.arange(pooled_total, dtype=jnp.int32)

        def one_block(block_index):
            first_row = (block_index * per_block).astype(jnp.int32)
            distance = (first_row + per_block - 1 - jnp.arange(per_block + pooled_total - 1, dtype=jnp.int32)).astype(jnp.float32)
            lookup_table_rows = low(low_back(matmul(low(sinusoid(distance)), position_weight)))
            content = lax.dynamic_slice_in_dim(query_content, first_row, per_block, 0)
            token_position = lax.dynamic_slice_in_dim(query_token_position, first_row, per_block, 0)
            query_place = first_row + jnp.arange(per_block, dtype=jnp.int32)
            visible = pooled_visible(query_place, key_place, lengths)
            return softmax_attend(content, token_position, key_row_matrix, value_rows, lookup_table_rows, visible)
        blocks = lax.map(jax.checkpoint(one_block), jnp.arange(pooled_total // per_block, dtype=jnp.int32))
        return blocks.reshape(pooled_total, D)
    return attention

def block(inputs, layer_index, layers, attention):
    norm_gain, norm_shift, relative_bias, attention_in, attention_out, expand_weight, expand_bias, contract_weight, contract_bias = layers
    layer_in = attention_in[:, layer_index, :]
    normed = low(layer_norm(inputs, norm_gain[layer_index, 0], norm_shift[layer_index, 0]))
    queries = low_back(matmul(normed, layer_in[:, :D]))
    key_row_matrix = low(low_back(matmul(normed, layer_in[:, D:2 * D])))
    value_rows = low(low_back(matmul(normed, layer_in[:, 2 * D:3 * D])))
    query_content = low(queries + relative_bias[layer_index, 0])
    query_token_position = low(queries + relative_bias[layer_index, 1])
    mixed_rows = low(low_back(attention(query_content, query_token_position, key_row_matrix, value_rows, layer_in[:, 3 * D:])))
    middle = inputs + low_back(matmul(mixed_rows, attention_out[:, layer_index, :]))
    normed_two = low(layer_norm(middle, norm_gain[layer_index, 1], norm_shift[layer_index, 1]))
    expanded = low_back(matmul(normed_two, expand_weight[:, layer_index, :]) + expand_bias[layer_index])
    activated = low(jax.nn.gelu(expanded, approximate=False))
    return middle + low_back(matmul(activated, contract_weight[:, layer_index, :]) + contract_bias[layer_index])

def forward_row(inputs, lengths, weights):
    layers = weights[:9]
    pool_weight, pool_bias, upsample_weight, upsample_bias = weights[9:]
    row_total = inputs.shape[0]
    first_out = block(inputs, 0, layers, window_attention(lengths))
    token_place = jnp.arange(row_total, dtype=jnp.int32)
    keep_mask = (token_place >= 2) & (document_of(token_place - 2, lengths) == document_of(token_place, lengths))
    shifted = jnp.concatenate([jnp.zeros((2, D), jnp.float32), low(first_out)[:row_total - 2]], axis=0)
    shifted = jnp.where(keep_mask[:, None], shifted, 0.0)
    pooled = low_back(matmul(shifted.reshape(row_total // 3, 3 * D), pool_weight) + pool_bias)
    short_out = block(pooled, 1, layers, pooled_attention(lengths))
    upsampled = low_back(matmul(low(short_out), upsample_weight) + upsample_bias).reshape(row_total, D)
    final = block(first_out + upsampled, 2, layers, window_attention(lengths))
    squares = jnp.stack([jnp.sum(first_out * first_out), jnp.sum(short_out * short_out), jnp.sum(final * final)])
    return (final, squares)

def reference(tokens, doc_lengths, cotangent, norm_gain, norm_shift, relative_bias, attention_in, attention_out, expand_weight, expand_bias, contract_weight, contract_bias, pool_weight, pool_bias, upsample_weight, upsample_bias):
    params = tuple((weight.astype(jnp.float32) for weight in (norm_gain, norm_shift, relative_bias, attention_in, attention_out, expand_weight, expand_bias, contract_weight, contract_bias, pool_weight, pool_bias, upsample_weight, upsample_bias)))

    def row_step(carried, batch_item):
        summed, squares_total = carried
        inputs, lengths, grad_out = batch_item
        result, pull_back, squares = jax.vjp(lambda values, *weights: forward_row(values, lengths, weights), inputs.astype(jnp.float32), *params, has_aux=True)
        gradients = pull_back(grad_out.astype(jnp.float32))
        summed = tuple((accumulated + incoming for accumulated, incoming in zip(summed, gradients[1:])))
        return ((summed, squares_total + squares), (result.astype(jnp.bfloat16), gradients[0].astype(jnp.bfloat16)))
    initial = (tuple((jnp.zeros_like(weight) for weight in params)), jnp.zeros((3,), jnp.float32))
    (summed, squares_total), (outputs, input_grads) = lax.scan(row_step, initial, (tokens, doc_lengths, cotangent))
    counts = jnp.array([BATCH * ROW * D, BATCH * (ROW // 3) * D, BATCH * ROW * D], jnp.float32)
    rms = jnp.sqrt(squares_total / counts)
    return (outputs, input_grads, summed[0], summed[1], summed[2], summed[3], summed[4], summed[5], summed[6], summed[7], summed[8], summed[9], summed[10], summed[11], summed[12], rms)
```

```python
from functools import partial

import jax
import jax.numpy as jnp
from jax import lax
from jax.experimental import pallas as pl
from jax.experimental.pallas import tpu as pltpu
from jax.sharding import PartitionSpec as P

D = 512
HEADS = 8
HD = 64
WIN = 256
QBLK = 384
DOCS = 8
VMEM_BYTES = 48 * 2**20
epsilon = 1e-05


LANES = 128
PAIR = 2 * HD
MASKED = -1e30


def nt(first, second):
    return lax.dot_general(
        first, second, (((1,), (1,)), ((), ())), preferred_element_type=jnp.float32
    )


def nn(first, second):
    return lax.dot_general(
        first, second, (((1,), (0,)), ((), ())), preferred_element_type=jnp.float32
    )


def tn(first, second):
    return lax.dot_general(
        first, second, (((0,), (0,)), ((), ())), preferred_element_type=jnp.float32
    )


def document(places, info):
    total = jnp.zeros(places.shape, jnp.int32)
    for index in range(DOCS):
        total = total + (places >= info[1 + index]).astype(jnp.int32)
    return total


def lanes_and_rows():
    lane = lax.broadcasted_iota(jnp.int32, (LANES, LANES), 1)
    row = lax.broadcasted_iota(jnp.int32, (LANES, LANES), 0)
    return lane, row


def turned(values, index):
    return [
        jnp.take_along_axis(values[:, m * LANES : (m + 1) * LANES], index, axis=1)
        for m in range(values.shape[1] // LANES)
    ]


def skew_window(table):
    lane, row = lanes_and_rows()
    blocks = turned(table, (lane - row + LANES) % LANES)
    out = [blocks[0]] + [
        jnp.where(lane >= row, here, before) for before, here in zip(blocks, blocks[1:])
    ]
    return jnp.concatenate(out, axis=1)


def unskew_window(scores):
    lane, row = lanes_and_rows()
    blocks = turned(scores, (lane + row) % LANES)
    blocks.append(jnp.zeros_like(blocks[0]))
    out = [
        jnp.where(lane + row < LANES, here, after) for here, after in zip(blocks, blocks[1:])
    ]
    return jnp.concatenate(out, axis=1)


def skew_pooled(table):
    lane, row = lanes_and_rows()
    here, after = turned(table, (lane + LANES - 1 - row) % LANES)
    return jnp.where(lane <= row, here, after)


def unskew_pooled(scores):
    lane, row = lanes_and_rows()
    (block,) = turned(scores, (lane + row + 1) % LANES)
    zero = jnp.zeros_like(block)
    first = lane + row >= LANES - 1
    return jnp.concatenate([jnp.where(first, block, zero), jnp.where(first, zero, block)], axis=1)


def head_lanes(rows):
    return lax.broadcasted_iota(jnp.int32, (rows, PAIR), 1) // HD


def softmax_rows(scores):
    highest = jnp.max(scores, axis=1, keepdims=True)
    powers = jnp.exp(scores - highest)
    return powers / jnp.sum(powers, axis=1, keepdims=True)


def window_mask(info, part):
    place = info[0] + part * LANES
    row = lax.broadcasted_iota(jnp.int32, (LANES, LANES + WIN), 0)
    column = lax.broadcasted_iota(jnp.int32, (LANES, LANES + WIN), 1)
    behind = row + WIN - column
    query = place + lax.broadcasted_iota(jnp.int32, (LANES, 1), 0)
    key = place - WIN + lax.broadcasted_iota(jnp.int32, (1, LANES + WIN), 1)
    same = document(query, info) == document(key, info)
    return (behind >= 0) & (behind <= WIN) & same & (key >= 0)


def pooled_mask(info, start):
    query = info[0] + lax.broadcasted_iota(jnp.int32, (LANES, 1), 0)
    key = start + lax.broadcasted_iota(jnp.int32, (1, LANES), 1)
    return (key <= query) & (document(3 * query, info) == document(3 * key, info))


def heads_forward(content, position, keys, values, table, visible, skew):
    head = head_lanes(LANES)
    weights, mixed = [], []
    for index in range(2):
        mine = head == index
        score = nt(jnp.where(mine, content, 0), keys)
        place = nt(jnp.where(mine, position, 0), table)
        score = jnp.where(visible, (score + skew(place)) * HD**-0.5, MASKED)
        weight = softmax_rows(score).astype(jnp.bfloat16)
        weights.append(weight)
        mixed.append(nn(weight, values))
    return weights, jnp.where(head == 0, mixed[0], mixed[1])


def heads_backward(content, position, keys, values, table, weights, grad, unskew):
    head = head_lanes(LANES)
    scores, places, contents, positions, grads, to_content, to_position = ([] for _ in range(7))
    for index in range(2):
        mine = head == index
        grads.append(jnp.where(mine, grad, 0))
        contents.append(jnp.where(mine, content, 0))
        positions.append(jnp.where(mine, position, 0))
        grad_weight = nt(grads[index], values)
        weight = weights[index].astype(jnp.float32)
        delta = jnp.sum(weight * grad_weight, axis=1, keepdims=True)
        score = (weight * (grad_weight - delta)).astype(jnp.bfloat16)
        place = unskew(score.astype(jnp.float32)).astype(jnp.bfloat16)
        scores.append(score)
        places.append(place)
        to_content.append(nn(score, keys))
        to_position.append(nn(place, table))
    scale = HD**-0.5
    grad_content = jnp.where(head == 0, to_content[0], to_content[1]) * scale
    grad_position = jnp.where(head == 0, to_position[0], to_position[1]) * scale

    def summed(first, second):
        return tn(jnp.concatenate(first, axis=0), jnp.concatenate(second, axis=0))

    grad_keys = summed(scores, contents) * scale
    grad_values = summed(weights, grads)
    grad_table = summed(places, positions) * scale
    return grad_content, grad_position, grad_keys, grad_values, grad_table


def window_forward_kernel(
    info, content, position, keys, values, table, mixed_ref, weights_ref
):
    for part in range(QBLK // LANES):
        rows = pl.ds(part * LANES, LANES)
        seen = pl.ds(part * LANES, LANES + WIN)
        weights, mixed = heads_forward(
            content[rows, :],
            position[rows, :],
            keys[seen, :],
            values[seen, :],
            table[...],
            window_mask(info, part),
            skew_window,
        )
        for index in range(2):
            weights_ref[index, part] = weights[index]
        mixed_ref[rows, :] = mixed.astype(jnp.bfloat16)


def window_backward_kernel(
    content,
    position,
    keys,
    values,
    table,
    weights,
    grad,
    dq_ref,
    bias_ref,
    dk_ref,
    dv_ref,
    dt_ref,
):
    dk_ref[...] = jnp.zeros_like(dk_ref)
    dv_ref[...] = jnp.zeros_like(dv_ref)
    total = jnp.zeros(table.shape, jnp.float32)
    bias = jnp.zeros((2, PAIR), jnp.float32)
    for part in range(QBLK // LANES):
        rows = pl.ds(part * LANES, LANES)
        seen = pl.ds(part * LANES, LANES + WIN)
        grad_content, grad_position, grad_keys, grad_values, grad_table = heads_backward(
            content[rows, :],
            position[rows, :],
            keys[seen, :],
            values[seen, :],
            table[...],
            [weights[0, part], weights[1, part]],
            grad[rows, :],
            unskew_window,
        )
        dq_ref[rows, :] = (grad_content + grad_position).astype(jnp.bfloat16)
        bias = bias + jnp.concatenate(
            [
                jnp.sum(grad_content, axis=0, keepdims=True),
                jnp.sum(grad_position, axis=0, keepdims=True),
            ],
            axis=0,
        )
        dk_ref[seen, :] += grad_keys
        dv_ref[seen, :] += grad_values
        total = total + grad_table
    bias_ref[...] = bias
    dt_ref[...] = total.astype(dt_ref.dtype)


def table_rows(order, block, count):
    start = order[block] + count - 1 - order[count]
    return pl.ds(pl.multiple_of(LANES * jnp.minimum(start, count - 1), LANES), 2 * LANES)


def pooled_forward_kernel(
    info, order, content, position, keys, values, table, mixed_ref, weights_ref
):
    head = head_lanes(LANES)
    count = keys.shape[0] // LANES
    mixed = []
    visible = [pooled_mask(info, LANES * order[block]) for block in range(count)]
    for index in range(2):
        mine = head == index
        here = jnp.where(mine, content[...], 0)
        there = jnp.where(mine, position[...], 0)
        scores = []
        for block in range(count):
            score = nt(here, keys[pl.ds(block * LANES, LANES), :])
            place = nt(there, table[table_rows(order, block, count), :])
            score = (score + skew_pooled(place)) * HD**-0.5
            scores.append(jnp.where(visible[block], score, MASKED))
        weight = softmax_rows(jnp.concatenate(scores, axis=1)).astype(jnp.bfloat16)
        weights_ref[index] = weight
        mixed.append(nn(weight, values[...]))
    mixed_ref[...] = jnp.where(head == 0, mixed[0], mixed[1]).astype(jnp.bfloat16)


def pooled_backward_kernel(
    order,
    content,
    position,
    keys,
    values,
    table,
    weights,
    grad,
    dq_ref,
    bias_ref,
    dk_ref,
    dv_ref,
    dt_ref,
    sum_ref,
):
    head = head_lanes(LANES)
    count = keys.shape[0] // LANES
    scale = HD**-0.5
    sum_ref[...] = jnp.zeros_like(sum_ref)
    contents, grads, positions, scores, to_content, to_position = ([] for _ in range(6))
    for index in range(2):
        mine = head == index
        contents.append(jnp.where(mine, content[...], 0))
        positions.append(jnp.where(mine, position[...], 0))
        grads.append(jnp.where(mine, grad[...], 0))
        grad_weight = nt(grads[index], values[...])
        weight = weights[index].astype(jnp.float32)
        delta = jnp.sum(weight * grad_weight, axis=1, keepdims=True)
        score = weight * (grad_weight - delta)
        scores.append(score.astype(jnp.bfloat16))
        to_content.append(nn(scores[index], keys[...]))
    positions = jnp.concatenate(positions, axis=0)
    to_position = [jnp.zeros((LANES, PAIR), jnp.float32) for _ in range(2)]
    for block in range(count):
        rows = table_rows(order, block, count)
        places = []
        for index in range(2):
            score = scores[index][:, block * LANES : (block + 1) * LANES]
            place = unskew_pooled(score.astype(jnp.float32)).astype(jnp.bfloat16)
            to_position[index] = to_position[index] + nn(place, table[rows, :])
            places.append(place)
        sum_ref[rows, :] += tn(jnp.concatenate(places, axis=0), positions)
    grad_content = jnp.where(head == 0, to_content[0], to_content[1]) * scale
    grad_position = jnp.where(head == 0, to_position[0], to_position[1]) * scale
    grad_keys = tn(jnp.concatenate(scores, axis=0), jnp.concatenate(contents, axis=0)) * scale
    grad_values = tn(
        jnp.concatenate([weights[0], weights[1]], axis=0), jnp.concatenate(grads, axis=0)
    )
    dq_ref[...] = (grad_content + grad_position).astype(jnp.bfloat16)
    bias_ref[...] = jnp.concatenate(
        [
            jnp.sum(grad_content, axis=0, keepdims=True),
            jnp.sum(grad_position, axis=0, keepdims=True),
        ],
        axis=0,
    )
    dk_ref[...] = grad_keys.astype(dk_ref.dtype)
    dv_ref[...] = grad_values.astype(dv_ref.dtype)
    dt_ref[...] = (sum_ref[...] * scale).astype(dt_ref.dtype)


def by_pair(array):
    return pl.BlockSpec((array.shape[0], PAIR), lambda pair: (0, pair))


def weights_block(shape):
    return pl.BlockSpec((2,) + shape[1:], lambda pair: (pair,) + (0,) * (len(shape) - 1))


def attention_forward(kernel, scalars, operands, weights_shape):
    content = operands[0]
    return pl.pallas_call(
        kernel,
        grid=(HEADS // 2,),
        in_specs=[pl.BlockSpec(memory_space=pltpu.SMEM)] * len(scalars)
        + [by_pair(a) for a in operands],
        out_specs=[by_pair(content), weights_block(weights_shape)],
        out_shape=[
            jax.ShapeDtypeStruct(content.shape, jnp.bfloat16),
            jax.ShapeDtypeStruct(weights_shape, jnp.bfloat16),
        ],
        compiler_params=pltpu.CompilerParams(vmem_limit_bytes=VMEM_BYTES),
    )(*scalars, *operands)


def attention_backward(kernel, scalars, operands, weights, grad, types, scratch=()):
    content, _, keys, values, table = operands
    bias = jax.ShapeDtypeStruct((2, D), jnp.float32)
    summed = [jax.ShapeDtypeStruct(a.shape, t) for a, t in zip((keys, values, table), types)]
    return pl.pallas_call(
        kernel,
        grid=(HEADS // 2,),
        in_specs=[pl.BlockSpec(memory_space=pltpu.SMEM)] * len(scalars)
        + [by_pair(a) for a in operands]
        + [weights_block(weights.shape), by_pair(grad)],
        out_specs=[by_pair(content), by_pair(bias)] + [by_pair(a) for a in summed],
        out_shape=[jax.ShapeDtypeStruct(content.shape, jnp.bfloat16), bias] + summed,
        scratch_shapes=scratch,
        compiler_params=pltpu.CompilerParams(vmem_limit_bytes=VMEM_BYTES),
    )(*scalars, *operands, weights, grad)


def crossed(block, axis, bit):
    count = lax.axis_size(axis)
    return lax.ppermute(block, axis, [(index, index ^ bit) for index in range(count)])


def both(low, high, bit):
    return jnp.where(bit, high, low), jnp.where(bit, low, high)


def halves(matrix, bit):
    middle = matrix.shape[1] // 2
    return both(matrix[:, :middle], matrix[:, middle:], bit)


def rounded_sum(*terms):
    return sum(term.astype(jnp.float32) for term in terms).astype(jnp.bfloat16)


def gather_pooled(rows):
    half = rows.shape[0] // 2
    from_x = crossed(rows, "seq", 2)
    from_y = crossed(rows, "seq", 4)
    from_core = crossed(rows, "seq", 1)
    first = crossed(from_x[:half], "seq", 4)
    second = crossed(from_y[half:], "seq", 2)
    core_x = crossed(from_x, "seq", 1)
    core_y = crossed(from_y, "seq", 1)
    opposite = jnp.concatenate([first, second], axis=0)
    core_opposite = crossed(opposite, "seq", 1)
    return jnp.concatenate(
        [rows, from_core, from_x, core_x, from_y, core_y, opposite, core_opposite], axis=0
    )


def scatter_pooled(rows):
    count = rows.shape[0] // 8
    blocks = rows.reshape(4, 2, count, rows.shape[1])
    arrived = crossed(blocks[:, 1], "seq", 1)
    blocks = rounded_sum(blocks[:, 0], arrived)
    middle = rows.shape[1] // 2
    left, right = blocks[:, :, :middle], blocks[:, :, middle:]
    left_arrived = crossed(jnp.stack([left[1], left[3]]), "seq", 2)
    right_arrived = crossed(right[2:], "seq", 4)
    left_next = crossed(rounded_sum(left[2], left_arrived[1]), "seq", 4)
    right_next = crossed(rounded_sum(right[1], right_arrived[1]), "seq", 2)
    sums = [
        left[0].astype(jnp.float32)
        + left_arrived[0].astype(jnp.float32)
        + left_next.astype(jnp.float32),
        right[0].astype(jnp.float32)
        + right_arrived[0].astype(jnp.float32)
        + right_next.astype(jnp.float32),
    ]
    return jnp.concatenate(sums, axis=1)


def piece_lanes(piece):
    features, columns = piece[0].shape[1], piece[2].shape[1] * 2
    return features // D * (columns // 4)


def pair_kernel(count, place, *refs):
    inputs, (keep_one, send_one, keep_two, send_two) = refs[: 4 * count], refs[4 * count :]
    offset = 0
    for index in range(count):
        own_x, pair_x, own_dy, pair_dy = inputs[4 * index : 4 * index + 4]
        height = own_x.shape[1] // 4
        quarter = own_dy.shape[1] // 2
        groups = height // LANES
        for block in range(4):
            columns = pl.ds(pl.multiple_of((place[0] ^ block) * height, LANES), height)
            total = tn(own_x[:, columns], own_dy[...]) + tn(pair_x[:, columns], pair_dy[...])
            total = total.astype(jnp.bfloat16)
            first = (keep_one, send_one)[block % 2]
            second = (keep_two, send_two)[block // 2]
            for out, slot, lanes in (
                (first, block // 2, total[:, :quarter]),
                (second, block % 2, total[:, quarter:]),
            ):
                if groups == 1:
                    out[slot, :, offset : offset + quarter] = lanes
                else:
                    for group in range(groups):
                        start = offset + quarter * group
                        low = HD * group
                        high = height // 2 + low
                        out[slot, :HD, start : start + quarter] = lanes[low : low + HD]
                        out[slot, HD:, start : start + quarter] = lanes[high : high + HD]
        offset += groups * quarter


def pair_gradients(place, pieces):
    lanes = sum(piece_lanes(piece) for piece in pieces)
    out = jax.ShapeDtypeStruct((2, LANES, lanes), jnp.bfloat16)
    operands = [array for piece in pieces for array in piece]
    return pl.pallas_call(
        partial(pair_kernel, len(pieces)),
        in_specs=[pl.BlockSpec(memory_space=pltpu.SMEM)]
        + [pl.BlockSpec(memory_space=pltpu.VMEM)] * len(operands),
        out_specs=[pl.BlockSpec(memory_space=pltpu.VMEM)] * 4,
        out_shape=[out] * 4,
        compiler_params=pltpu.CompilerParams(vmem_limit_bytes=VMEM_BYTES),
    )(place, *operands)


def reduced(pieces, place, core, depth):
    keep_one, send_one, keep_two, send_two = pair_gradients(place, pieces)
    one = crossed(send_one, "seq", 2)
    two = crossed(send_two, "seq", 4)
    next_one = crossed(rounded_sum(keep_one[1], one[1]), "seq", 4)
    next_two = crossed(rounded_sum(keep_two[1], two[1]), "seq", 2)
    first = rounded_sum(keep_one[0], one[0], next_one)
    second = rounded_sum(keep_two[0], two[0], next_two)
    keep, send = both(first, second, depth)
    keep = rounded_sum(keep, crossed(send, "dp", 1))
    keep = rounded_sum(keep, crossed(keep, "dp", 2))
    other = crossed(keep, "dp", 1)
    first, second = both(keep, other, depth)
    share = jnp.concatenate([first, second], axis=1)
    keep, send = both(share[:HD], share[HD:], core)
    return both(keep, crossed(send, "seq", 1), core)


def final_kernel(plan, *refs):
    groups = len(plan)
    buffers, outs = refs[: 2 * groups], refs[2 * groups :]
    for index, pieces in enumerate(plan):
        lanes = buffers[2 * index].shape[1] // 2
        offset = 0
        for out_index, layer, first_column, columns, height in pieces:
            out = outs[out_index]
            quarter = columns // 4
            for group in range(height // HD):
                rows = pl.ds(HD * group, HD)
                for part in range(4):
                    buffer = buffers[2 * index + part // 2]
                    start = (part % 2) * lanes + offset
                    value = buffer[:, start : start + quarter].astype(jnp.float32)
                    begin = first_column + part * quarter
                    if layer is None:
                        out[rows, begin : begin + quarter] = value
                    else:
                        out[layer, rows, begin : begin + quarter] = value
                offset += quarter


def final_outputs(plan, buffers, shapes):
    flat = [array for pair in buffers for array in pair]
    return pl.pallas_call(
        partial(final_kernel, plan),
        in_specs=[pl.BlockSpec(memory_space=pltpu.VMEM)] * len(flat),
        out_specs=[pl.BlockSpec(memory_space=pltpu.VMEM)] * len(shapes),
        out_shape=[jax.ShapeDtypeStruct(shape, jnp.float32) for shape in shapes],
        compiler_params=pltpu.CompilerParams(vmem_limit_bytes=VMEM_BYTES),
    )(*flat)


def summed_everywhere(values):
    flat = jnp.concatenate([value.reshape(-1) for value in values])
    size = flat.shape[0]
    rows = -(-size // (8 * LANES)) * 8
    flat = jnp.pad(flat, (0, rows * LANES - size)).reshape(rows, LANES)
    for axis in ("seq", "dp"):
        count = lax.axis_size(axis)
        for bit in range(count.bit_length() - 1):
            flat = flat + crossed(flat, axis, 1 << bit)
    flat = flat.reshape(-1)
    out, start = [], 0
    for value in values:
        out.append(flat[start : start + value.size].reshape(value.shape))
        start += value.size
    return out


def passed_along(block, axis, distance):
    devices = range(lax.axis_size(axis))
    route = [(i - distance, i) for i in devices if i - distance in devices]
    return lax.ppermute(block, axis, route)


def layer_norm(values, scaling, offset):
    centre = values - jnp.mean(values, axis=-1, keepdims=True)
    spread = jnp.mean(centre * centre, axis=-1, keepdims=True)
    return centre * lax.rsqrt(spread + epsilon) * scaling + offset


def sinusoid(distance):
    halfway = D // 2
    frequency = jnp.power(10000.0, -2.0 * jnp.arange(halfway, dtype=jnp.float32) / D)
    phases = distance[:, None] * frequency[None, :]
    return jnp.concatenate([jnp.sin(phases), jnp.cos(phases)], axis=1)


def embedding(first, count):
    distance = first - jnp.arange(count)
    return sinusoid(distance.astype(jnp.float32)).astype(jnp.bfloat16)


def document_of(places, ending):
    return jnp.sum((places[:, None] >= ending[None, :]).astype(jnp.int32), axis=1)


def dot_float(first_matrix, second_matrix):
    return jnp.dot(first_matrix, second_matrix, preferred_element_type=jnp.float32)


def outer_float(first_matrix, second_matrix):
    return jnp.einsum("rc,re->ce", first_matrix, second_matrix, preferred_element_type=jnp.float32)


def dot_back(first_matrix, second_matrix):
    return jnp.einsum("rc,ec->re", first_matrix, second_matrix, preferred_element_type=jnp.float32)


class Window:
    def __init__(self, start, ends, table):
        self.info = jnp.concatenate([start[None], ends]).astype(jnp.int32)
        self.embedded = table

    def forward(self, content, position, keys, values, weight):
        border = passed_along(jnp.stack([keys[-WIN:], values[-WIN:]]), "seq", 1)
        keys_all = jnp.concatenate([border[0], keys], axis=0)
        values_all = jnp.concatenate([border[1], values], axis=0)
        table = dot_float(self.embedded, weight).astype(jnp.bfloat16)
        operands = (content, position, keys_all, values_all, table)
        shape = (HEADS, QBLK // LANES, LANES, LANES + WIN)
        mixed, weights = attention_forward(window_forward_kernel, [self.info], operands, shape)
        return mixed, (operands, weights)

    def backward(self, stored, grad):
        operands, weights = stored
        types = (jnp.float32, jnp.float32, jnp.bfloat16)
        dq, bias, dk, dv, dt = attention_backward(
            window_backward_kernel, [], operands, weights, grad, types
        )
        returned = passed_along(
            jnp.stack([dk[:WIN], dv[:WIN]]).astype(jnp.bfloat16), "seq", -1
        ).astype(jnp.float32)
        rest = QBLK - WIN
        dk = jnp.concatenate([dk[WIN : WIN + rest], dk[WIN + rest :] + returned[0]], axis=0)
        dv = jnp.concatenate([dv[WIN : WIN + rest], dv[WIN + rest :] + returned[1]], axis=0)
        return dq, bias, dk.astype(jnp.bfloat16), dv.astype(jnp.bfloat16), dt


class Pooled:
    def __init__(self, device, count, rows, ends, crossing):
        self.crossing = crossing
        order = jnp.arange(count)
        if crossing:
            order = order ^ device
        self.order = jnp.concatenate([order, device[None]]).astype(jnp.int32)
        self.info = jnp.concatenate([device[None] * rows, ends]).astype(jnp.int32)
        self.embedded = embedding(count * rows - 1, (count + 1) * rows)

    def forward(self, content, position, keys, values, weight):
        both_rows = jnp.concatenate([keys, values], axis=1)
        if self.crossing:
            both_rows = gather_pooled(both_rows)
        else:
            both_rows = lax.all_gather(both_rows, "seq", axis=0, tiled=True)
        table = dot_float(self.embedded, weight).astype(jnp.bfloat16)
        operands = (content, position, both_rows[:, :D], both_rows[:, D:], table)
        shape = (HEADS, LANES, both_rows.shape[0])
        mixed, weights = attention_forward(
            pooled_forward_kernel, [self.info, self.order], operands, shape
        )
        return mixed, (operands, weights)

    def backward(self, stored, grad):
        operands, weights = stored
        types = (jnp.bfloat16,) * 3
        scratch = [pltpu.VMEM((operands[4].shape[0], PAIR), jnp.float32)]
        dq, bias, dk, dv, dt = attention_backward(
            pooled_backward_kernel, [self.order], operands, weights, grad, types, scratch
        )
        joined = jnp.concatenate([dk, dv], axis=1)
        if self.crossing:
            joined = scatter_pooled(joined)
        else:
            joined = lax.psum_scatter(joined, "seq", scatter_dimension=0, tiled=True)
        joined = joined.astype(jnp.bfloat16)
        return dq, bias, joined[:, :D], joined[:, D:], dt


def block_forward(inputs, layer, params, attention):
    gain, shift, bias, w_in, w_out, w_expand, b_expand, w_contract, b_contract = params
    layer_in = w_in[layer]
    normed = layer_norm(inputs, gain[layer, 0], shift[layer, 0]).astype(jnp.bfloat16)
    projected = dot_float(normed, layer_in[:, : 3 * D])
    queries = projected[:, :D]
    keys = projected[:, D : 2 * D].astype(jnp.bfloat16)
    values = projected[:, 2 * D :].astype(jnp.bfloat16)
    content = (queries + bias[layer, 0]).astype(jnp.bfloat16)
    position = (queries + bias[layer, 1]).astype(jnp.bfloat16)
    mixed, kept = attention.forward(content, position, keys, values, layer_in[:, 3 * D :])
    middle = inputs + dot_float(mixed, w_out[layer])
    normed_two = layer_norm(middle, gain[layer, 1], shift[layer, 1]).astype(jnp.bfloat16)
    expanded = dot_float(normed_two, w_expand[layer]) + b_expand[layer]
    activated = jax.nn.gelu(expanded, approximate=False).astype(jnp.bfloat16)
    result = middle + dot_float(activated, w_contract[layer]) + b_contract[layer]
    return result, (inputs, normed, kept, mixed, middle, normed_two, expanded, activated)


def norm_backward(inputs, gain, shift, grad):
    pull = jax.vjp(layer_norm, inputs, gain.astype(jnp.float32), shift.astype(jnp.float32))[1]
    return pull(grad)


def block_backward(grad_result, layer, params, stored, attention, near):
    gain, shift, bias, w_in, w_out, w_expand, b_expand, w_contract, b_contract = params
    inputs, normed, kept, mixed, middle, normed_two, expanded, activated = stored
    layer_in = w_in[layer]
    branch = grad_result.astype(jnp.bfloat16)
    contract_bias = jnp.sum(branch.astype(jnp.float32), axis=0)
    grad_activated = dot_back(branch, w_contract[layer])
    gelu_pull = jax.vjp(lambda value: jax.nn.gelu(value, approximate=False), expanded)[1]
    grad_expanded = gelu_pull(grad_activated)[0].astype(jnp.bfloat16)
    expand_bias = jnp.sum(grad_expanded.astype(jnp.float32), axis=0)
    grad_normed_two = dot_back(grad_expanded, w_expand[layer])
    grad_norm, gain_two, shift_two = norm_backward(
        middle, gain[layer, 1], shift[layer, 1], grad_normed_two
    )
    grad_middle = grad_result + grad_norm
    grad_attend = grad_middle.astype(jnp.bfloat16)
    grad_mixed = dot_back(grad_attend, w_out[layer]).astype(jnp.bfloat16)
    dq, bias_pair, dk, dv, dt = attention.backward(kept, grad_mixed)
    grad_projected = jnp.concatenate([dq, dk, dv], axis=1)
    grad_normed = dot_back(grad_projected, layer_in[:, : 3 * D])
    grad_norm, gain_one, shift_one = norm_backward(
        inputs, gain[layer, 0], shift[layer, 0], grad_normed
    )
    small = (
        jnp.stack([gain_one, gain_two]),
        jnp.stack([shift_one, shift_two]),
        bias_pair,
        expand_bias,
        contract_bias,
    )
    early = [near(normed_two, grad_expanded), near(activated, branch), near(mixed, grad_attend)]
    late = [near(normed, grad_projected), near(attention.embedded, dt)]
    return grad_middle + grad_norm, small, early, late


def summed_pieces(groups, shapes, core, depth):
    place = (lax.axis_index("seq") // 2).astype(jnp.int32)[None]
    plan, buffers = [], []
    for pieces, targets in groups:
        plan.append(targets)
        buffers.append(reduced(pieces, place, core, depth))
    return final_outputs(plan, buffers, shapes)


def summed_plainly(groups, shapes):
    count = lax.axis_size("seq")
    outs = [[] for _ in shapes]
    for pieces, targets in groups:
        for (features, grad), (index, layer, first, columns, _) in zip(pieces, targets):
            total = outer_float(features, grad).astype(jnp.bfloat16)
            total = lax.psum_scatter(total, "seq", scatter_dimension=0, tiled=True)
            total = lax.psum(total, "dp").astype(jnp.float32)
            outs[index].append((layer, first, total))
    results = []
    for parts in outs:
        layers = []
        for layer in sorted({part[0] for part in parts}):
            chosen = sorted((p for p in parts if p[0] == layer), key=lambda p: p[1])
            layers.append(jnp.concatenate([p[2] for p in chosen], axis=1))
        results.append(jnp.stack(layers))
    return results


def per_device(
    tokens,
    doc_lengths,
    cotangent,
    norm_gain,
    norm_shift,
    relative_bias,
    attention_in,
    attention_out,
    expand_weight,
    expand_bias,
    contract_weight,
    contract_bias,
    pool_weight,
    pool_bias,
    upsample_weight,
    upsample_bias,
):
    def by_layer(weight):
        return jnp.transpose(weight, (1, 0, 2))

    params = (
        norm_gain,
        norm_shift,
        relative_bias,
        by_layer(attention_in),
        by_layer(attention_out),
        by_layer(expand_weight),
        expand_bias,
        by_layer(contract_weight),
        contract_bias,
    )
    inputs = tokens[0].astype(jnp.float32)
    row_count = inputs.shape[0]
    pooled_count = row_count // 3
    device = lax.axis_index("seq").astype(jnp.int32)
    seq_count = lax.axis_size("seq")
    usual = seq_count == 8 and lax.axis_size("dp") == 4
    core = device % 2 == 1
    depth = lax.axis_index("dp") % 2 == 1
    ends = jnp.cumsum(doc_lengths[0]).astype(jnp.int32)
    token_start = device * row_count
    token_place = token_start + jnp.arange(row_count)
    window = Window(token_start, ends, embedding(WIN, QBLK))
    pooled_level = Pooled(device, seq_count, pooled_count, ends, usual)

    def near(features, grad):
        if not usual:
            return features, grad
        own, other = halves(grad, core)
        return features, crossed(features, "seq", 1), own, crossed(other, "seq", 1)

    first_out, first_stored = block_forward(inputs, 0, params, window)
    first_low = first_out.astype(jnp.bfloat16)
    edge_rows = passed_along(first_low[row_count - 2 :], "seq", 1)
    keep_mask = (token_place >= 2) & (
        document_of(token_place - 2, ends) == document_of(token_place, ends)
    )
    shifted = jnp.concatenate([edge_rows, first_low[: row_count - 2]], axis=0)
    shifted = jnp.where(keep_mask[:, None], shifted, jnp.zeros_like(shifted))
    grouped = shifted.reshape(pooled_count, 3 * D)
    pooled = dot_float(grouped, pool_weight) + pool_bias
    short_out, short_stored = block_forward(pooled, 1, params, pooled_level)
    short_low = short_out.astype(jnp.bfloat16)
    upsampled = (dot_float(short_low, upsample_weight) + upsample_bias).reshape(row_count, D)
    output, last_stored = block_forward(first_out + upsampled, 2, params, window)
    level_squares = jnp.stack(
        [jnp.sum(first_out * first_out), jnp.sum(short_out * short_out), jnp.sum(output * output)]
    )

    grad_joined, small_last, early_last, late_last = block_backward(
        cotangent[0].astype(jnp.float32), 2, params, last_stored, window, near
    )
    grad_upsampled = grad_joined.reshape(pooled_count, 3 * D).astype(jnp.bfloat16)
    grad_upsample_bias = jnp.sum(grad_upsampled.astype(jnp.float32), axis=0)
    grad_short = dot_back(grad_upsampled, upsample_weight)
    grad_pooled, small_short, early_short, late_short = block_backward(
        grad_short, 1, params, short_stored, pooled_level, near
    )
    grad_pooled_low = grad_pooled.astype(jnp.bfloat16)
    grad_pool_bias = jnp.sum(grad_pooled_low.astype(jnp.float32), axis=0)
    grad_shifted = dot_back(grad_pooled_low, pool_weight).reshape(row_count, D)
    grad_shifted = jnp.where(keep_mask[:, None], grad_shifted, 0.0)
    came_back = passed_along(grad_shifted[:2], "seq", -1)
    grad_first = grad_joined + jnp.concatenate([grad_shifted[2:], came_back], axis=0)
    grad_inputs, small_first, early_first, late_first = block_backward(
        grad_first, 0, params, first_stored, window, near
    )

    share = D // seq_count
    shapes = [
        (3, share, 4 * D),
        (3, share, D),
        (3, share, 4 * D),
        (3, 4 * share, D),
        (3 * share, D),
        (share, 3 * D),
    ]

    def early(layer):
        return [(2, layer, 0, 4 * D, share), (3, layer, 0, D, 4 * share), (1, layer, 0, D, share)]

    def late(layer):
        return [(0, layer, 0, 3 * D, share), (0, layer, 3 * D, D, share)]

    groups = [
        (
            early_last + late_last + [near(short_low, grad_upsampled)],
            early(2) + late(2) + [(5, None, 0, 3 * D, share)],
        ),
        (
            early_short + late_short + [near(grouped, grad_pooled_low)],
            early(1) + late(1) + [(4, None, 0, D, 3 * share)],
        ),
        (early_first, early(0)),
        (late_first, late(0)),
    ]
    if usual:
        sums = summed_pieces(groups, shapes, core, depth)
    else:
        groups = [
            (pieces, [(i, l or 0, f, c, h) for i, l, f, c, h in targets])
            for pieces, targets in groups
        ]
        sums = summed_plainly(groups, shapes)
        sums[4], sums[5] = sums[4][0], sums[5][0]
    in_grad, out_grad, expand_grad, contract_grad = [by_layer(total) for total in sums[:4]]
    small = [jnp.stack(parts) for parts in zip(small_first, small_short, small_last)]
    small_sums = summed_everywhere(small + [grad_pool_bias, grad_upsample_bias, level_squares])
    whole_rows = lax.axis_size("dp") * seq_count * row_count * D
    counts = jnp.array([whole_rows, whole_rows // 3, whole_rows], jnp.float32)
    rms = jnp.sqrt(small_sums[7] / counts)
    return (
        output[None].astype(jnp.bfloat16),
        grad_inputs[None].astype(jnp.bfloat16),
        small_sums[0],
        small_sums[1],
        small_sums[2],
        in_grad,
        out_grad,
        expand_grad,
        small_sums[3],
        contract_grad,
        small_sums[4],
        sums[4],
        small_sums[5],
        sums[5],
        small_sums[6],
        rms,
    )


def solution(mesh):
    rows = P("dp", "seq", None)
    in_specs = (rows, P("dp", None), rows) + (P(),) * 13
    split = P("seq", None, None)
    flat = P("seq", None)
    out_specs = (rows, rows, P(), P(), P(), split, split, split, P(), split, P())
    out_specs += (flat, P(), flat, P(), P())
    return jax.shard_map(
        per_device, mesh=mesh, in_specs=in_specs, out_specs=out_specs, check_vma=False
    )
```

```python
import math
from functools import partial

import jax
import jax.numpy as jnp
from jax import lax
from jax.experimental import pallas as pl
from jax.experimental.pallas import tpu as pltpu
from jax.sharding import PartitionSpec as P

D = 512
HEADS = 8
HD = 64
WIN = 256
QBLK = 384
DOCS = 8
epsilon = 1e-05
GAIN, SHIFT, BIAS, CONTRACT, EXPAND, POOL, UP = 0, 6, 12, 18, 21, 33, 34

VMEM = pl.BlockSpec(memory_space=pltpu.VMEM)
SMEM = pl.BlockSpec(memory_space=pltpu.SMEM)
HBM = pl.BlockSpec(memory_space=pltpu.HBM)


LANES = 128
PAIR = 2 * HD
MASKED = -1e30
PARTS = QBLK // LANES
SEEN = LANES + WIN
REACH = QBLK + WIN


def nt(first, second):
    return lax.dot_general(
        first, second, (((1,), (1,)), ((), ())), preferred_element_type=jnp.float32
    )


def nn(first, second):
    return lax.dot_general(
        first, second, (((1,), (0,)), ((), ())), preferred_element_type=jnp.float32
    )


def tn(first, second):
    return lax.dot_general(
        first, second, (((0,), (0,)), ((), ())), preferred_element_type=jnp.float32
    )


def document(places, info):
    total = jnp.zeros(places.shape, jnp.int32)
    for index in range(DOCS):
        total = total + (places >= info[1 + index]).astype(jnp.int32)
    return total


def lanes_and_rows():
    lane = lax.broadcasted_iota(jnp.int32, (LANES, LANES), 1)
    row = lax.broadcasted_iota(jnp.int32, (LANES, LANES), 0)
    return lane, row


def turned(values, index):
    return [
        jnp.take_along_axis(values[:, m * LANES : (m + 1) * LANES], index, axis=1)
        for m in range(values.shape[1] // LANES)
    ]


def skew_window(table):
    lane, row = lanes_and_rows()
    blocks = turned(table, (lane - row + LANES) % LANES)
    out = [blocks[0]] + [
        jnp.where(lane >= row, here, before) for before, here in zip(blocks, blocks[1:])
    ]
    return jnp.concatenate(out, axis=1)


def unskew_window(scores):
    lane, row = lanes_and_rows()
    blocks = turned(scores, (lane + row) % LANES)
    blocks.append(jnp.zeros_like(blocks[0]))
    out = [
        jnp.where(lane + row < LANES, here, after) for here, after in zip(blocks, blocks[1:])
    ]
    return jnp.concatenate(out, axis=1)


def skew_pooled(table):
    lane, row = lanes_and_rows()
    here, after = turned(table, (lane + LANES - 1 - row) % LANES)
    return jnp.where(lane <= row, here, after)


def unskew_pooled(scores):
    lane, row = lanes_and_rows()
    (block,) = turned(scores, (lane + row + 1) % LANES)
    zero = jnp.zeros_like(block)
    first = lane + row >= LANES - 1
    return jnp.concatenate([jnp.where(first, block, zero), jnp.where(first, zero, block)], axis=1)


def stacked(rows):
    head = lax.broadcasted_iota(jnp.int32, rows.shape, 1) // HD
    zero = jnp.zeros_like(rows)
    return jnp.concatenate([jnp.where(head == 0, rows, zero), jnp.where(head == 1, rows, zero)], axis=0)


def unstacked(rows):
    count = rows.shape[0] // 2
    head = lax.broadcasted_iota(jnp.int32, (count, PAIR), 1) // HD
    return jnp.where(head == 0, rows[:count], rows[count:])


def softmax_rows(scores):
    highest = jnp.max(scores, axis=1, keepdims=True)
    powers = jnp.exp(scores - highest)
    return powers * (1.0 / jnp.sum(powers, axis=1, keepdims=True))


def window_mask(info, part):
    place = info[0] + part * LANES
    row = lax.broadcasted_iota(jnp.int32, (LANES, SEEN), 0)
    column = lax.broadcasted_iota(jnp.int32, (LANES, SEEN), 1)
    behind = row + WIN - column
    query = place + lax.broadcasted_iota(jnp.int32, (LANES, 1), 0)
    key = place - WIN + lax.broadcasted_iota(jnp.int32, (1, SEEN), 1)
    same = document(query, info) == document(key, info)
    return (behind >= 0) & (behind <= WIN) & same & (key >= 0)


def pooled_mask(info, start):
    query = info[0] + lax.broadcasted_iota(jnp.int32, (LANES, 1), 0)
    key = start + lax.broadcasted_iota(jnp.int32, (1, LANES), 1)
    return (key <= query) & (document(3 * query, info) == document(3 * key, info))


def column_sums(first, second):
    return jnp.concatenate(
        [jnp.sum(first, axis=0, keepdims=True), jnp.sum(second, axis=0, keepdims=True)], axis=0
    )


def backward_scores(weights, grad_weights):
    delta = jnp.sum(weights * grad_weights, axis=1, keepdims=True)
    return weights * (grad_weights - delta)


def window_forward_kernel(
    raw,
    info,
    content,
    position,
    keys,
    values,
    border,
    gain,
    shift,
    key_weight,
    value_weight,
    table,
    mixed_ref,
    normed_ref,
    border_ref,
    weights_ref,
    bias,
    normed,
    places,
):
    pair = pl.program_id(0)

    @pl.when(pair == 0)
    def _():
        if raw is None:
            normed[...] = border[...]
        else:
            hat, _ = normalised(border[...].astype(jnp.float32))
            scale = gain[raw].astype(jnp.float32)[0:1, :]
            normed[...] = (hat * scale + shift[raw].astype(jnp.float32)[0:1, :]).astype(jnp.bfloat16)
        normed_ref[...] = normed[...]
        for part in range(PARTS):
            bias[part] = jnp.where(window_mask(info, part), 0.0, MASKED)

    border_keys = nn(normed[...], key_weight[...]).astype(jnp.bfloat16)
    border_values = nn(normed[...], value_weight[...]).astype(jnp.bfloat16)
    border_ref[0] = border_keys
    border_ref[1] = border_values
    all_keys = jnp.concatenate([border_keys, keys[...]], axis=0)
    all_values = jnp.concatenate([border_values, values[...]], axis=0)
    scale = jnp.asarray(HD**-0.5, jnp.bfloat16)
    order = [
        stacked(position[part * LANES : (part + 1) * LANES, :] * scale) for part in range(PARTS)
    ]
    places[...] = nt(jnp.concatenate(order, axis=0), table[...])
    for part in range(PARTS):
        rows = slice(part * LANES, (part + 1) * LANES)
        seen = slice(part * LANES, part * LANES + SEEN)
        scores = nt(stacked(content[rows, :] * scale), all_keys[seen])
        weights = []
        for index in range(2):
            start = (2 * part + index) * LANES
            score = scores[index * LANES : (index + 1) * LANES]
            score = score + skew_window(places[start : start + LANES, :]) + bias[part]
            weights.append(softmax_rows(score).astype(jnp.bfloat16))
            weights_ref[index, part] = weights[index]
        mixed = nn(jnp.concatenate(weights, axis=0), all_values[seen])
        mixed_ref[rows, :] = unstacked(mixed).astype(jnp.bfloat16)


def window_backward_kernel(
    place,
    content,
    position,
    keys,
    values,
    border,
    key_weight,
    value_weight,
    table,
    weights,
    grad,
    bias_ref,
    returned_ref,
    pack,
    dk_sum,
    dv_sum,
    returned,
    places,
    dq_out,
    dk_out,
    dv_out,
    dt_out,
    sems,
):
    pair = pl.program_id(0)
    all_keys = jnp.concatenate([border[0], keys[...]], axis=0)
    all_values = jnp.concatenate([border[1], values[...]], axis=0)
    scale = HD**-0.5
    low_scale = jnp.asarray(scale, jnp.bfloat16)
    dk_sum[...] = jnp.zeros_like(dk_sum)
    dv_sum[...] = jnp.zeros_like(dv_sum)
    contents = []
    for part in range(PARTS):
        rows = slice(part * LANES, (part + 1) * LANES)
        seen = slice(part * LANES, part * LANES + SEEN)
        grads = stacked(grad[rows, :])
        grad_weights = nt(grads, all_values[seen])
        scores, lows = [], []
        for index in range(2):
            low = weights[index, part]
            score = backward_scores(
                low.astype(jnp.float32), grad_weights[index * LANES : (index + 1) * LANES]
            ).astype(jnp.bfloat16)
            start = (2 * part + index) * LANES
            places[start : start + LANES, :] = unskew_window(score.astype(jnp.float32)).astype(
                jnp.bfloat16
            )
            scores.append(score)
            lows.append(low)
        scores = jnp.concatenate(scores, axis=0)
        contents.append(unstacked(nn(scores, all_keys[seen])) * scale)
        dk_sum[seen, :] += tn(scores, stacked(content[rows, :] * low_scale))
        dv_sum[seen, :] += tn(jnp.concatenate(lows, axis=0), grads)
    order = [
        stacked(position[part * LANES : (part + 1) * LANES, :] * low_scale)
        for part in range(PARTS)
    ]
    to_position = nn(places[...], table[...]) * scale
    positions = [
        unstacked(to_position[2 * part * LANES : 2 * (part + 1) * LANES]) for part in range(PARTS)
    ]
    grad_content = jnp.concatenate(contents, axis=0)
    grad_position = jnp.concatenate(positions, axis=0)
    bias_ref[...] = column_sums(grad_content, grad_position)
    dq_out[...] = (grad_content + grad_position).astype(jnp.bfloat16)
    dk_out[...] = dk_sum[...].astype(jnp.bfloat16)
    dv_out[...] = dv_sum[...].astype(jnp.bfloat16)
    dt_out[...] = tn(places[...], jnp.concatenate(order, axis=0)).astype(jnp.bfloat16)
    copies = pack_copies(place, pair, pack, (dq_out, dk_out, dv_out, dt_out), sems)
    back = nt(dk_out[:WIN, :], key_weight[...]) + nt(dv_out[:WIN, :], value_weight[...])

    @pl.when(pair == 0)
    def _():
        returned[...] = back

    @pl.when(pair != 0)
    def _():
        returned[...] += back

    @pl.when(pair == HEADS // 2 - 1)
    def _():
        returned_ref[...] = returned[...].astype(jnp.bfloat16)

    for copy in copies:
        copy.wait()


def pack_copies(place, pair, pack, outs, sems):
    slot = (pair // 2) ^ place[1]
    copies = []
    for index, out in enumerate(outs):
        lane = pl.multiple_of(index * D // 2 + pair % 2 * PAIR, PAIR)
        target = pack.at[slot, pl.ds(0, out.shape[0]), pl.ds(lane, PAIR)]
        copies.append(pltpu.make_async_copy(out, target, sems.at[index]))
        copies[-1].start()
    return copies


def table_rows(order, block, count):
    start = order[block] + count - 1 - order[count]
    return pl.ds(pl.multiple_of(LANES * jnp.minimum(start, count - 1), LANES), 2 * LANES)


def pooled_forward_kernel(
    info,
    order,
    content,
    position,
    normed,
    key_weight,
    value_weight,
    table,
    mixed_ref,
    keys_ref,
    values_ref,
    weights_ref,
):
    count = normed.shape[0] // LANES
    scale = jnp.asarray(HD**-0.5, jnp.bfloat16)
    keys_ref[...] = nn(normed[...], key_weight[...]).astype(jnp.bfloat16)
    values_ref[...] = nn(normed[...], value_weight[...]).astype(jnp.bfloat16)
    scores = nt(stacked(content[...] * scale), keys_ref[...])
    there = stacked(position[...] * scale)
    rows = [[], []]
    for block in range(count):
        place = nt(there, table[table_rows(order, block, count), :])
        bias = jnp.where(pooled_mask(info, LANES * order[block]), 0.0, MASKED)
        lanes = slice(block * LANES, (block + 1) * LANES)
        for index in range(2):
            half = slice(index * LANES, (index + 1) * LANES)
            rows[index].append(scores[half, lanes] + skew_pooled(place[half]) + bias)
    weights = []
    for index in range(2):
        weight = softmax_rows(jnp.concatenate(rows[index], axis=1)).astype(jnp.bfloat16)
        weights_ref[index] = weight
        weights.append(weight)
    mixed = nn(jnp.concatenate(weights, axis=0), values_ref[...])
    mixed_ref[...] = unstacked(mixed).astype(jnp.bfloat16)


def pooled_backward_kernel(
    order,
    place,
    content,
    position,
    keys,
    values,
    key_weight,
    value_weight,
    table,
    weights,
    grad,
    bias_ref,
    even_ref,
    odd_ref,
    pack,
    table_sum,
    total,
    dq_out,
    dk_out,
    dv_out,
    dt_out,
    sems,
):
    pair = pl.program_id(0)
    count = keys.shape[0] // LANES
    scale = HD**-0.5
    low_scale = jnp.asarray(scale, jnp.bfloat16)
    table_sum[...] = jnp.zeros_like(table_sum)
    grads = stacked(grad[...])
    grad_weights = nt(grads, values[...])
    lows = jnp.concatenate([weights[0], weights[1]], axis=0)
    scores = backward_scores(lows.astype(jnp.float32), grad_weights)
    low_scores = scores.astype(jnp.bfloat16)
    grad_content = unstacked(nn(low_scores, keys[...])) * scale
    positions = stacked(position[...] * low_scale)
    to_position = jnp.zeros((2 * LANES, PAIR), jnp.float32)
    for block in range(count):
        rows = table_rows(order, block, count)
        lanes = slice(block * LANES, (block + 1) * LANES)
        parts = []
        for index in range(2):
            half = low_scores[index * LANES : (index + 1) * LANES, lanes]
            parts.append(unskew_pooled(half.astype(jnp.float32)).astype(jnp.bfloat16))
        parts = jnp.concatenate(parts, axis=0)
        to_position = to_position + nn(parts, table[rows, :])
        table_sum[rows, :] += tn(parts, positions)
    grad_position = unstacked(to_position) * scale
    bias_ref[...] = column_sums(grad_content, grad_position)
    dq_out[...] = (grad_content + grad_position).astype(jnp.bfloat16)
    dk_out[...] = tn(low_scores, stacked(content[...] * low_scale)).astype(jnp.bfloat16)
    dv_out[...] = tn(lows, grads).astype(jnp.bfloat16)
    dt_out[...] = table_sum[...].astype(jnp.bfloat16)
    copies = pack_copies(place, pair, pack, (dq_out, dk_out, dv_out, dt_out), sems)
    back = nt(dk_out[...], key_weight[...]) + nt(dv_out[...], value_weight[...])

    @pl.when(pair == 0)
    def _():
        total[...] = back

    @pl.when(pair != 0)
    def _():
        total[...] += back

    @pl.when(pair == HEADS // 2 - 1)
    def _():
        for block in range(count):
            target = (even_ref, odd_ref)[block % 2]
            start = block // 2 * LANES
            rows = total[block * LANES : (block + 1) * LANES, :]
            target[start : start + LANES, :] = rows.astype(jnp.bfloat16)

    for copy in copies:
        copy.wait()


def by_pair(shape, first=0):
    front = tuple(shape[:-1])
    zeros = (0,) * len(front)
    return pl.BlockSpec(front + (PAIR,), lambda pair: zeros + (first + pair,))


def entire(shape):
    zeros = (0,) * len(shape)
    return pl.BlockSpec(tuple(shape), lambda pair: zeros)


def of_layer(shape, layer, first):
    return pl.BlockSpec((None, shape[1], PAIR), lambda pair: (layer, 0, first + pair))


def weights_block(shape):
    return pl.BlockSpec((2,) + tuple(shape[1:]), lambda pair: (pair,) + (0,) * (len(shape) - 1))


def attention_call(micros, kernel, scalars, operands, outs, scratch, mib):
    return pl.pallas_call(
        kernel,
        grid=(HEADS // 2,),
        in_specs=[SMEM] * len(scalars) + [spec for _, spec in operands],
        out_specs=[HBM if spec is None else spec for _, _, spec in outs],
        out_shape=[pltpu.HBM(shape, kind) for shape, kind, _ in outs],
        scratch_shapes=scratch,
        compiler_params=pltpu.CompilerParams(vmem_limit_bytes=mib * 2**20),
        cost_estimate=lasting(micros),
    )(*scalars, *[in_hbm(array) for array, _ in operands])


def vector(vectors, row):
    gain, shift, bias, contract, expand, pool, up = vectors
    for start, ref in ((GAIN, gain), (SHIFT, shift), (BIAS, bias)):
        if start <= row < start + 6:
            layer, index = divmod(row - start, 2)
            return ref[layer].astype(jnp.float32)[index : index + 1, :]
    if row < EXPAND:
        return contract[...].astype(jnp.float32)[row - CONTRACT : row - CONTRACT + 1, :]
    if row < POOL:
        layer, part = divmod(row - EXPAND, 4)
        lanes = slice(part * D, (part + 1) * D)
        return expand[:, lanes].astype(jnp.float32)[layer : layer + 1, :]
    if row < UP:
        return pool[...].astype(jnp.float32)
    part = row - UP
    return up[:, part * D : (part + 1) * D].astype(jnp.float32)


def normalised(values):
    centre = values - jnp.mean(values, axis=1, keepdims=True)
    spread = jnp.mean(centre * centre, axis=1, keepdims=True)
    rate = lax.rsqrt(spread + epsilon)
    return centre * rate, rate


def norm_forward(values, vectors, layer, index):
    hat, _ = normalised(values)
    gain = vector(vectors, GAIN + 2 * layer + index)
    return (hat * gain + vector(vectors, SHIFT + 2 * layer + index)).astype(jnp.bfloat16)


def norm_backward(values, vectors, layer, index, grad):
    hat, rate = normalised(values)
    scaled = grad * vector(vectors, GAIN + 2 * layer + index)
    mean = jnp.mean(scaled, axis=1, keepdims=True)
    along = jnp.mean(scaled * hat, axis=1, keepdims=True)
    result = rate * (scaled - mean - hat * along)
    return result, jnp.sum(grad * hat, axis=0, keepdims=True), jnp.sum(grad, axis=0, keepdims=True)


class Copies:
    def __init__(self, sems):
        self.sems, self.used, self.open = sems, 0, []

    def start(self, source, target):
        copy = pltpu.make_async_copy(source, target, self.sems.at[self.used])
        self.used += 1
        copy.start()
        return copy

    def send(self, source, target):
        self.open.append(self.start(source, target))

    def finish(self):
        for copy in self.open:
            copy.wait()


class Output:
    def __init__(self, buffer, target, copies):
        self.buffer, self.target, self.copies, self.sent = buffer, target, copies, False
        self.shape, self.dtype = buffer.shape, buffer.dtype

    def __setitem__(self, index, value):
        self.buffer[index] = value

    def __getitem__(self, index):
        return self.buffer[index]

    def send(self, lanes=None):
        self.sent = True
        if lanes is None:
            self.copies.send(self.buffer, self.target)
        else:
            self.copies.send(self.buffer.at[:, lanes], self.target.at[:, lanes])


def queries(layer, normed, vectors, weight, content, position):
    value = nn(normed, weight[:, :D])
    content[...] = (value + vector(vectors, BIAS + 2 * layer)).astype(jnp.bfloat16)
    position[...] = (value + vector(vectors, BIAS + 2 * layer + 1)).astype(jnp.bfloat16)
    content.send()
    position.send()


def window_project_kernel(
    layer, inputs, vectors, embedded, w_in, content, position, keys, values, table, *normed
):
    weight, copy = w_in
    rows = inputs[...]
    if normed:
        rows = norm_forward(rows.astype(jnp.float32), vectors, layer, 0)
        normed[0][...] = rows
        normed[0].send()
    copy.wait()
    queries(layer, rows, vectors, weight, content, position)
    for index, out in ((1, keys), (2, values)):
        out[...] = nn(rows, weight[:, index * D : (index + 1) * D]).astype(jnp.bfloat16)
        out.send()
    table[...] = nn(embedded[...], weight[:, 3 * D :]).astype(jnp.bfloat16)


def third_rows(ref, start):
    rows = pl.ds(start, LANES, stride=3)
    return jnp.concatenate([ref[index, rows, :] for index in range(D // LANES)], axis=1)


def put_third_rows(ref, start, values):
    for index in range(D // LANES):
        lanes = slice(index * LANES, (index + 1) * LANES)
        ref[index, pl.ds(start, LANES, stride=3), :] = values[:, lanes]


def put_rows(ref, start, values):
    for index in range(D // LANES):
        lanes = slice(index * LANES, (index + 1) * LANES)
        ref[index, start : start + values.shape[0], :] = values[:, lanes]


def all_rows(ref):
    return jnp.concatenate([ref[index] for index in range(D // LANES)], axis=1)


def kept(info, offset):
    count = LANES
    place = info[0] + 3 * lax.broadcasted_iota(jnp.int32, (count, 1), 0) + offset
    return (place >= 2) & (document(place - 2, info) == document(place, info))


def pool_kernel(info, full, edge, vectors, w_pool, normed, inputs, grouped, moved):
    pool_weight, pool_copy = w_pool
    put_rows(moved, 8, full[...])
    put_rows(moved, 6, edge[...].astype(jnp.float32))
    parts = []
    for offset in range(3):
        rows = third_rows(moved, offset + 6)
        parts.append(jnp.where(kept(info, offset), rows, 0.0).astype(jnp.bfloat16))
        grouped[:, offset * D : (offset + 1) * D] = parts[offset]
    pool_copy.wait()
    total = vector(vectors, POOL)
    for offset in range(3):
        total = total + nn(parts[offset], pool_weight[offset * D : (offset + 1) * D, :])
    normed[...] = norm_forward(total, vectors, 1, 0)
    normed.send()
    inputs[...] = total


def pooled_project_kernel(normed, vectors, embedded, w_in, content, position, table):
    weight, copy = w_in
    copy.wait()
    queries(1, normed[...], vectors, weight, content, position)
    table[...] = nn(embedded[...], weight[:, 3 * D :]).astype(jnp.bfloat16)


def feed(layer, mixed, inputs, vectors, weights, middle_ref, slope, pack):
    w_out, w_expand, w_contract = [buffer for buffer, _ in weights]
    copies = [copy for _, copy in weights]
    pack[:, :D] = mixed[...]
    copies[0].wait()
    middle = inputs[...].astype(jnp.float32) + nn(mixed[...], w_out[...])
    middle_ref[...] = middle
    middle_ref.send()
    normed_two = norm_forward(middle, vectors, layer, 1)
    pack[:, D : 2 * D] = normed_two
    pack.send(slice(0, 2 * D))
    copies[1].wait()
    copies[2].wait()
    total = middle + vector(vectors, CONTRACT + layer)
    for part in range(4):
        lanes = slice(part * D, (part + 1) * D)
        value = nn(normed_two, w_expand[:, lanes]) + vector(vectors, EXPAND + 4 * layer + part)
        below = 0.5 + 0.5 * lax.erf(value * 0.5**0.5)
        density = jnp.exp(value * value * -0.5) * (0.5 / math.pi) ** 0.5
        slope[:, lanes] = (below + value * density).astype(jnp.bfloat16)
        active = (value * below).astype(jnp.bfloat16)
        pack[:, (2 + part) * D : (3 + part) * D] = active
        slope.send(lanes)
        pack.send(slice((2 + part) * D, (3 + part) * D))
        total = total + nn(active, w_contract[lanes, :])
    return total


def window_feed_kernel(
    layer,
    mixed,
    inputs,
    vectors,
    w_out,
    w_expand,
    w_contract,
    middle,
    slope,
    pack,
    result,
    squares,
):
    weights = (w_out, w_expand, w_contract)
    total = feed(layer, mixed, inputs, vectors, weights, middle, slope, pack)
    result[...] = total.astype(result.dtype)
    squares[...] = jnp.sum(total * total, axis=0, keepdims=True)


def pooled_feed_kernel(
    mixed,
    inputs,
    grouped,
    full,
    vectors,
    w_out,
    w_expand,
    w_contract,
    w_up,
    middle,
    slope,
    pack,
    next_normed,
    result,
    squares,
    spread,
):
    weights = (w_out, w_expand, w_contract)
    total = feed(1, mixed, inputs, vectors, weights, middle, slope, pack)
    squares[...] = jnp.sum(total * total, axis=0, keepdims=True)
    low = total.astype(jnp.bfloat16)
    pack[:, 6 * D : 7 * D] = low
    pack[:, 7 * D :] = grouped[...]
    pack.send(slice(6 * D, 10 * D))
    up_buffer, copy = w_up
    copy.wait()
    for offset in range(3):
        raised = nn(low, up_buffer[:, offset * D : (offset + 1) * D])
        put_third_rows(spread, offset, raised + vector(vectors, UP + offset))
    raised = full[...] + all_rows(spread)
    next_normed[...] = norm_forward(raised, vectors, 2, 0)
    next_normed.send()
    result[...] = raised


def store_halves(core, own, other, offset, values):
    half = values.shape[1] // 2
    low = values[:, :half].astype(jnp.bfloat16)
    high = values[:, half:].astype(jnp.bfloat16)
    rows = values.shape[0]

    @pl.when(core == 0)
    def _():
        own[:rows, offset : offset + half] = low
        other[:rows, offset : offset + half] = high

    @pl.when(core != 0)
    def _():
        own[:rows, offset : offset + half] = high
        other[:rows, offset : offset + half] = low


def feed_backward(
    layer,
    place,
    grad,
    slope,
    middle,
    vectors,
    w_contract,
    w_expand,
    w_out,
    middle_grad,
    mixed_grad,
    own,
    other,
    small,
):
    contract, expand, out = [weight[0] for weight in (w_contract, w_expand, w_out)]
    copies = [weight[1] for weight in (w_contract, w_expand, w_out)]
    core = place[1]
    branch = grad.astype(jnp.bfloat16)
    small[...] = jnp.zeros_like(small)
    small[0:1, :] = jnp.sum(branch.astype(jnp.float32), axis=0, keepdims=True)
    store_halves(core, own, other, 2 * D, branch)
    copies[0].wait()
    copies[1].wait()
    normed_grad = jnp.zeros(grad.shape, jnp.float32)
    changes = []
    for part in range(4):
        lanes = slice(part * D, (part + 1) * D)
        change = nt(branch, contract[lanes, :]) * slope[:, lanes].astype(jnp.float32)
        change = change.astype(jnp.bfloat16)
        changes.append(change)
        small[3 + part : 4 + part, :] = jnp.sum(
            change.astype(jnp.float32), axis=0, keepdims=True
        )
        normed_grad = normed_grad + nt(change, expand[:, lanes])
    store_halves(core, own, other, 0, jnp.concatenate(changes, axis=1))
    norm, gain, shift = norm_backward(middle[...], vectors, layer, 1, normed_grad)
    small[1:2, :] = gain
    small[2:3, :] = shift
    total = grad + norm
    middle_grad[...] = total
    attend = total.astype(jnp.bfloat16)
    store_halves(core, own, other, 2 * D + D // 2, attend)
    other.send()
    copies[2].wait()
    mixed_grad[...] = nt(attend, out[...]).astype(jnp.bfloat16)


def feed_backward_kernel(layer, place, grad, *refs):
    feed_backward(layer, place, grad[...].astype(jnp.float32), *refs)


def first_feed_backward_kernel(place, joined, shifted, came_back, *refs):
    moved = refs[-1]
    rows = shifted.shape[0]
    moved[:rows, :] = shifted[...]
    moved[rows : rows + 2, :] = came_back[...]
    feed_backward(0, place, joined[...] + moved[2 : rows + 2, :], *refs[:-1])


def project_backward(layer, core, pack, rows, weight, extra, inputs, middle_grad, vectors, small):
    small[...] = jnp.zeros_like(small)
    normed_grad = extra
    for index, chosen in enumerate(rows):
        for slot in range(2):
            half = slot ^ core
            begin = pl.multiple_of(index * D + half * (D // 2), D // 2)
            grad = pack[slot, chosen, index * D // 2 : (index + 1) * D // 2]
            normed_grad = normed_grad + nt(grad, weight[:, pl.ds(begin, D // 2)])
    norm, gain, shift = norm_backward(inputs, vectors, layer, 0, normed_grad)
    small[0:1, :] = gain
    small[1:2, :] = shift
    return middle_grad[...] + norm


def window_project_backward(layer, core, pack, returned, weight, *rest):
    extra = jnp.concatenate(
        [jnp.zeros((QBLK - WIN, D), jnp.float32), returned[...].astype(jnp.float32)], axis=0
    )
    rows = (slice(0, QBLK), slice(WIN, REACH), slice(WIN, REACH))
    return project_backward(layer, core, pack, rows, weight, extra, *rest)


def first_project_backward_kernel(
    place, pack, returned, inputs, middle_grad, vectors, w_in, inputs_grad, small
):
    weight, copy = w_in
    copy.wait()
    rows = inputs[...].astype(jnp.float32)
    total = window_project_backward(
        0, place[1], pack, returned, weight, rows, middle_grad, vectors, small
    )
    inputs_grad[...] = total.astype(inputs_grad.dtype)


def last_project_backward_kernel(
    place,
    pack,
    returned,
    inputs,
    middle_grad,
    vectors,
    w_in,
    w_up,
    inputs_grad,
    short_grad,
    own,
    other,
    small,
    spread,
):
    (weight, copy), (up_weight, up_copy) = w_in, w_up
    copy.wait()
    total = window_project_backward(
        2, place[1], pack, returned, weight, inputs[...], middle_grad, vectors, small
    )
    inputs_grad[...] = total
    inputs_grad.send()
    put_rows(spread, 0, total)
    parts = [third_rows(spread, offset).astype(jnp.bfloat16) for offset in range(3)]
    up_copy.wait()
    result = jnp.zeros((LANES, D), jnp.float32)
    for offset in range(3):
        small[2 + offset : 3 + offset, :] = jnp.sum(
            parts[offset].astype(jnp.float32), axis=0, keepdims=True
        )
        result = result + nt(parts[offset], up_weight[:, offset * D : (offset + 1) * D])
    short_grad[...] = result
    joined = jnp.concatenate(parts, axis=1)
    half = 3 * D // 2
    quarter = half // 3

    def place_parts(target, values):
        for index in range(3):
            target[index * LANES : (index + 1) * LANES, :] = values[
                :, index * quarter : (index + 1) * quarter
            ]

    @pl.when(place[1] == 0)
    def _():
        place_parts(own, joined[:, :half])
        place_parts(other, joined[:, half:])

    @pl.when(place[1] != 0)
    def _():
        place_parts(own, joined[:, half:])
        place_parts(other, joined[:, :half])


def pooled_project_backward_kernel(
    info,
    place,
    pack,
    normed_grad,
    inputs,
    middle_grad,
    vectors,
    w_in,
    w_pool,
    shifted_grad,
    own,
    other,
    small,
    spread,
):
    (weight, copy), (pool_weight, pool_copy) = w_in, w_pool
    copy.wait()
    total = project_backward(
        1,
        place[1],
        pack,
        (slice(0, LANES),),
        weight,
        normed_grad[...],
        inputs[...],
        middle_grad,
        vectors,
        small,
    )
    low = total.astype(jnp.bfloat16)
    small[2:3, :] = jnp.sum(low.astype(jnp.float32), axis=0, keepdims=True)
    store_halves(place[1], own, other, 0, low)
    pool_copy.wait()
    for offset in range(3):
        rows = nt(low, pool_weight[offset * D : (offset + 1) * D, :])
        put_third_rows(spread, offset, jnp.where(kept(info, offset), rows, 0.0))
    shifted_grad[...] = all_rows(spread)


def lasting(micros):
    return pl.CostEstimate(
        flops=int(micros * 1e8), bytes_accessed=int(micros * 3e5), transcendentals=0
    )


class Part:
    def __init__(self, array, shape):
        self.array, self.shape = array, tuple(shape)

    def of(self, ref):
        if self.shape == self.array.shape:
            return ref
        return ref.at[tuple(slice(0, size) for size in self.shape)]


def whole(micros, kernel, scalars, arrays, weights, outs, scratch=(), mib=24):
    flat, groups, parts = [], [], []
    for array in arrays:
        groups.append(len(array) if isinstance(array, tuple) else 0)
        for item in array if isinstance(array, tuple) else (array,):
            part = item if isinstance(item, Part) else Part(item, item.shape)
            flat.append(part.array)
            parts.append(part)
    shapes = [(part.shape, part.array.dtype) for part in parts]
    shapes += [(w.shape if layer is None else w.shape[1:], w.dtype) for w, layer in weights]
    shapes += list(outs) + list(scratch)
    scalar_count, flat_count, weight_count = len(scalars), len(flat), len(weights)
    sem_count = 64

    def run(*refs):
        copies = Copies(refs[-1])
        refs = list(refs[:-1])

        def take(count):
            taken, refs[:count] = refs[:count], []
            return taken

        taken = take(scalar_count)
        sources, weight_sources, targets = take(flat_count), take(weight_count), take(len(outs))
        buffers, weight_buffers, out_buffers = take(flat_count), take(weight_count), take(len(outs))
        loads = [copies.start(p.of(s), b) for p, s, b in zip(parts, sources, buffers)]
        loaded = []
        for (_, layer), source, buffer in zip(weights, weight_sources, weight_buffers):
            source = source if layer is None else source.at[layer]
            loaded.append((buffer, copies.start(source, buffer)))
        for copy in loads:
            copy.wait()
        position = 0
        for size in groups:
            taken.append(buffers[position : position + size] if size else buffers[position])
            position += size or 1
        results = [Output(b, t, copies) for b, t in zip(out_buffers, targets)]
        kernel(*taken, *loaded, *results, *refs)
        for result in results:
            if not result.sent:
                result.send()
        copies.finish()

    return pl.pallas_call(
        run,
        in_specs=[SMEM] * scalar_count + [HBM] * (flat_count + weight_count),
        out_specs=[HBM] * len(outs),
        out_shape=[pltpu.HBM(shape, kind) for shape, kind in outs],
        scratch_shapes=[pltpu.VMEM(*item) for item in shapes]
        + [pltpu.SemaphoreType.DMA((sem_count,))],
        compiler_params=pltpu.CompilerParams(vmem_limit_bytes=mib * 2**20),
        cost_estimate=lasting(micros),
    )(*scalars, *[in_hbm(a) for a in flat + [w for w, _ in weights]])


def in_hbm(array):
    return pltpu.with_memory_space_constraint(array, pltpu.HBM)


def crossed(block, axis, bit):
    count = lax.axis_size(axis)
    return lax.ppermute(block, axis, [(index, index ^ bit) for index in range(count)])


def passed_along(block, axis, distance):
    devices = range(lax.axis_size(axis))
    route = [(i - distance, i) for i in devices if i - distance in devices]
    return lax.ppermute(block, axis, route)


def both(low, high, bit):
    return jnp.where(bit, high, low), jnp.where(bit, low, high)


def rounded_sum(*terms):
    return sum(term.astype(jnp.float32) for term in terms).astype(jnp.bfloat16)


def gather_pooled(rows):
    half = rows.shape[0] // 2
    from_x = crossed(rows, "seq", 2)
    from_y = crossed(rows, "seq", 4)
    from_core = crossed(rows, "seq", 1)
    first = crossed(from_x[:half], "seq", 4)
    second = crossed(from_y[half:], "seq", 2)
    core_x = crossed(from_x, "seq", 1)
    core_y = crossed(from_y, "seq", 1)
    opposite = jnp.concatenate([first, second], axis=0)
    core_opposite = crossed(opposite, "seq", 1)
    return jnp.concatenate(
        [rows, from_core, from_x, core_x, from_y, core_y, opposite, core_opposite], axis=0
    )


def scatter_pooled(even, odd, meanwhile):
    arrived = crossed(odd, "seq", 1)
    total = rounded_sum(even, arrived).reshape(4, LANES, D)
    made = meanwhile(total)
    left, right = total[:, :, : D // 2], total[:, :, D // 2 :]
    left_arrived = crossed(jnp.stack([left[1], left[3]]), "seq", 2)
    right_arrived = crossed(right[2:], "seq", 4)
    (left_arrived, right_arrived), _ = together((left_arrived, right_arrived), made)
    left_next = crossed(rounded_sum(left[2], left_arrived[1]), "seq", 4)
    right_next = crossed(rounded_sum(right[1], right_arrived[1]), "seq", 2)

    def added(*terms):
        return sum(term.astype(jnp.float32) for term in terms)

    total = jnp.concatenate(
        [
            added(left[0], left_arrived[0], left_next),
            added(right[0], right_arrived[0], right_next),
        ],
        axis=1,
    )
    return total, made


class Piece:
    def __init__(self, features, halves, reads, compute):
        self.height, self.halves, self.reads, self.compute = features // 4, halves, reads, compute
        self.lanes = sum(features // D * half // 2 for half in halves)


def plain_piece(x, first, features, dy, start, half):
    def compute(refs, chosen):
        return [sum(tn(a[:, chosen], b[...]) for a, b in zip(refs[x], refs[dy]))]

    return Piece(features, [half], {x: (first, features), dy: (start, half)}, compute)


def table_part(embedded, grads, chosen):
    rows = embedded.shape[0]
    lanes = slice(3 * D // 2, 2 * D)
    summed = sum(grad[:rows, lanes].astype(jnp.float32) for grad in grads)
    return tn(embedded[:, chosen], summed.astype(jnp.bfloat16))


def window_piece(normed, grads, table):
    def compute(refs, chosen):
        totals = []
        for index, (rows, grad_rows) in enumerate(
            ((slice(WIN, REACH), slice(0, QBLK)),) + ((slice(0, REACH),) * 2,) * 2
        ):
            lanes = slice(index * D // 2, (index + 1) * D // 2)
            totals.append(
                sum(
                    tn(features[rows, chosen], grad[grad_rows, lanes])
                    for features, grad in zip(refs[normed], refs[grads])
                )
            )
        return totals + [table_part(refs[table][0], refs[grads], chosen)]

    return Piece(D, [D // 2] * 4, {normed: (0, D), grads: (0, 2 * D), table: (0, D)}, compute)


def pooled_piece(normed, grads, table):
    def compute(refs, chosen):
        (features,) = refs[normed]
        own, pair = refs[grads]
        count = features.shape[0] // LANES
        lanes = slice(0, D // 2)
        query = sum(
            tn(features[index * LANES : (index + 1) * LANES, chosen], grad[:LANES, lanes])
            for index, grad in enumerate((own, pair))
        )
        totals = [query]
        for index in (1, 2):
            lanes = slice(index * D // 2, (index + 1) * D // 2)
            parts = []
            for block in range(count):
                near, far = block * LANES, (block ^ 1) * LANES
                parts.append(
                    rounded_sum(own[near : near + LANES, lanes], pair[far : far + LANES, lanes])
                )
            totals.append(tn(features[:, chosen], jnp.concatenate(parts, axis=0)))
        return totals + [table_part(refs[table][0], refs[grads], chosen)]

    return Piece(D, [D // 2] * 4, {normed: (0, D), grads: (0, 2 * D), table: (0, D)}, compute)


def upsample_piece(x, first, dy):
    def compute(refs, chosen):
        parts = []
        for index in range(3):
            rows = slice(index * LANES, (index + 1) * LANES)
            parts.append(sum(tn(a[:, chosen], b[rows, :]) for a, b in zip(refs[x], refs[dy])))
        return [jnp.concatenate(parts, axis=1)]

    return Piece(D, [3 * D // 2], {x: (first, D), dy: (0, D // 2)}, compute)


def pair_gradients(micros, place, sources, pieces):
    lanes = sum(piece.lanes for piece in pieces)
    flat, first = [], {}
    for name, arrays in sources.items():
        first[name] = len(flat)
        flat.extend(arrays)
    buffers = []
    for piece in pieces:
        for name, (_, width) in piece.reads.items():
            for array in sources[name]:
                buffers.append(pltpu.VMEM((array.shape[-2], width), array.dtype))
    count = len(flat)
    out = (2, LANES, lanes)

    def kernel(place, *refs):
        arrays, targets = refs[:count], refs[count : count + 4]
        spaces, sems = list(refs[count + 4 : -5]), refs[-1]
        copies = Copies(sems)
        keep_one, send_one, keep_two, send_two = refs[-5:-1]
        ready = []
        for piece in pieces:
            inputs, loads = {}, []
            for name, (start, width) in piece.reads.items():
                inputs[name] = []
                for index in range(len(sources[name])):
                    source = arrays[first[name] + index]
                    space = spaces.pop(0)
                    if len(source.shape) == 3:
                        source = source.at[0]
                    if width != source.shape[1]:
                        source = source.at[:, start : start + width]
                    loads.append(copies.start(source, space))
                    inputs[name].append(space)
            ready.append((inputs, loads))
        offset = 0
        for piece, (inputs, loads) in zip(pieces, ready):
            for load in loads:
                load.wait()
            groups = piece.height // LANES
            for block in range(4):
                begin = pl.multiple_of((place[0] ^ block) * piece.height, LANES)
                totals = piece.compute(inputs, pl.ds(begin, piece.height))
                position = offset
                for total in totals:
                    total = total.astype(jnp.bfloat16)
                    quarter = total.shape[1] // 2
                    for space, slot, part in (
                        ((keep_one, send_one)[block % 2], block // 2, total[:, :quarter]),
                        ((keep_two, send_two)[block // 2], block % 2, total[:, quarter:]),
                    ):
                        if groups == 1:
                            space[slot, :, position : position + quarter] = part
                            continue
                        for group in range(groups):
                            start = position + quarter * group
                            low = HD * group
                            high = piece.height // 2 + low
                            space[slot, :HD, start : start + quarter] = part[low : low + HD]
                            space[slot, HD:, start : start + quarter] = part[high : high + HD]
                    position += quarter * groups
            done = slice(offset, offset + piece.lanes)
            for space, target in zip((keep_one, send_one, keep_two, send_two), targets):
                copies.send(space.at[:, :, done], target.at[:, :, done])
            offset += piece.lanes
        copies.finish()

    return pl.pallas_call(
        kernel,
        in_specs=[SMEM] + [HBM] * count,
        out_specs=[HBM] * 4,
        out_shape=[pltpu.HBM(out, jnp.bfloat16)] * 4,
        scratch_shapes=buffers
        + [pltpu.VMEM(out, jnp.bfloat16)] * 4
        + [pltpu.SemaphoreType.DMA((64,))],
        compiler_params=pltpu.CompilerParams(vmem_limit_bytes=32 * 2**20),
        cost_estimate=lasting(micros),
    )(place, *[in_hbm(a) for a in flat])


def first_step(keep_one, send_one, keep_two, send_two):
    return keep_one, crossed(send_one, "seq", 2), keep_two, crossed(send_two, "seq", 4)


def first_sums(*groups):
    parts = [[], [], [], []]
    for keep_one, one, keep_two, two in groups:
        for index in range(2):
            parts[index].append(rounded_sum(keep_one[index], one[index]))
            parts[2 + index].append(rounded_sum(keep_two[index], two[index]))
    return tuple(jnp.concatenate(part, axis=1) for part in parts)


def second_step(one, send_one, two, send_two):
    return one, crossed(send_one, "seq", 4), two, crossed(send_two, "seq", 2)


def second_sums(one, add_one, two, add_two):
    return rounded_sum(one, add_one), rounded_sum(two, add_two)


def depth_halves(first, second, depth):
    keep, send = both(first, second, depth)
    return keep, crossed(send, "dp", 1)


def depth_quarters(keep, arrived):
    keep = rounded_sum(keep, arrived)
    return keep, crossed(keep, "dp", 2)


def depth_back(keep, arrived):
    keep = rounded_sum(keep, arrived)
    return keep, crossed(keep, "dp", 1)


def shared(keep, other, depth, core):
    first, second = both(keep, other, depth)
    share = jnp.concatenate([first, second], axis=1)
    keep, send = both(share[:HD], share[HD:], core)
    return both(keep, crossed(send, "seq", 1), core)


def together(*groups):
    return lax.optimization_barrier(tuple(tuple(group) for group in groups))


def final_kernel(plan, *refs):
    groups = len(plan)
    buffers, outs = refs[: 2 * groups], refs[2 * groups :]
    for index, pieces in enumerate(plan):
        lanes = buffers[2 * index].shape[1] // 2
        offset = 0
        for out_index, layer, first_column, columns, height in pieces:
            out = outs[out_index]
            quarter = columns // 4
            for group in range(height // HD):
                rows = pl.ds(HD * group, HD)
                for part in range(4):
                    buffer = buffers[2 * index + part // 2]
                    start = (part % 2) * lanes + offset
                    value = buffer[:, start : start + quarter].astype(jnp.float32)
                    begin = first_column + part * quarter
                    if layer is None:
                        out[rows, begin : begin + quarter] = value
                    else:
                        out[layer, rows, begin : begin + quarter] = value
                offset += quarter


def final_outputs(plan, buffers, shapes):
    flat = [array for pair in buffers for array in pair]
    return pl.pallas_call(
        partial(final_kernel, plan),
        in_specs=[VMEM] * len(flat),
        out_specs=[VMEM] * len(shapes),
        out_shape=[jax.ShapeDtypeStruct(shape, jnp.float32) for shape in shapes],
        compiler_params=pltpu.CompilerParams(vmem_limit_bytes=16 * 2**20),
        cost_estimate=lasting(3),
    )(*flat)


def summed_everywhere(flat):
    for axis in ("seq", "dp"):
        for bit in range(lax.axis_size(axis).bit_length() - 1):
            flat = flat + crossed(flat, axis, 1 << bit)
    return flat


def phases(distance):
    frequency = jnp.power(10000.0, -2.0 * jnp.arange(D // 2, dtype=jnp.float32) / D)
    angle = distance.astype(jnp.float32)[:, None] * frequency[None, :]
    return jnp.sin(angle), jnp.cos(angle)


def embedding(first, count):
    step = 32
    high_sin, high_cos = phases(first - step * jnp.arange(count // step))
    low_sin, low_cos = phases(-jnp.arange(step))
    high_sin, high_cos = high_sin[:, None], high_cos[:, None]
    sines = high_sin * low_cos[None] + high_cos * low_sin[None]
    cosines = high_cos * low_cos[None] - high_sin * low_sin[None]
    return jnp.concatenate([sines, cosines], axis=2).astype(jnp.bfloat16).reshape(count, D)


def outer_float(first_matrix, second_matrix):
    return jnp.einsum("rc,re->ce", first_matrix, second_matrix, preferred_element_type=jnp.float32)


BF, FL = jnp.bfloat16, jnp.float32


def window_project(layer, inputs, vectors, embedded, w_in, normalise):
    one = (inputs.shape, BF)
    outs = [one, one, one, one, (embedded.shape, BF)] + [one] * normalise
    return whole(
        4,
        partial(window_project_kernel, layer),
        [],
        [inputs, vectors, embedded],
        [(w_in, layer)],
        outs,
    )


def window_attention(layer, raw, info, heads, border, vectors, w_in, table):
    rows = heads[0].shape[0]
    operands = [(a, by_pair(a.shape)) for a in heads]
    operands += [(a, entire(a.shape)) for a in (border, vectors[0], vectors[1])]
    operands += [(w_in, of_layer(w_in.shape, layer, first)) for first in (4, 8)]
    operands.append((table, by_pair(table.shape)))
    weights = (HEADS, PARTS, LANES, SEEN)
    pair_border = (2, WIN, D)
    outs = [
        ((rows, D), BF, by_pair((rows, D))),
        (border.shape, BF, entire(border.shape)),
        (pair_border, BF, by_pair(pair_border)),
        (weights, BF, weights_block(weights)),
    ]
    scratch = [
        pltpu.VMEM((PARTS, LANES, SEEN), FL),
        pltpu.VMEM(border.shape, BF),
        pltpu.VMEM((2 * rows, SEEN), FL),
    ]
    kernel = partial(window_forward_kernel, layer if raw else None)
    return attention_call(11, kernel, [info], operands, outs, scratch, 20)


def window_attention_back(layer, place, heads, border, w_in, table, weights, grad):
    rows = heads[0].shape[0]
    operands = [(a, by_pair(a.shape)) for a in (*heads, border)]
    operands += [(w_in, of_layer(w_in.shape, layer, first)) for first in (4, 8)]
    operands += [(table, by_pair(table.shape)), (weights, weights_block(weights.shape))]
    operands.append((grad, by_pair(grad.shape)))
    outs = [
        ((2, D), FL, by_pair((2, D))),
        ((WIN, D), BF, entire((WIN, D))),
        ((2, REACH, 2 * D), BF, None),
    ]
    scratch = [pltpu.VMEM((REACH, PAIR), FL)] * 2
    scratch += [pltpu.VMEM((WIN, D), FL), pltpu.VMEM((2 * rows, SEEN), BF)]
    scratch += [pltpu.VMEM((size, PAIR), BF) for size in (rows, REACH, REACH, table.shape[0])]
    scratch.append(pltpu.SemaphoreType.DMA((4,)))
    return attention_call(13, window_backward_kernel, [place], operands, outs, scratch, 20)


def pooled_attention(info, order, content, position, normed, w_in, table):
    rows, total = content.shape[0], normed.shape[0]
    operands = [(a, by_pair(a.shape)) for a in (content, position)]
    operands.append((normed, entire(normed.shape)))
    operands += [(w_in, of_layer(w_in.shape, 1, first)) for first in (4, 8)]
    operands.append((table, by_pair(table.shape)))
    weights = (HEADS, LANES, total)
    outs = [
        ((rows, D), BF, by_pair((rows, D))),
        ((total, D), BF, by_pair((total, D))),
        ((total, D), BF, by_pair((total, D))),
        (weights, BF, weights_block(weights)),
    ]
    mib = 10 + total // LANES * 3 // 2
    return attention_call(13, pooled_forward_kernel, [info, order], operands, outs, [], mib)


def pooled_attention_back(order, place, heads, w_in, table, weights, grad):
    rows, total = heads[0].shape[0], heads[2].shape[0]
    operands = [(a, by_pair(a.shape)) for a in heads]
    operands += [(w_in, of_layer(w_in.shape, 1, first)) for first in (4, 8)]
    operands += [(table, by_pair(table.shape)), (weights, weights_block(weights.shape))]
    operands.append((grad, by_pair(grad.shape)))
    half = ((total // LANES + 1) // 2 * LANES, D)
    outs = [
        ((2, D), FL, by_pair((2, D))),
        (half, BF, entire(half)),
        (half, BF, entire(half)),
        ((2, table.shape[0], 2 * D), BF, None),
    ]
    scratch = [pltpu.VMEM((table.shape[0], PAIR), FL), pltpu.VMEM((total, D), FL)]
    scratch += [pltpu.VMEM((size, PAIR), BF) for size in (rows, total, total, table.shape[0])]
    scratch.append(pltpu.SemaphoreType.DMA((4,)))
    mib = 10 + total // LANES * 3 // 2
    return attention_call(13, pooled_backward_kernel, [order, place], operands, outs, scratch, mib)


def window_feed(layer, mixed, inputs, vectors, weights, kind):
    rows = mixed.shape[0]
    outs = [
        ((rows, D), FL),
        ((rows, 4 * D), BF),
        ((rows, 6 * D), BF),
        ((rows, D), kind),
        ((1, D), FL),
    ]
    return whole(
        7,
        partial(window_feed_kernel, layer),
        [],
        [mixed, inputs, vectors],
        [(w, layer) for w in weights],
        outs,
    )


def feed_back(kernel, layer, place, arrays, rows, weights, extra=()):
    outs = [((rows, D), FL), ((rows, D), BF), ((rows, 3 * D), BF), ((rows, 3 * D), BF)]
    outs.append(((8, D), FL))
    return whole(8, kernel, [place], arrays, [(w, layer) for w in weights], outs, extra)


def per_device(
    tokens,
    doc_lengths,
    cotangent,
    norm_gain,
    norm_shift,
    relative_bias,
    attention_in,
    attention_out,
    expand_weight,
    expand_bias,
    contract_weight,
    contract_bias,
    pool_weight,
    pool_bias,
    upsample_weight,
    upsample_bias,
):
    def by_layer(weight):
        return jnp.transpose(weight, (1, 0, 2))

    w_in, w_out = by_layer(attention_in), by_layer(attention_out)
    w_expand, w_contract = by_layer(expand_weight), by_layer(contract_weight)
    ff_weights = [w_out, w_expand, w_contract]
    vectors = (norm_gain, norm_shift, relative_bias, contract_bias, expand_bias)
    vectors += (pool_bias[None], upsample_bias[None])

    inputs = tokens[0]
    rows = inputs.shape[0]
    pooled_rows = rows // 3
    device = lax.axis_index("seq").astype(jnp.int32)
    seq_count = lax.axis_size("seq")
    usual = seq_count == 8 and lax.axis_size("dp") == 4
    core_index = device % 2
    core = core_index == 1
    depth = lax.axis_index("dp") % 2 == 1
    place = jnp.stack([device // 2, core_index])
    ends = jnp.cumsum(doc_lengths[0]).astype(jnp.int32)
    info = jnp.concatenate([(device * rows)[None], ends]).astype(jnp.int32)
    pooled_info = jnp.concatenate([(device * pooled_rows)[None], ends]).astype(jnp.int32)
    order = jnp.arange(seq_count, dtype=jnp.int32)
    if usual:
        order = order ^ device
    order = jnp.concatenate([order, device[None]])
    near_table = embedding(WIN, QBLK)
    far_table = embedding(seq_count * pooled_rows - 1, (seq_count + 1) * pooled_rows)

    def swapped(array):
        return (array, crossed(array, "seq", 1)) if usual else array

    def swapped_halves(own, other):
        return (own, crossed(other, "seq", 1)) if usual else (own, other)

    border0 = passed_along(inputs[rows - WIN :], "seq", 1)
    *heads0, table0, normed0 = window_project(0, inputs, vectors, near_table, w_in, True)
    mixed0, edge_normed0, border0, weights0 = window_attention(
        0, True, info, heads0, border0, vectors, w_in, table0
    )
    middle0, slope0, pack0, full0, squares0 = window_feed(
        0, mixed0, inputs, vectors, ff_weights, FL
    )
    edge = passed_along(full0[rows - 2 :].astype(BF), "seq", 1)
    x0, n0 = swapped(pack0), swapped(jnp.concatenate([edge_normed0, normed0], axis=0))

    one = ((pooled_rows, D), BF)
    spread = ((D // LANES, rows, LANES), FL)
    normed1, inputs1, grouped = whole(
        4,
        pool_kernel,
        [info],
        [full0, edge, vectors],
        [(pool_weight, None)],
        [one, ((pooled_rows, D), FL), ((pooled_rows, 3 * D), BF)],
        [((D // LANES, rows + 8, LANES), FL)],
    )
    if usual:
        normed1_all = gather_pooled(normed1)
    else:
        normed1_all = lax.all_gather(normed1, "seq", axis=0, tiled=True)
    content1, position1, table1 = whole(
        4,
        pooled_project_kernel,
        [],
        [normed1, vectors, far_table],
        [(w_in, 1)],
        [one, one, (far_table.shape, BF)],
    )
    mixed1, keys1, values1, weights1 = pooled_attention(
        pooled_info, order, content1, position1, normed1_all, w_in, table1
    )
    if usual:
        (mixed1,), x0, n0 = together((mixed1,), x0, n0)
    middle1, slope1, pack1, normed2, inputs2, squares1 = whole(
        7,
        pooled_feed_kernel,
        [],
        [mixed1, inputs1, grouped, full0, vectors],
        [(w, 1) for w in ff_weights] + [(upsample_weight, None)],
        [
            ((pooled_rows, D), FL),
            ((pooled_rows, 4 * D), BF),
            ((pooled_rows, 10 * D), BF),
            ((rows, D), BF),
            ((rows, D), FL),
            ((1, D), FL),
        ],
        [spread],
    )

    border2 = passed_along(normed2[rows - WIN :], "seq", 1)
    *heads2, table2 = window_project(2, normed2, vectors, near_table, w_in, False)
    mixed2, edge_normed2, border2, weights2 = window_attention(
        2, False, info, heads2, border2, vectors, w_in, table2
    )
    x1, n2 = swapped(pack1), swapped(jnp.concatenate([edge_normed2, normed2], axis=0))
    if usual:
        (mixed2,), x1, n2 = together((mixed2,), x1, n2)
    middle2, slope2, pack2, output, squares2 = window_feed(
        2, mixed2, inputs2, vectors, ff_weights, BF
    )

    share = D // seq_count
    shapes = [
        (3, share, 4 * D),
        (3, share, D),
        (3, share, 4 * D),
        (3, 4 * share, D),
        (3 * share, D),
        (share, 3 * D),
    ]

    every = {"near": (near_table,), "far": (far_table,)}

    def feed_pieces(x, dy, layer):
        pieces = [
            plain_piece(x, D, D, dy, 0, 2 * D),
            plain_piece(x, 2 * D, 4 * D, dy, 2 * D, D // 2),
            plain_piece(x, 0, D, dy, 2 * D + D // 2, D // 2),
        ]
        targets = [
            (2, layer, 0, 4 * D, share),
            (3, layer, 0, D, 4 * share),
            (1, layer, 0, D, share),
        ]
        return pieces, targets

    def project_targets(layer):
        return [(0, layer, index * D, D, share) for index in range(4)]

    feed2 = feed_pieces("x2", "a2", 2)
    project2 = [window_piece("n2", "b2", "near")], project_targets(2)
    up = [upsample_piece("x1", 6 * D, "u2")], [(5, None, 0, 3 * D, share)]
    feed1 = feed_pieces("x1", "a1", 1)
    project1 = [pooled_piece("n1", "b1", "far")], project_targets(1)
    pool = [plain_piece("x1", 7 * D, 3 * D, "p1", 0, D // 2)], [(4, None, 0, D, 3 * share)]
    feed0 = feed_pieces("x0", "a0", 0)
    project0 = [window_piece("n0", "b0", "near")], project_targets(0)

    def gradients(names, follows, *parts):
        if not usual:
            return ()
        pieces = sum((part[0] for part in parts), [])
        sources = {name: every[name] for name in names}
        first = names[0]
        sources[first], _ = together(sources[first], follows)
        return tuple(pair_gradients(7, place, sources, pieces))

    def step(function, values, *options):
        return tuple(function(*values, *options)) if usual else ()

    back_weights = [w_contract, w_expand, w_out]
    x2 = swapped(pack2)
    every["x0"], every["x1"], every["x2"] = x0, x1, x2
    every["n0"], every["n1"], every["n2"] = n0, (normed1_all,), n2

    def swapped_pack(pack):
        return (pack, crossed(pack[1], "seq", 1)) if usual else pack

    middle_grad2, mixed_grad2, own_a2, other_a2, small_a2 = feed_back(
        partial(feed_backward_kernel, 2),
        2,
        place,
        [cotangent[0], slope2, middle2, vectors],
        rows,
        back_weights,
    )
    every["a2"] = swapped_halves(own_a2, other_a2)
    if usual:
        (mixed_grad2,), every["x2"] = together((mixed_grad2,), x2)
    bias2, leaving2, grads2 = window_attention_back(
        2, place, heads2, border2, w_in, table2, weights2, mixed_grad2
    )
    returned2 = passed_along(leaving2, "seq", -1)
    every["b2"] = swapped_pack(grads2)
    group2a = gradients(("a2", "x2", "b2", "n2", "near"), (bias2,), feed2, project2)
    (returned2,), group2a = together((returned2,), group2a)
    group2a = step(first_step, group2a)
    joined, short_grad, own_u2, other_u2, small_b2 = whole(
        6,
        last_project_backward_kernel,
        [place],
        [Part(grads2, (2, REACH, 3 * D // 2)), returned2, inputs2, middle_grad2, vectors],
        [(w_in, 2), (upsample_weight, None)],
        [
            ((rows, D), FL),
            ((pooled_rows, D), FL),
            ((rows, D // 2), BF),
            ((rows, D // 2), BF),
            ((8, D), FL),
        ],
        [spread],
    )
    every["u2"] = swapped_halves(own_u2, other_u2)

    middle_grad1, mixed_grad1, own_a1, other_a1, small_a1 = feed_back(
        partial(feed_backward_kernel, 1),
        1,
        place,
        [short_grad, slope1, middle1, vectors],
        pooled_rows,
        back_weights,
    )
    every["a1"] = swapped_halves(own_a1, other_a1)
    (mixed_grad1,), group2a = together((mixed_grad1,), group2a)
    group2a = step(first_sums, (group2a,))
    (mixed_grad1,), group2a = together((mixed_grad1,), group2a)
    group2a = step(second_step, group2a)
    heads1 = (content1, position1, keys1, values1)
    bias1, even, odd, grads1 = pooled_attention_back(
        order, place, heads1, w_in, table1, weights1, mixed_grad1
    )
    every["b1"] = swapped_pack(grads1)

    def group1_gradients(total):
        return gradients(("a1", "x1", "u2"), (total,), up, feed1)

    if usual:
        (even, odd), group2a = together((even, odd), group2a)
        normed_grad1, group1 = scatter_pooled(even, odd, group1_gradients)
    else:
        group1 = ()
        split = (seq_count // 2, 1, LANES, D)
        summed = jnp.concatenate([even.reshape(split), odd.reshape(split)], axis=1)
        summed = summed.reshape(seq_count * LANES, D)
        normed_grad1 = lax.psum_scatter(summed, "seq", scatter_dimension=0, tiled=True).astype(FL)
    (normed_grad1,), group1, group2a = together((normed_grad1,), group1, group2a)
    group1 = step(first_step, group1)
    group2a = step(second_sums, group2a)
    group2a = step(depth_halves, group2a, depth)
    shifted_grad, own_p1, other_p1, small_b1 = whole(
        5,
        pooled_project_backward_kernel,
        [info, place],
        [Part(grads1, (2, LANES, D // 2)), normed_grad1, inputs1, middle_grad1, vectors],
        [(w_in, 1), (pool_weight, None)],
        [((rows, D), FL), ((pooled_rows, D // 2), BF), ((pooled_rows, D // 2), BF), ((8, D), FL)],
        [spread],
    )
    every["p1"] = swapped_halves(own_p1, other_p1)
    came_back = passed_along(shifted_grad[:2], "seq", -1)
    group1b = gradients(("p1", "x1", "b1", "n1", "far"), (shifted_grad,), pool, project1)
    (came_back,), group1b, group2a = together((came_back,), group1b, group2a)
    group1b = step(first_step, group1b)
    group2a = step(depth_quarters, group2a)
    middle_grad0, mixed_grad0, own_a0, other_a0, small_a0 = feed_back(
        first_feed_backward_kernel,
        0,
        place,
        [joined, shifted_grad, came_back, slope0, middle0, vectors],
        rows,
        back_weights,
        [((rows + 8, D), FL)],
    )
    every["a0"] = swapped_halves(own_a0, other_a0)
    (mixed_grad0,), group1, group1b = together((mixed_grad0,), group1, group1b)
    group1 = step(first_sums, (group1, group1b))
    (mixed_grad0,), group1 = together((mixed_grad0,), group1)
    group1 = step(second_step, group1)
    bias0, leaving0, grads0 = window_attention_back(
        0, place, heads0, border0, w_in, table0, weights0, mixed_grad0
    )
    every["b0"] = swapped_pack(grads0)
    returned0 = passed_along(leaving0, "seq", -1)

    clock = (bias0,)
    if usual:
        clock, group1, group2a = together(clock, group1, group2a)
        group1 = step(second_sums, group1)
        group1 = step(depth_halves, group1, depth)
        group2a = step(depth_back, group2a)
        group0 = gradients(("a0", "x0"), clock, feed0)
        clock, group0 = together(clock, group0)
        group0 = step(first_step, group0)
        last = gradients(("b0", "n0", "near"), clock, project0)
        clock, last = together(clock, last)
        last = step(first_step, last)
    (returned0,), clock = together((returned0,), clock)
    tokens_grad, small_b0 = whole(
        5,
        first_project_backward_kernel,
        [place],
        [Part(grads0, (2, REACH, 3 * D // 2)), returned0, inputs, middle_grad0, vectors],
        [(w_in, 0)],
        [((rows, D), BF), ((8, D), FL)],
    )
    small = jnp.concatenate(
        [
            small_b0[:2],
            small_b1[:3],
            small_b2[:5],
            small_a0[:7],
            small_a1[:7],
            small_a2[:7],
            bias0,
            bias1,
            bias2,
            squares0,
            squares1,
            squares2,
        ],
        axis=0,
    )
    if usual:
        clock, (small,), group1 = together(clock, (small,), group1)
        group1 = step(depth_quarters, group1)
        small = small + crossed(small, "seq", 1)
        clock, (small,), group0 = together(clock, (small,), group0)
        group0 = step(first_sums, (group0,))
        group0 = step(second_step, group0)
        small = small + crossed(small, "seq", 2)
        clock, (small,), last = together(clock, (small,), last)
        last = step(first_sums, (last,))
        last = step(second_step, last)
        small = small + crossed(small, "seq", 4)
        clock, (small,), group0, group1 = together(clock, (small,), group0, group1)
        group0 = step(second_sums, group0)
        group0 = step(depth_halves, group0, depth)
        group1 = step(depth_back, group1)
        clock, last = together(clock, last)
        last = step(second_sums, last)
        last = step(depth_halves, last, depth)
        clock, group0 = together(clock, group0)
        group0 = step(depth_quarters, group0)
        clock, last, group1 = together(clock, last, group1)
        last = step(depth_quarters, last)
        small = small + crossed(small, "dp", 1)
        clock, (small,), group0 = together(clock, (small,), group0)
        group0 = step(depth_back, group0)
        clock, last = together(clock, last)
        last = step(depth_back, last)
        small = small + crossed(small, "dp", 2)
        plan = [feed2[1] + project2[1], up[1] + feed1[1] + pool[1] + project1[1]]
        plan += [feed0[1], project0[1]]
        buffers = [shared(*group, depth, core) for group in (group2a, group1, group0, last)]
        sums = final_outputs(plan, buffers, shapes)
    else:
        small = summed_everywhere(small)
        sums = plain_sums(
            shapes,
            core,
            (pack0, pack1, pack2),
            (every["n0"], normed1, every["n2"]),
            (every["n0"], normed1_all, every["n2"]),
            (every["a0"], every["a1"], every["a2"]),
            (grads0, grads1, grads2),
            every["p1"],
            every["u2"],
            (near_table, far_table),
        )
    in_grad, out_grad, expand_grad, contract_grad = [by_layer(total) for total in sums[:4]]

    gain, shift, expand_sum, contract_sum = [], [], [], []
    for layer, b in enumerate((0, 2, 5)):
        a = 10 + 7 * layer
        gain.append(jnp.stack([small[b], small[a + 1]]))
        shift.append(jnp.stack([small[b + 1], small[a + 2]]))
        contract_sum.append(small[a])
        expand_sum.append(small[a + 3 : a + 7].reshape(4 * D))
    bias_sum = small[31:37].reshape(3, 2, D)
    whole_rows = lax.axis_size("dp") * seq_count * rows * D
    counts = jnp.array([whole_rows, whole_rows // 3, whole_rows], FL)
    rms = jnp.sqrt(jnp.sum(small[37:40], axis=1) / counts)
    return (
        output[None],
        tokens_grad[None],
        jnp.stack(gain),
        jnp.stack(shift),
        bias_sum,
        in_grad,
        out_grad,
        expand_grad,
        jnp.stack(expand_sum),
        contract_grad,
        jnp.stack(contract_sum),
        sums[4],
        small[4],
        sums[5],
        small[7:10].reshape(3 * D),
        rms,
    )


def plain_sums(
    shapes, core, packs, normed, normed_all, a_pairs, grads, pool_pair, up_pair, tables
):
    def full(pair, start, half):
        own, other = (array[:, start : start + half] for array in pair)
        return jnp.concatenate(both(own, other, core), axis=1)

    def summed(features, grad):
        total = outer_float(features, grad).astype(BF)
        total = lax.psum_scatter(total, "seq", scatter_dimension=0, tiled=True)
        return lax.psum(total, "dp").astype(FL)

    into, out, expand, contract = [], [], [], []
    for layer in range(3):
        x, a, b = packs[layer], a_pairs[layer], (grads[layer][0], grads[layer][1])
        table, near, every = tables[layer % 2], normed[layer], normed_all[layer]
        own = x.shape[0]
        near = near[near.shape[0] - own :]
        columns = [
            summed(near, full(b, 0, D // 2)[:own]),
            summed(every, full(b, D // 2, D // 2)[: every.shape[0]]),
            summed(every, full(b, D, D // 2)[: every.shape[0]]),
            summed(table, full(b, 3 * D // 2, D // 2)[: table.shape[0]]),
        ]
        into.append(jnp.concatenate(columns, axis=1))
        out.append(summed(x[:, :D], full(a, 2 * D + D // 2, D // 2)))
        expand.append(summed(x[:, D : 2 * D], full(a, 0, 2 * D)))
        contract.append(summed(x[:, 2 * D : 6 * D], full(a, 2 * D, D // 2)))
    pool = summed(packs[1][:, 7 * D :], full(pool_pair, 0, D // 2))
    sides = []
    for array in up_pair:
        parts = [array[index * LANES : (index + 1) * LANES] for index in range(3)]
        sides.append(jnp.concatenate(parts, axis=1))
    up = summed(packs[1][:, 6 * D : 7 * D], jnp.concatenate(both(*sides, core), axis=1))
    stacks = [jnp.stack(parts) for parts in (into, out, expand, contract)]
    return stacks + [pool, up]


def solution(mesh):
    rows = P("dp", "seq", None)
    in_specs = (rows, P("dp", None), rows) + (P(),) * 13
    split = P("seq", None, None)
    flat = P("seq", None)
    out_specs = (rows, rows, P(), P(), P(), split, split, split, P(), split, P())
    out_specs += (flat, P(), flat, P(), P())
    return jax.shard_map(
        per_device, mesh=mesh, in_specs=in_specs, out_specs=out_specs, check_vma=False
    )
```

```python
import math
from functools import partial

import jax
import jax.numpy as jnp
from jax import lax
from jax.experimental import pallas as pl
from jax.experimental.pallas import tpu as pltpu
from jax.sharding import PartitionSpec as P

D = 512
HEADS = 8
HD = 64
WIN = 256
QBLK = 384
DOCS = 8
EDGE = 16
epsilon = 1e-05
GAIN, SHIFT, BIAS, CONTRACT, EXPAND, POOL, UP = 0, 6, 12, 18, 21, 33, 34

VMEM = pl.BlockSpec(memory_space=pltpu.VMEM)
SMEM = pl.BlockSpec(memory_space=pltpu.SMEM)
HBM = pl.BlockSpec(memory_space=pltpu.HBM)
ANY = pl.BlockSpec(memory_space=pl.ANY)


LANES = 128
PAIR = 2 * HD
MASKED = -1e30
PARTS = QBLK // LANES
SEEN = LANES + WIN
REACH = QBLK + WIN


def nt(first, second):
    return lax.dot_general(
        first, second, (((1,), (1,)), ((), ())), preferred_element_type=jnp.float32
    )


def nn(first, second):
    return lax.dot_general(
        first, second, (((1,), (0,)), ((), ())), preferred_element_type=jnp.float32
    )


def tn(first, second):
    return lax.dot_general(
        first, second, (((0,), (0,)), ((), ())), preferred_element_type=jnp.float32
    )


def document(places, info):
    total = jnp.zeros(places.shape, jnp.int32)
    for index in range(DOCS):
        total = total + (places >= info[1 + index]).astype(jnp.int32)
    return total


def lanes_and_rows():
    lane = lax.broadcasted_iota(jnp.int32, (LANES, LANES), 1)
    row = lax.broadcasted_iota(jnp.int32, (LANES, LANES), 0)
    return lane, row


def turned(values, index):
    return [
        jnp.take_along_axis(values[:, m * LANES : (m + 1) * LANES], index, axis=1)
        for m in range(values.shape[1] // LANES)
    ]


def skew_window(table):
    lane, row = lanes_and_rows()
    blocks = turned(table, (lane - row + LANES) % LANES)
    out = [blocks[0]] + [
        jnp.where(lane >= row, here, before) for before, here in zip(blocks, blocks[1:])
    ]
    return jnp.concatenate(out, axis=1)


def unskew_window(scores):
    lane, row = lanes_and_rows()
    blocks = turned(scores, (lane + row) % LANES)
    blocks.append(jnp.zeros_like(blocks[0]))
    out = [
        jnp.where(lane + row < LANES, here, after) for here, after in zip(blocks, blocks[1:])
    ]
    return jnp.concatenate(out, axis=1)


def unskew_pooled(scores):
    lane, row = lanes_and_rows()
    (block,) = turned(scores, (lane + row + 1) % LANES)
    zero = jnp.zeros_like(block)
    first = lane + row >= LANES - 1
    return jnp.concatenate([jnp.where(first, block, zero), jnp.where(first, zero, block)], axis=1)


def stacked(rows):
    head = lax.broadcasted_iota(jnp.int32, rows.shape, 1) // HD
    zero = jnp.zeros_like(rows)
    return jnp.concatenate([jnp.where(head == 0, rows, zero), jnp.where(head == 1, rows, zero)], axis=0)


def unstacked(rows):
    count = rows.shape[0] // 2
    head = lax.broadcasted_iota(jnp.int32, (count, PAIR), 1) // HD
    return jnp.where(head == 0, rows[:count], rows[count:])


def softmax_rows(scores):
    highest = jnp.max(scores, axis=1, keepdims=True)
    powers = jnp.exp(scores - highest)
    return powers * (1.0 / jnp.sum(powers, axis=1, keepdims=True))


def window_mask(info, part):
    place = info[0] + part * LANES
    row = lax.broadcasted_iota(jnp.int32, (LANES, SEEN), 0)
    column = lax.broadcasted_iota(jnp.int32, (LANES, SEEN), 1)
    behind = row + WIN - column
    query = place + lax.broadcasted_iota(jnp.int32, (LANES, 1), 0)
    key = place - WIN + lax.broadcasted_iota(jnp.int32, (1, SEEN), 1)
    same = document(query, info) == document(key, info)
    return (behind >= 0) & (behind <= WIN) & same & (key >= 0)


def pooled_mask(info, start):
    query = info[0] + lax.broadcasted_iota(jnp.int32, (LANES, 1), 0)
    key = start + lax.broadcasted_iota(jnp.int32, (1, LANES), 1)
    return (key <= query) & (document(3 * query, info) == document(3 * key, info))


def column_sums(first, second):
    return jnp.concatenate(
        [jnp.sum(first, axis=0, keepdims=True), jnp.sum(second, axis=0, keepdims=True)], axis=0
    )


def backward_scores(weights, grad_weights):
    delta = jnp.sum(weights * grad_weights, axis=1, keepdims=True)
    return weights * (grad_weights - delta)


def window_forward_kernel(
    raw,
    info,
    content,
    position,
    keys,
    values,
    border,
    gain,
    shift,
    key_weight,
    value_weight,
    table,
    mixed_ref,
    normed_ref,
    border_ref,
    weights_ref,
    bias,
    normed,
    places,
):
    pair = pl.program_id(0)

    @pl.when(pair == 0)
    def _():
        if raw is None:
            normed[...] = border[...]
        else:
            hat, _ = normalised(border[...].astype(jnp.float32))
            scale = gain[raw].astype(jnp.float32)[0:1, :]
            normed[...] = (hat * scale + shift[raw].astype(jnp.float32)[0:1, :]).astype(jnp.bfloat16)
        normed_ref[...] = normed[...]
        for part in range(PARTS):
            bias[part] = jnp.where(window_mask(info, part), 0.0, MASKED)

    border_keys = nn(normed[...], key_weight[...]).astype(jnp.bfloat16)
    border_values = nn(normed[...], value_weight[...]).astype(jnp.bfloat16)
    border_ref[0] = border_keys
    border_ref[1] = border_values
    all_keys = jnp.concatenate([border_keys, keys[...]], axis=0)
    all_values = jnp.concatenate([border_values, values[...]], axis=0)
    scale = jnp.asarray(HD**-0.5, jnp.bfloat16)
    order = [
        stacked(position[part * LANES : (part + 1) * LANES, :] * scale) for part in range(PARTS)
    ]
    places[...] = nt(jnp.concatenate(order, axis=0), table[...])
    for part in range(PARTS):
        rows = slice(part * LANES, (part + 1) * LANES)
        seen = slice(part * LANES, part * LANES + SEEN)
        scores = nt(stacked(content[rows, :] * scale), all_keys[seen])
        weights = []
        for index in range(2):
            start = (2 * part + index) * LANES
            score = scores[index * LANES : (index + 1) * LANES]
            score = score + skew_window(places[start : start + LANES, :]) + bias[part]
            weights.append(softmax_rows(score).astype(jnp.bfloat16))
            weights_ref[index, part] = weights[index]
        mixed = nn(jnp.concatenate(weights, axis=0), all_values[seen])
        mixed_ref[rows, :] = unstacked(mixed).astype(jnp.bfloat16)


def window_backward_kernel(
    place,
    content,
    position,
    keys,
    values,
    border,
    key_weight,
    value_weight,
    table,
    weights,
    grad,
    bias_ref,
    returned_ref,
    own_pack,
    other_pack,
    dk_sum,
    dv_sum,
    returned,
    places,
    dq_out,
    dk_out,
    dv_out,
    dt_out,
    sems,
):
    pair = pl.program_id(0)
    all_keys = jnp.concatenate([border[0], keys[...]], axis=0)
    all_values = jnp.concatenate([border[1], values[...]], axis=0)
    scale = HD**-0.5
    low_scale = jnp.asarray(scale, jnp.bfloat16)
    dk_sum[...] = jnp.zeros_like(dk_sum)
    dv_sum[...] = jnp.zeros_like(dv_sum)
    contents = []
    for part in range(PARTS):
        rows = slice(part * LANES, (part + 1) * LANES)
        seen = slice(part * LANES, part * LANES + SEEN)
        grads = stacked(grad[rows, :])
        grad_weights = nt(grads, all_values[seen])
        scores, lows = [], []
        for index in range(2):
            low = weights[index, part]
            score = backward_scores(
                low.astype(jnp.float32), grad_weights[index * LANES : (index + 1) * LANES]
            ).astype(jnp.bfloat16)
            start = (2 * part + index) * LANES
            places[start : start + LANES, :] = unskew_window(score.astype(jnp.float32)).astype(
                jnp.bfloat16
            )
            scores.append(score)
            lows.append(low)
        scores = jnp.concatenate(scores, axis=0)
        contents.append(unstacked(nn(scores, all_keys[seen])) * scale)
        dk_sum[seen, :] += tn(scores, stacked(content[rows, :] * low_scale))
        dv_sum[seen, :] += tn(jnp.concatenate(lows, axis=0), grads)
    order = [
        stacked(position[part * LANES : (part + 1) * LANES, :] * low_scale)
        for part in range(PARTS)
    ]
    to_position = nn(places[...], table[...]) * scale
    positions = [
        unstacked(to_position[2 * part * LANES : 2 * (part + 1) * LANES]) for part in range(PARTS)
    ]
    grad_content = jnp.concatenate(contents, axis=0)
    grad_position = jnp.concatenate(positions, axis=0)
    bias_ref[...] = column_sums(grad_content, grad_position)
    slot = pair % 2
    grad_keys = dk_sum[...].astype(jnp.bfloat16)
    grad_values = dv_sum[...].astype(jnp.bfloat16)
    dq_out[slot] = (grad_content + grad_position).astype(jnp.bfloat16)
    dk_out[slot] = grad_keys
    dv_out[slot] = grad_values
    dt_out[slot] = tn(places[...], jnp.concatenate(order, axis=0)).astype(jnp.bfloat16)
    outs = (dq_out, dk_out, dv_out, dt_out)
    send_pack(place, pair, (own_pack, other_pack), outs, sems)
    back = nt(grad_keys[:WIN], key_weight[...]) + nt(grad_values[:WIN], value_weight[...])

    @pl.when(pair == 0)
    def _():
        returned[...] = back

    @pl.when(pair != 0)
    def _():
        returned[...] += back

    @pl.when(pair == HEADS // 2 - 1)
    def _():
        returned_ref[...] = returned[...].astype(jnp.bfloat16)


def pack_copies(place, pair, packs, outs, sems, act):
    for slot, pack in enumerate(packs):

        @pl.when((pair // 2) ^ place[1] == slot)
        def _(pack=pack):
            for index, out in enumerate(outs):
                lane = pl.multiple_of(index * D // 2 + pair % 2 * PAIR, PAIR)
                source = out.at[pair % 2]
                target = pack.at[pl.ds(0, source.shape[0]), pl.ds(lane, PAIR)]
                act(pltpu.make_async_copy(source, target, sems.at[pair % 2, index]))


def send_pack(place, pair, packs, outs, sems):
    def start(copy):
        copy.start()

    def wait(copy):
        copy.wait()

    pack_copies(place, pair, packs, outs, sems, start)

    @pl.when(pair > 0)
    def _():
        pack_copies(place, pair - 1, packs, outs, sems, wait)

    @pl.when(pair == HEADS // 2 - 1)
    def _():
        pack_copies(place, pair, packs, outs, sems, wait)


def table_rows(order, block, count):
    start = jnp.minimum(order[block] + count - 1 - order[count], count - 1)
    return pl.ds(pl.multiple_of(LANES * start, LANES), 2 * LANES)


def table_lanes(order, block, count, offset):
    start = jnp.minimum(order[block] + count - 1 - order[count], count - 1) + offset
    return pl.ds(pl.multiple_of(LANES * start, LANES), LANES)


def pooled_forward_kernel(
    info,
    order,
    content,
    position,
    normed,
    key_weight,
    value_weight,
    table,
    mixed_ref,
    keys_ref,
    values_ref,
    weights_ref,
    bias,
    places,
):
    count = normed.shape[0] // LANES

    @pl.when(pl.program_id(0) == 0)
    def _():
        for block in range(count):
            visible = pooled_mask(info, LANES * order[block])
            bias[block] = jnp.where(visible, 0.0, MASKED)

    scale = jnp.asarray(HD**-0.5, jnp.bfloat16)
    keys_ref[...] = nn(normed[...], key_weight[...]).astype(jnp.bfloat16)
    values_ref[...] = nn(normed[...], value_weight[...]).astype(jnp.bfloat16)
    scores = nt(stacked(content[...] * scale), keys_ref[...])
    lane, row = lanes_and_rows()
    place = nt(stacked(position[...] * scale), table[...])
    turn = (lane + LANES - 1 - row) % LANES
    rows = [[], []]
    for index in range(2):
        half = slice(index * LANES, (index + 1) * LANES)
        places[half, :] = jnp.concatenate(turned(place[half], turn), axis=1)
        for block in range(count):
            here = places[half, table_lanes(order, block, count, 0)]
            there = places[half, table_lanes(order, block, count, 1)]
            score = scores[half, block * LANES : (block + 1) * LANES]
            rows[index].append(score + jnp.where(lane <= row, here, there) + bias[block])
    weights = []
    for index in range(2):
        weight = softmax_rows(jnp.concatenate(rows[index], axis=1)).astype(jnp.bfloat16)
        weights_ref[index] = weight
        weights.append(weight)
    mixed = nn(jnp.concatenate(weights, axis=0), values_ref[...])
    mixed_ref[...] = unstacked(mixed).astype(jnp.bfloat16)


def pooled_backward_kernel(
    order,
    place,
    content,
    position,
    keys,
    values,
    key_weight,
    value_weight,
    table,
    weights,
    grad,
    bias_ref,
    even_ref,
    odd_ref,
    own_pack,
    other_pack,
    table_sum,
    total,
    dq_out,
    dk_out,
    dv_out,
    dt_out,
    sems,
):
    pair = pl.program_id(0)
    count = keys.shape[0] // LANES
    scale = HD**-0.5
    low_scale = jnp.asarray(scale, jnp.bfloat16)
    table_sum[...] = jnp.zeros_like(table_sum)
    grads = stacked(grad[...])
    grad_weights = nt(grads, values[...])
    lows = jnp.concatenate([weights[0], weights[1]], axis=0)
    scores = backward_scores(lows.astype(jnp.float32), grad_weights)
    low_scores = scores.astype(jnp.bfloat16)
    grad_content = unstacked(nn(low_scores, keys[...])) * scale
    positions = stacked(position[...] * low_scale)
    to_position = jnp.zeros((2 * LANES, PAIR), jnp.float32)
    for block in range(count):
        rows = table_rows(order, block, count)
        lanes = slice(block * LANES, (block + 1) * LANES)
        parts = []
        for index in range(2):
            half = low_scores[index * LANES : (index + 1) * LANES, lanes]
            parts.append(unskew_pooled(half.astype(jnp.float32)).astype(jnp.bfloat16))
        parts = jnp.concatenate(parts, axis=0)
        to_position = to_position + nn(parts, table[rows, :])
        table_sum[rows, :] += tn(parts, positions)
    grad_position = unstacked(to_position) * scale
    bias_ref[...] = column_sums(grad_content, grad_position)
    slot = pair % 2
    grad_keys = tn(low_scores, stacked(content[...] * low_scale)).astype(jnp.bfloat16)
    grad_values = tn(lows, grads).astype(jnp.bfloat16)
    dq_out[slot] = (grad_content + grad_position).astype(jnp.bfloat16)
    dk_out[slot] = grad_keys
    dv_out[slot] = grad_values
    dt_out[slot] = table_sum[...].astype(jnp.bfloat16)
    outs = (dq_out, dk_out, dv_out, dt_out)
    send_pack(place, pair, (own_pack, other_pack), outs, sems)
    back = nt(grad_keys, key_weight[...]) + nt(grad_values, value_weight[...])

    @pl.when(pair == 0)
    def _():
        total[...] = back

    @pl.when(pair != 0)
    def _():
        total[...] += back

    @pl.when(pair == HEADS // 2 - 1)
    def _():
        for block in range(count):
            target = (even_ref, odd_ref)[block % 2]
            start = block // 2 * LANES
            rows = total[block * LANES : (block + 1) * LANES, :]
            target[start : start + LANES, :] = rows.astype(jnp.bfloat16)


def by_pair(shape, first=0):
    front = tuple(shape[:-1])
    zeros = (0,) * len(front)
    return pl.BlockSpec(front + (PAIR,), lambda pair: zeros + (first + pair,))


def entire(shape):
    zeros = (0,) * len(shape)
    return pl.BlockSpec(tuple(shape), lambda pair: zeros)


def of_layer(shape, layer, first):
    return pl.BlockSpec((None, shape[1], PAIR), lambda pair: (layer, 0, first + pair))


def weights_block(shape):
    return pl.BlockSpec((2,) + tuple(shape[1:]), lambda pair: (pair,) + (0,) * (len(shape) - 1))


def attention_call(micros, kernel, scalars, operands, outs, scratch, mib, follows=()):
    first = len(scalars) + len(operands)

    def run(*refs):
        kernel(*refs[:first], *refs[first + len(follows) :])

    return pl.pallas_call(
        run,
        grid=(HEADS // 2,),
        in_specs=[SMEM] * len(scalars) + [spec for _, spec in operands] + [HBM] * len(follows),
        out_specs=[HBM if spec is None else spec for _, _, spec in outs],
        out_shape=[pltpu.HBM(shape, kind) for shape, kind, _ in outs],
        scratch_shapes=scratch,
        compiler_params=pltpu.CompilerParams(vmem_limit_bytes=mib * 2**20),
        cost_estimate=lasting(micros),
    )(*scalars, *[in_hbm(array) for array, _ in operands], *[in_hbm(a) for a in follows])


def vector(vectors, row):
    gain, shift, bias, contract, expand, pool, up = vectors
    for start, ref in ((GAIN, gain), (SHIFT, shift), (BIAS, bias)):
        if start <= row < start + 6:
            layer, index = divmod(row - start, 2)
            return ref[layer].astype(jnp.float32)[index : index + 1, :]
    if row < EXPAND:
        return contract[...].astype(jnp.float32)[row - CONTRACT : row - CONTRACT + 1, :]
    if row < POOL:
        layer, part = divmod(row - EXPAND, 4)
        lanes = slice(part * D, (part + 1) * D)
        return expand[:, lanes].astype(jnp.float32)[layer : layer + 1, :]
    if row < UP:
        return pool[...].astype(jnp.float32)
    part = row - UP
    return up[:, part * D : (part + 1) * D].astype(jnp.float32)


def normalised(values):
    centre = values - jnp.mean(values, axis=1, keepdims=True)
    spread = jnp.mean(centre * centre, axis=1, keepdims=True)
    rate = lax.rsqrt(spread + epsilon)
    return centre * rate, rate


def norm_forward(values, vectors, layer, index):
    hat, _ = normalised(values)
    gain = vector(vectors, GAIN + 2 * layer + index)
    return (hat * gain + vector(vectors, SHIFT + 2 * layer + index)).astype(jnp.bfloat16)


def norm_backward(values, vectors, layer, index, grad):
    hat, rate = normalised(values)
    scaled = grad * vector(vectors, GAIN + 2 * layer + index)
    mean = jnp.mean(scaled, axis=1, keepdims=True)
    along = jnp.mean(scaled * hat, axis=1, keepdims=True)
    result = rate * (scaled - mean - hat * along)
    return result, jnp.sum(grad * hat, axis=0, keepdims=True), jnp.sum(grad, axis=0, keepdims=True)


class Copies:
    def __init__(self, sems):
        self.sems, self.used, self.open = sems, 0, []

    def start(self, source, target):
        copy = pltpu.make_async_copy(source, target, self.sems.at[self.used])
        self.used += 1
        copy.start()
        return copy

    def send(self, source, target):
        self.open.append(self.start(source, target))

    def finish(self):
        for copy in self.open:
            copy.wait()


class Output:
    def __init__(self, buffer, target, copies):
        self.buffer, self.target, self.copies, self.sent = buffer, target, copies, False
        self.shape, self.dtype = buffer.shape, buffer.dtype

    def __setitem__(self, index, value):
        self.buffer[index] = value

    def __getitem__(self, index):
        return self.buffer[index]

    def send(self, lanes=None):
        self.sent = True
        if lanes is None:
            self.copies.send(self.buffer, self.target)
        else:
            self.copies.send(self.buffer.at[:, lanes], self.target.at[:, lanes])


def write_table(frequency, first, out):
    step = 32
    count = out.shape[0]

    def waves(start, change, rows):
        distance = start + change * lax.broadcasted_iota(jnp.int32, (rows, 1), 0)
        angle = distance.astype(jnp.float32) * frequency[...]
        return jnp.sin(angle), jnp.cos(angle)

    high_sin, high_cos = waves(first, -step, count // step)
    low_sin, low_cos = waves(0, -1, step)
    for index in range(count // step):
        rows = slice(index * step, (index + 1) * step)
        sine, cosine = high_sin[index : index + 1], high_cos[index : index + 1]
        out[rows, : D // 2] = (sine * low_cos + cosine * low_sin).astype(jnp.bfloat16)
        out[rows, D // 2 :] = (cosine * low_cos - sine * low_sin).astype(jnp.bfloat16)
    out.send()


def queries(layer, normed, vectors, weight, content, position):
    value = nn(normed, weight[:, :D])
    content[...] = (value + vector(vectors, BIAS + 2 * layer)).astype(jnp.bfloat16)
    position[...] = (value + vector(vectors, BIAS + 2 * layer + 1)).astype(jnp.bfloat16)
    content.send()
    position.send()


def window_project_kernel(
    layer, inputs, vectors, embedded, w_in, content, position, keys, values, table, *more
):
    weight, copy = w_in
    rows = inputs[...]
    if more:
        normed, waves = more
        rows = norm_forward(rows.astype(jnp.float32), vectors, layer, 0)
        normed[...] = rows
        normed.send()
        write_table(embedded, WIN, waves)
        embedded = waves
    copy.wait()
    queries(layer, rows, vectors, weight, content, position)
    for index, out in ((1, keys), (2, values)):
        out[...] = nn(rows, weight[:, index * D : (index + 1) * D]).astype(jnp.bfloat16)
        out.send()
    table[...] = nn(embedded[...], weight[:, 3 * D :]).astype(jnp.bfloat16)


def third_rows(ref, start):
    rows = pl.ds(start, LANES, stride=3)
    return jnp.concatenate([ref[index, rows, :] for index in range(D // LANES)], axis=1)


def put_third_rows(ref, start, values):
    for index in range(D // LANES):
        lanes = slice(index * LANES, (index + 1) * LANES)
        ref[index, pl.ds(start, LANES, stride=3), :] = values[:, lanes]


def put_rows(ref, start, values):
    for index in range(D // LANES):
        lanes = slice(index * LANES, (index + 1) * LANES)
        ref[index, start : start + values.shape[0], :] = values[:, lanes]


def all_rows(ref):
    return jnp.concatenate([ref[index] for index in range(D // LANES)], axis=1)


def kept(info, offset):
    count = LANES
    place = info[0] + 3 * lax.broadcasted_iota(jnp.int32, (count, 1), 0) + offset
    return (place >= 2) & (document(place - 2, info) == document(place, info))


def pool_kernel(info, full, edge, vectors, w_pool, normed, inputs, grouped, moved):
    pool_weight, pool_copy = w_pool
    put_rows(moved, 8, full[...])
    put_rows(moved, 6, edge[-2:, :].astype(jnp.float32))
    parts = []
    for offset in range(3):
        rows = third_rows(moved, offset + 6)
        parts.append(jnp.where(kept(info, offset), rows, 0.0).astype(jnp.bfloat16))
        grouped[:, offset * D : (offset + 1) * D] = parts[offset]
    pool_copy.wait()
    total = vector(vectors, POOL)
    for offset in range(3):
        total = total + nn(parts[offset], pool_weight[offset * D : (offset + 1) * D, :])
    normed[...] = norm_forward(total, vectors, 1, 0)
    normed.send()
    inputs[...] = total


def pooled_project_kernel(normed, vectors, frequency, w_in, content, position, table, waves):
    weight, copy = w_in
    write_table(frequency, waves.shape[0] - LANES - 1, waves)
    copy.wait()
    queries(1, normed[...], vectors, weight, content, position)
    table[...] = nn(waves[...], weight[:, 3 * D :]).astype(jnp.bfloat16)


def feed(layer, mixed, inputs, vectors, weights, middle_ref, slope, pack):
    w_out, w_expand, w_contract = [buffer for buffer, _ in weights]
    copies = [copy for _, copy in weights]
    pack[:, :D] = mixed[...]
    copies[0].wait()
    middle = inputs[...].astype(jnp.float32) + nn(mixed[...], w_out[...])
    middle_ref[...] = middle
    middle_ref.send()
    normed_two = norm_forward(middle, vectors, layer, 1)
    pack[:, D : 2 * D] = normed_two
    pack.send(slice(0, 2 * D))
    copies[1].wait()
    copies[2].wait()
    total = middle + vector(vectors, CONTRACT + layer)
    for part in range(4):
        lanes = slice(part * D, (part + 1) * D)
        value = nn(normed_two, w_expand[:, lanes]) + vector(vectors, EXPAND + 4 * layer + part)
        below = 0.5 + 0.5 * lax.erf(value * 0.5**0.5)
        density = jnp.exp(value * value * -0.5) * (0.5 / math.pi) ** 0.5
        slope[:, lanes] = (below + value * density).astype(jnp.bfloat16)
        active = (value * below).astype(jnp.bfloat16)
        pack[:, (2 + part) * D : (3 + part) * D] = active
        slope.send(lanes)
        pack.send(slice((2 + part) * D, (3 + part) * D))
        total = total + nn(active, w_contract[lanes, :])
    return total


def window_feed_kernel(
    layer,
    mixed,
    inputs,
    vectors,
    w_out,
    w_expand,
    w_contract,
    middle,
    slope,
    pack,
    result,
    squares,
    edge,
):
    weights = (w_out, w_expand, w_contract)
    total = feed(layer, mixed, inputs, vectors, weights, middle, slope, pack)
    result[...] = total.astype(result.dtype)
    edge[...] = total[-EDGE:].astype(jnp.bfloat16)
    squares[...] = jnp.sum(total * total, axis=0, keepdims=True)


def pooled_feed_kernel(
    mixed,
    inputs,
    grouped,
    full,
    vectors,
    w_out,
    w_expand,
    w_contract,
    w_up,
    middle,
    slope,
    pack,
    next_normed,
    result,
    squares,
    spread,
):
    weights = (w_out, w_expand, w_contract)
    total = feed(1, mixed, inputs, vectors, weights, middle, slope, pack)
    squares[...] = jnp.sum(total * total, axis=0, keepdims=True)
    low = total.astype(jnp.bfloat16)
    pack[:, 6 * D : 7 * D] = low
    pack[:, 7 * D :] = grouped[...]
    pack.send(slice(6 * D, 10 * D))
    up_buffer, copy = w_up
    copy.wait()
    for offset in range(3):
        raised = nn(low, up_buffer[:, offset * D : (offset + 1) * D])
        put_third_rows(spread, offset, raised + vector(vectors, UP + offset))
    raised = full[...] + all_rows(spread)
    next_normed[...] = norm_forward(raised, vectors, 2, 0)
    next_normed.send()
    result[...] = raised


def store_halves(core, own, other, offset, values):
    half = values.shape[1] // 2
    low = values[:, :half].astype(jnp.bfloat16)
    high = values[:, half:].astype(jnp.bfloat16)
    rows = values.shape[0]

    @pl.when(core == 0)
    def _():
        own[:rows, offset : offset + half] = low
        other[:rows, offset : offset + half] = high

    @pl.when(core != 0)
    def _():
        own[:rows, offset : offset + half] = high
        other[:rows, offset : offset + half] = low


def feed_backward(
    layer,
    place,
    grad,
    slope,
    middle,
    vectors,
    w_contract,
    w_expand,
    w_out,
    middle_grad,
    mixed_grad,
    own,
    other,
    small,
):
    contract, expand, out = [weight[0] for weight in (w_contract, w_expand, w_out)]
    copies = [weight[1] for weight in (w_contract, w_expand, w_out)]
    core = place[1]
    branch = grad.astype(jnp.bfloat16)
    small[...] = jnp.zeros_like(small)
    small[0:1, :] = jnp.sum(branch.astype(jnp.float32), axis=0, keepdims=True)
    store_halves(core, own, other, 2 * D, branch)
    copies[0].wait()
    copies[1].wait()
    normed_grad = jnp.zeros(grad.shape, jnp.float32)
    changes = []
    for part in range(4):
        lanes = slice(part * D, (part + 1) * D)
        change = nt(branch, contract[lanes, :]) * slope[:, lanes].astype(jnp.float32)
        change = change.astype(jnp.bfloat16)
        changes.append(change)
        small[3 + part : 4 + part, :] = jnp.sum(
            change.astype(jnp.float32), axis=0, keepdims=True
        )
        normed_grad = normed_grad + nt(change, expand[:, lanes])
    store_halves(core, own, other, 0, jnp.concatenate(changes, axis=1))
    norm, gain, shift = norm_backward(middle[...], vectors, layer, 1, normed_grad)
    small[1:2, :] = gain
    small[2:3, :] = shift
    total = grad + norm
    middle_grad[...] = total
    attend = total.astype(jnp.bfloat16)
    store_halves(core, own, other, 2 * D + D // 2, attend)
    other.send()
    copies[2].wait()
    mixed_grad[...] = nt(attend, out[...]).astype(jnp.bfloat16)


def feed_backward_kernel(layer, place, grad, *refs):
    feed_backward(layer, place, grad[...].astype(jnp.float32), *refs)


def first_feed_backward_kernel(place, joined, shifted, came_back, *refs):
    moved = refs[-1]
    rows = shifted.shape[0]
    moved[:rows, :] = shifted[...]
    moved[rows : rows + 2, :] = came_back[:2, :]
    feed_backward(0, place, joined[...] + moved[2 : rows + 2, :], *refs[:-1])


def project_backward(layer, core, packs, rows, weight, extra, inputs, middle_grad, vectors, small):
    small[...] = jnp.zeros_like(small)
    normed_grad = extra
    for index, chosen in enumerate(rows):
        for slot in range(2):
            half = slot ^ core
            begin = pl.multiple_of(index * D + half * (D // 2), D // 2)
            grad = packs[slot][chosen, index * D // 2 : (index + 1) * D // 2]
            normed_grad = normed_grad + nt(grad, weight[:, pl.ds(begin, D // 2)])
    norm, gain, shift = norm_backward(inputs, vectors, layer, 0, normed_grad)
    small[0:1, :] = gain
    small[1:2, :] = shift
    return middle_grad[...] + norm


def window_project_backward(layer, core, packs, returned, weight, *rest):
    extra = jnp.concatenate(
        [jnp.zeros((QBLK - WIN, D), jnp.float32), returned[...].astype(jnp.float32)], axis=0
    )
    rows = (slice(0, QBLK), slice(WIN, REACH), slice(WIN, REACH))
    return project_backward(layer, core, packs, rows, weight, extra, *rest)


def first_project_backward_kernel(
    place, packs, returned, inputs, middle_grad, vectors, w_in, inputs_grad, small
):
    weight, copy = w_in
    copy.wait()
    rows = inputs[...].astype(jnp.float32)
    total = window_project_backward(
        0, place[1], packs, returned, weight, rows, middle_grad, vectors, small
    )
    inputs_grad[...] = total.astype(inputs_grad.dtype)


def last_project_backward_kernel(
    place,
    packs,
    returned,
    inputs,
    middle_grad,
    vectors,
    w_in,
    w_up,
    inputs_grad,
    short_grad,
    own,
    other,
    small,
    spread,
):
    (weight, copy), (up_weight, up_copy) = w_in, w_up
    copy.wait()
    total = window_project_backward(
        2, place[1], packs, returned, weight, inputs[...], middle_grad, vectors, small
    )
    inputs_grad[...] = total
    inputs_grad.send()
    put_rows(spread, 0, total)
    parts = [third_rows(spread, offset).astype(jnp.bfloat16) for offset in range(3)]
    up_copy.wait()
    result = jnp.zeros((LANES, D), jnp.float32)
    for offset in range(3):
        small[2 + offset : 3 + offset, :] = jnp.sum(
            parts[offset].astype(jnp.float32), axis=0, keepdims=True
        )
        result = result + nt(parts[offset], up_weight[:, offset * D : (offset + 1) * D])
    short_grad[...] = result
    joined = jnp.concatenate(parts, axis=1)
    half = 3 * D // 2
    quarter = half // 3

    def place_parts(target, values):
        for index in range(3):
            target[index * LANES : (index + 1) * LANES, :] = values[
                :, index * quarter : (index + 1) * quarter
            ]

    @pl.when(place[1] == 0)
    def _():
        place_parts(own, joined[:, :half])
        place_parts(other, joined[:, half:])

    @pl.when(place[1] != 0)
    def _():
        place_parts(own, joined[:, half:])
        place_parts(other, joined[:, :half])


def pooled_project_backward_kernel(
    info,
    place,
    packs,
    normed_grad,
    inputs,
    middle_grad,
    vectors,
    w_in,
    w_pool,
    shifted_grad,
    first_rows,
    own,
    other,
    small,
    spread,
):
    (weight, copy), (pool_weight, pool_copy) = w_in, w_pool
    copy.wait()
    total = project_backward(
        1,
        place[1],
        packs,
        (slice(0, LANES),),
        weight,
        normed_grad[...],
        inputs[...],
        middle_grad,
        vectors,
        small,
    )
    low = total.astype(jnp.bfloat16)
    small[2:3, :] = jnp.sum(low.astype(jnp.float32), axis=0, keepdims=True)
    store_halves(place[1], own, other, 0, low)
    pool_copy.wait()
    for offset in range(3):
        rows = nt(low, pool_weight[offset * D : (offset + 1) * D, :])
        put_third_rows(spread, offset, jnp.where(kept(info, offset), rows, 0.0))
    shifted_grad[...] = all_rows(spread)
    first_rows[...] = shifted_grad[:EDGE, :]


def lasting(micros):
    return pl.CostEstimate(
        flops=int(micros * 1e9), bytes_accessed=int(micros * 3e6), transcendentals=0
    )


class Part:
    def __init__(self, array, shape=None, place=None):
        self.array, self.place = array, place
        self.shape = tuple(shape or (array.shape if place is None else array.shape[1:]))

    def of(self, ref):
        if self.place is not None:
            return ref.at[self.place]
        if self.shape == self.array.shape:
            return ref
        return ref.at[tuple(slice(0, size) for size in self.shape)]


def whole(micros, kernel, scalars, arrays, weights, outs, scratch=(), mib=24, follows=()):
    flat, groups, parts = [], [], []
    for array in arrays:
        groups.append(len(array) if isinstance(array, tuple) else 0)
        for item in array if isinstance(array, tuple) else (array,):
            part = item if isinstance(item, Part) else Part(item, item.shape)
            flat.append(part.array)
            parts.append(part)
    shapes = [(part.shape, part.array.dtype) for part in parts]
    shapes += [(w.shape if layer is None else w.shape[1:], w.dtype) for w, layer in weights]
    shapes += list(outs) + list(scratch)
    scalar_count, flat_count, weight_count = len(scalars), len(flat), len(weights)
    sem_count = 64

    def run(*refs):
        copies = Copies(refs[-1])
        refs = list(refs[:-1])

        def take(count):
            taken, refs[:count] = refs[:count], []
            return taken

        taken = take(scalar_count)
        sources, weight_sources = take(flat_count), take(weight_count)
        take(len(follows))
        targets = take(len(outs))
        buffers, weight_buffers, out_buffers = take(flat_count), take(weight_count), take(len(outs))
        loads = [copies.start(p.of(s), b) for p, s, b in zip(parts, sources, buffers)]
        loaded = []
        for (_, layer), source, buffer in zip(weights, weight_sources, weight_buffers):
            source = source if layer is None else source.at[layer]
            loaded.append((buffer, copies.start(source, buffer)))
        for copy in loads:
            copy.wait()
        position = 0
        for size in groups:
            taken.append(buffers[position : position + size] if size else buffers[position])
            position += size or 1
        results = [Output(b, t, copies) for b, t in zip(out_buffers, targets)]
        kernel(*taken, *loaded, *results, *refs)
        for result in results:
            if not result.sent:
                result.send()
        copies.finish()

    return pl.pallas_call(
        run,
        in_specs=[SMEM] * scalar_count + [HBM] * (flat_count + weight_count + len(follows)),
        out_specs=[HBM] * len(outs),
        out_shape=[pltpu.HBM(shape, kind) for shape, kind in outs],
        scratch_shapes=[pltpu.VMEM(*item) for item in shapes]
        + [pltpu.SemaphoreType.DMA((sem_count,))],
        compiler_params=pltpu.CompilerParams(vmem_limit_bytes=mib * 2**20),
        cost_estimate=lasting(micros),
    )(*scalars, *[in_hbm(a) for a in flat + [w for w, _ in weights] + list(follows)])


def in_hbm(array):
    return pltpu.with_memory_space_constraint(array, pltpu.HBM)


def crossed(block, axis, bit):
    count = lax.axis_size(axis)
    return lax.ppermute(block, axis, [(index, index ^ bit) for index in range(count)])


def passed_along(block, axis, distance):
    devices = range(lax.axis_size(axis))
    route = [(i - distance, i) for i in devices if i - distance in devices]
    return lax.ppermute(block, axis, route)


def both(low, high, bit):
    return jnp.where(bit, high, low), jnp.where(bit, low, high)


def rounded_sum(*terms):
    return sum(term.astype(jnp.float32) for term in terms).astype(jnp.bfloat16)


def gather_pooled(rows):
    half = rows.shape[0] // 2
    from_x = crossed(rows, "seq", 2)
    from_y = crossed(rows, "seq", 4)
    from_core = crossed(rows, "seq", 1)
    first = crossed(from_x[:half], "seq", 4)
    second = crossed(from_y[half:], "seq", 2)
    core_x = crossed(from_x, "seq", 1)
    core_y = crossed(from_y, "seq", 1)
    opposite = jnp.concatenate([first, second], axis=0)
    core_opposite = crossed(opposite, "seq", 1)
    return jnp.concatenate(
        [rows, from_core, from_x, core_x, from_y, core_y, opposite, core_opposite], axis=0
    )


def scatter_pooled(even, odd, meanwhile):
    arrived = crossed(odd, "seq", 1)
    total = rounded_sum(even, arrived).reshape(4, LANES, D)
    made = meanwhile(total)
    left, right = total[:, :, : D // 2], total[:, :, D // 2 :]
    left_arrived = crossed(jnp.stack([left[1], left[3]]), "seq", 2)
    right_arrived = crossed(right[2:], "seq", 4)
    (left_arrived, right_arrived), _ = together((left_arrived, right_arrived), made)
    left_next = crossed(rounded_sum(left[2], left_arrived[1]), "seq", 4)
    right_next = crossed(rounded_sum(right[1], right_arrived[1]), "seq", 2)

    def added(*terms):
        return sum(term.astype(jnp.float32) for term in terms)

    total = jnp.concatenate(
        [
            added(left[0], left_arrived[0], left_next),
            added(right[0], right_arrived[0], right_next),
        ],
        axis=1,
    )
    return total, made


class Piece:
    def __init__(self, features, halves, reads, compute):
        self.height, self.halves, self.reads, self.compute = features // 4, halves, reads, compute
        self.lanes = sum(features // D * half // 2 for half in halves)


def plain_piece(x, first, features, dy, start, half):
    def compute(refs, chosen):
        return [sum(tn(a[:, chosen], b[...]) for a, b in zip(refs[x], refs[dy]))]

    return Piece(features, [half], {x: (first, features), dy: (start, half)}, compute)


def table_part(embedded, grads, chosen):
    rows = embedded.shape[0]
    lanes = slice(3 * D // 2, 2 * D)
    summed = sum(grad[:rows, lanes].astype(jnp.float32) for grad in grads)
    return tn(embedded[:, chosen], summed.astype(jnp.bfloat16))


def window_piece(normed, grads, table):
    def compute(refs, chosen):
        totals = []
        for index, (rows, grad_rows) in enumerate(
            ((slice(WIN, REACH), slice(0, QBLK)),) + ((slice(0, REACH),) * 2,) * 2
        ):
            lanes = slice(index * D // 2, (index + 1) * D // 2)
            totals.append(
                sum(
                    tn(features[rows, chosen], grad[grad_rows, lanes])
                    for features, grad in zip(refs[normed], refs[grads])
                )
            )
        return totals + [table_part(refs[table][0], refs[grads], chosen)]

    return Piece(D, [D // 2] * 4, {normed: (0, D), grads: (0, 2 * D), table: (0, D)}, compute)


def pooled_piece(normed, grads, table):
    def compute(refs, chosen):
        (features,) = refs[normed]
        own, pair = refs[grads]
        count = features.shape[0] // LANES
        lanes = slice(0, D // 2)
        query = sum(
            tn(features[index * LANES : (index + 1) * LANES, chosen], grad[:LANES, lanes])
            for index, grad in enumerate((own, pair))
        )
        totals = [query]
        for index in (1, 2):
            lanes = slice(index * D // 2, (index + 1) * D // 2)
            parts = []
            for block in range(count):
                near, far = block * LANES, (block ^ 1) * LANES
                parts.append(
                    rounded_sum(own[near : near + LANES, lanes], pair[far : far + LANES, lanes])
                )
            totals.append(tn(features[:, chosen], jnp.concatenate(parts, axis=0)))
        return totals + [table_part(refs[table][0], refs[grads], chosen)]

    return Piece(D, [D // 2] * 4, {normed: (0, D), grads: (0, 2 * D), table: (0, D)}, compute)


def upsample_piece(x, first, dy):
    def compute(refs, chosen):
        parts = []
        for index in range(3):
            rows = slice(index * LANES, (index + 1) * LANES)
            parts.append(sum(tn(a[:, chosen], b[rows, :]) for a, b in zip(refs[x], refs[dy])))
        return [jnp.concatenate(parts, axis=1)]

    return Piece(D, [3 * D // 2], {x: (first, D), dy: (0, D // 2)}, compute)


def pair_gradients(micros, place, sources, pieces, follows, natural=False):
    lanes = sum(piece.lanes for piece in pieces)
    flat, first = [], {}
    for name, arrays in sources.items():
        first[name] = len(flat)
        flat.extend(arrays)
    buffers = []
    for piece in pieces:
        for name, (_, width) in piece.reads.items():
            for array in sources[name]:
                buffers.append(pltpu.VMEM((array.shape[-2], width), array.dtype))
    count = len(flat)
    out = (2, LANES, lanes)
    shapes = [(4, LANES, 2 * lanes)] if natural else [out] * 4
    total_outs = len(shapes)

    def kernel(place, *refs):
        arrays = refs[:count]
        refs = refs[count + len(follows) :]
        targets, spaces, sems = refs[:total_outs], list(refs[total_outs : -1 - total_outs]), refs[-1]
        copies = Copies(sems)
        results = refs[-1 - total_outs : -1]
        ready = []
        for piece in pieces:
            inputs, loads = {}, []
            for name, (start, width) in piece.reads.items():
                inputs[name] = []
                for index in range(len(sources[name])):
                    source = arrays[first[name] + index]
                    space = spaces.pop(0)
                    if len(source.shape) == 3:
                        source = source.at[0]
                    if width != source.shape[1]:
                        source = source.at[:, start : start + width]
                    loads.append(copies.start(source, space))
                    inputs[name].append(space)
            ready.append((inputs, loads))
        offset = 0
        for piece, (inputs, loads) in zip(pieces, ready):
            for load in loads:
                load.wait()
            groups = piece.height // LANES
            for block in range(4):
                chip = block if natural else place[0] ^ block
                begin = chip * piece.height
                if not natural:
                    begin = pl.multiple_of(begin, LANES)
                totals = piece.compute(inputs, pl.ds(begin, piece.height))
                position = offset
                for total in totals:
                    total = total.astype(jnp.bfloat16)
                    quarter = total.shape[1] // 2
                    halves = (total[:, :quarter], total[:, quarter:])
                    for index, part in enumerate(halves):
                        if natural:
                            space, slot, lane = results[0], block, position + index * lanes
                        else:
                            which = (block % 2, block // 2)[index]
                            space, slot, lane = results[2 * index + which], block // 2, position
                            if index == 1:
                                slot = block % 2
                        if groups == 1:
                            space[slot, :, lane : lane + quarter] = part
                            continue
                        for group in range(groups):
                            start = lane + quarter * group
                            low = HD * group
                            high = piece.height // 2 + low
                            space[slot, :HD, start : start + quarter] = part[low : low + HD]
                            space[slot, HD:, start : start + quarter] = part[high : high + HD]
                    position += quarter * groups
            for begin in (offset, offset + lanes) if natural else (offset,):
                done = slice(begin, begin + piece.lanes)
                for space, target in zip(results, targets):
                    copies.send(space.at[:, :, done], target.at[:, :, done])
            offset += piece.lanes
        copies.finish()

    return pl.pallas_call(
        kernel,
        in_specs=[SMEM] + [ANY] * count + [HBM] * len(follows),
        out_specs=[HBM] * total_outs,
        out_shape=[pltpu.HBM(shape, jnp.bfloat16) for shape in shapes],
        scratch_shapes=buffers
        + [pltpu.VMEM(shape, jnp.bfloat16) for shape in shapes]
        + [pltpu.SemaphoreType.DMA((64,))],
        compiler_params=pltpu.CompilerParams(vmem_limit_bytes=32 * 2**20),
        cost_estimate=lasting(micros),
    )(place, *flat, *[in_hbm(a) for a in follows])


def first_step(keep_one, send_one, keep_two, send_two):
    return keep_one, crossed(send_one, "seq", 2), keep_two, crossed(send_two, "seq", 4)


def first_sums(*groups):
    parts = [[], [], [], []]
    for keep_one, one, keep_two, two in groups:
        for index in range(2):
            parts[index].append(rounded_sum(keep_one[index], one[index]))
            parts[2 + index].append(rounded_sum(keep_two[index], two[index]))
    return tuple(jnp.concatenate(part, axis=1) for part in parts)


def second_step(one, send_one, two, send_two):
    return one, crossed(send_one, "seq", 4), two, crossed(send_two, "seq", 2)


def second_sums(one, add_one, two, add_two):
    return rounded_sum(one, add_one), rounded_sum(two, add_two)


def depth_halves(first, second, depth):
    keep, send = both(first, second, depth)
    return keep, crossed(send, "dp", 1)


def depth_quarters(keep, arrived):
    keep = rounded_sum(keep, arrived)
    return keep, crossed(keep, "dp", 2)


def depth_back(keep, arrived):
    keep = rounded_sum(keep, arrived)
    return keep, crossed(keep, "dp", 1)


def depth_share(keep, other, depth):
    return jnp.concatenate(both(keep, other, depth), axis=1)


def core_rows(share, core):
    keep, send = both(share[:HD], share[HD:], core)
    return keep, crossed(send, "seq", 1)


def together(*groups):
    return lax.optimization_barrier(tuple(tuple(group) for group in groups))


def final_kernel(plan, place, *refs):
    groups = len(plan)
    buffers, outs = refs[: 2 * groups], refs[2 * groups :]
    for index, pieces in enumerate(plan):
        mine, other = buffers[2 * index : 2 * index + 2]
        lanes = mine.shape[1] // 2
        offset = 0
        for out_index, layer, first_column, columns, height in pieces:
            out = outs[out_index]
            quarter = columns // 4
            for group in range(height // HD):
                rows = slice(HD * group, HD * (group + 1))
                for part in range(4):
                    start = (part % 2) * lanes + offset
                    chosen = slice(start, start + quarter)
                    value = jnp.where(place[1] == part // 2, mine[:, chosen], other[:, chosen])
                    begin = first_column + part * quarter
                    where = (rows, slice(begin, begin + quarter))
                    out[where if layer is None else (layer, *where)] = value.astype(jnp.float32)
                offset += quarter


def final_outputs(place, plan, buffers, shapes):
    flat = [array for pair in buffers for array in pair]
    outs = [(shape, jnp.float32) for shape in shapes]
    return whole(3, partial(final_kernel, plan), [place], flat, [], outs, mib=32)


def summed_everywhere(flat):
    for axis in ("seq", "dp"):
        for bit in range(lax.axis_size(axis).bit_length() - 1):
            flat = flat + crossed(flat, axis, 1 << bit)
    return flat


def outer_float(first_matrix, second_matrix):
    return jnp.einsum("rc,re->ce", first_matrix, second_matrix, preferred_element_type=jnp.float32)


BF, FL = jnp.bfloat16, jnp.float32


def window_project(layer, inputs, vectors, embedded, w_in, first):
    one = (inputs.shape, BF)
    outs = [one, one, one, one, ((QBLK, D), BF)] + [one, ((QBLK, D), BF)] * first
    return whole(
        4,
        partial(window_project_kernel, layer),
        [],
        [inputs, vectors, embedded],
        [(w_in, layer)],
        outs,
    )


def window_attention(layer, raw, info, heads, border, vectors, w_in, table):
    rows = heads[0].shape[0]
    operands = [(a, by_pair(a.shape)) for a in heads]
    operands += [(a, entire(a.shape)) for a in (border, vectors[0], vectors[1])]
    operands += [(w_in, of_layer(w_in.shape, layer, first)) for first in (4, 8)]
    operands.append((table, by_pair(table.shape)))
    weights = (HEADS, PARTS, LANES, SEEN)
    pair_border = (2, WIN, D)
    outs = [
        ((rows, D), BF, by_pair((rows, D))),
        (border.shape, BF, entire(border.shape)),
        (pair_border, BF, by_pair(pair_border)),
        (weights, BF, weights_block(weights)),
    ]
    scratch = [
        pltpu.VMEM((PARTS, LANES, SEEN), FL),
        pltpu.VMEM(border.shape, BF),
        pltpu.VMEM((2 * rows, SEEN), FL),
    ]
    kernel = partial(window_forward_kernel, layer if raw else None)
    return attention_call(11, kernel, [info], operands, outs, scratch, 20)


def window_attention_back(
    layer, place, heads, border, w_in, table, weights, grad, follows=()
):
    rows = heads[0].shape[0]
    operands = [(a, by_pair(a.shape)) for a in (*heads, border)]
    operands += [(w_in, of_layer(w_in.shape, layer, first)) for first in (4, 8)]
    operands += [(table, by_pair(table.shape)), (weights, weights_block(weights.shape))]
    operands.append((grad, by_pair(grad.shape)))
    outs = [
        ((2, D), FL, by_pair((2, D))),
        ((WIN, D), BF, entire((WIN, D))),
        ((REACH, 2 * D), BF, None),
        ((REACH, 2 * D), BF, None),
    ]
    scratch = [pltpu.VMEM((REACH, PAIR), FL)] * 2
    scratch += [pltpu.VMEM((WIN, D), FL), pltpu.VMEM((2 * rows, SEEN), BF)]
    scratch += [pltpu.VMEM((2, size, PAIR), BF) for size in (rows, REACH, REACH, table.shape[0])]
    scratch.append(pltpu.SemaphoreType.DMA((2, 4)))
    return attention_call(
        13, window_backward_kernel, [place], operands, outs, scratch, 20, follows
    )


def pooled_attention(info, order, content, position, normed, w_in, table):
    rows, total = content.shape[0], normed.shape[0]
    operands = [(a, by_pair(a.shape)) for a in (content, position)]
    operands.append((normed, entire(normed.shape)))
    operands += [(w_in, of_layer(w_in.shape, 1, first)) for first in (4, 8)]
    operands.append((table, by_pair(table.shape)))
    weights = (HEADS, LANES, total)
    outs = [
        ((rows, D), BF, by_pair((rows, D))),
        ((total, D), BF, by_pair((total, D))),
        ((total, D), BF, by_pair((total, D))),
        (weights, BF, weights_block(weights)),
    ]
    scratch = [
        pltpu.VMEM((total // LANES, LANES, LANES), FL),
        pltpu.VMEM((2 * rows, table.shape[0]), FL),
    ]
    mib = 10 + total // LANES * 3 // 2
    return attention_call(13, pooled_forward_kernel, [info, order], operands, outs, scratch, mib)


def pooled_attention_back(order, place, heads, w_in, table, weights, grad, follows):
    rows, total = heads[0].shape[0], heads[2].shape[0]
    operands = [(a, by_pair(a.shape)) for a in heads]
    operands += [(w_in, of_layer(w_in.shape, 1, first)) for first in (4, 8)]
    operands += [(table, by_pair(table.shape)), (weights, weights_block(weights.shape))]
    operands.append((grad, by_pair(grad.shape)))
    half = ((total // LANES + 1) // 2 * LANES, D)
    outs = [
        ((2, D), FL, by_pair((2, D))),
        (half, BF, entire(half)),
        (half, BF, entire(half)),
        ((table.shape[0], 2 * D), BF, None),
        ((table.shape[0], 2 * D), BF, None),
    ]
    scratch = [pltpu.VMEM((table.shape[0], PAIR), FL), pltpu.VMEM((total, D), FL)]
    scratch += [pltpu.VMEM((2, size, PAIR), BF) for size in (rows, total, total, table.shape[0])]
    scratch.append(pltpu.SemaphoreType.DMA((2, 4)))
    mib = 10 + total // LANES * 3 // 2
    return attention_call(
        13, pooled_backward_kernel, [order, place], operands, outs, scratch, mib, follows
    )


def window_feed(layer, mixed, inputs, vectors, weights, kind, follows=()):
    rows = mixed.shape[0]
    outs = [
        ((rows, D), FL),
        ((rows, 4 * D), BF),
        ((rows, 6 * D), BF),
        ((rows, D), kind),
        ((1, D), FL),
        ((EDGE, D), BF),
    ]
    return whole(
        7,
        partial(window_feed_kernel, layer),
        [],
        [mixed, inputs, vectors],
        [(w, layer) for w in weights],
        outs,
        follows=follows,
    )


def feed_back(kernel, layer, place, arrays, rows, weights, extra=(), follows=()):
    outs = [((rows, D), FL), ((rows, D), BF), ((rows, 3 * D), BF), ((rows, 3 * D), BF)]
    outs.append(((8, D), FL))
    return whole(
        8, kernel, [place], arrays, [(w, layer) for w in weights], outs, extra, follows=follows
    )


def first_lanes(arrays, rows, lanes):
    return tuple(Part(array, (rows, lanes)) for array in arrays)


def per_device(
    tokens,
    doc_lengths,
    cotangent,
    norm_gain,
    norm_shift,
    relative_bias,
    attention_in,
    attention_out,
    expand_weight,
    expand_bias,
    contract_weight,
    contract_bias,
    pool_weight,
    pool_bias,
    upsample_weight,
    upsample_bias,
):
    def by_layer(weight):
        return jnp.transpose(weight, (1, 0, 2))

    w_in, w_out = by_layer(attention_in), by_layer(attention_out)
    w_expand, w_contract = by_layer(expand_weight), by_layer(contract_weight)
    ff_weights = [w_out, w_expand, w_contract]
    vectors = (norm_gain, norm_shift, relative_bias, contract_bias, expand_bias)
    vectors += (pool_bias[None], upsample_bias[None])

    inputs = tokens[0]
    rows = inputs.shape[0]
    pooled_rows = rows // 3
    device = lax.axis_index("seq").astype(jnp.int32)
    seq_count = lax.axis_size("seq")
    usual = seq_count == 8 and lax.axis_size("dp") == 4
    core_index = device % 2
    core = core_index == 1
    depth = lax.axis_index("dp") % 2 == 1
    place = jnp.stack([device // 2, core_index])
    cores = [[core + chip for chip in range(0, seq_count, 2)] for core in range(2)]
    document = jnp.arange(DOCS)
    ends = jnp.sum(jnp.where(document[None] <= document[:, None], doc_lengths, 0), axis=1)
    info = jnp.concatenate([(device * rows)[None], ends]).astype(jnp.int32)
    pooled_info = jnp.concatenate([(device * pooled_rows)[None], ends]).astype(jnp.int32)
    order = jnp.arange(seq_count, dtype=jnp.int32)
    if usual:
        order = order ^ device
    order = jnp.concatenate([order, device[None]])
    frequency = jnp.power(10000.0, -2.0 * jnp.arange(D // 2, dtype=FL) / D)[None]

    def swapped(array):
        return (array, crossed(array, "seq", 1)) if usual else array

    def swapped_halves(own, other):
        return (own, crossed(other, "seq", 1)) if usual else (own, other)

    border0 = passed_along(inputs[rows - WIN :], "seq", 1)
    *heads0, table0, normed0, near_table = window_project(
        0, inputs, vectors, frequency, w_in, True
    )
    mixed0, edge_normed0, border0, weights0 = window_attention(
        0, True, info, heads0, border0, vectors, w_in, table0
    )
    middle0, slope0, pack0, full0, squares0, edge = window_feed(
        0, mixed0, inputs, vectors, ff_weights, FL
    )
    edge = passed_along(edge, "seq", 1)
    x0, n0 = swapped(pack0), swapped(jnp.concatenate([edge_normed0, normed0], axis=0))

    one = ((pooled_rows, D), BF)
    spread = ((D // LANES, rows, LANES), FL)
    normed1, inputs1, grouped = whole(
        4,
        pool_kernel,
        [info],
        [full0, edge, vectors],
        [(pool_weight, None)],
        [one, ((pooled_rows, D), FL), ((pooled_rows, 3 * D), BF)],
        [((D // LANES, rows + 8, LANES), FL)],
    )
    far_shape = (((seq_count + 1) * pooled_rows, D), BF)
    if usual:
        normed1_all = gather_pooled(normed1)
    else:
        normed1_all = lax.all_gather(normed1, "seq", axis=0, tiled=True)
    content1, position1, table1, far_table = whole(
        4,
        pooled_project_kernel,
        [],
        [normed1, vectors, frequency],
        [(w_in, 1)],
        [one, one, far_shape, far_shape],
    )
    mixed1, keys1, values1, weights1 = pooled_attention(
        pooled_info, order, content1, position1, normed1_all, w_in, table1
    )
    middle1, slope1, pack1, normed2, inputs2, squares1 = whole(
        7,
        pooled_feed_kernel,
        [],
        [mixed1, inputs1, grouped, full0, vectors],
        [(w, 1) for w in ff_weights] + [(upsample_weight, None)],
        [
            ((pooled_rows, D), FL),
            ((pooled_rows, 4 * D), BF),
            ((pooled_rows, 10 * D), BF),
            ((rows, D), BF),
            ((rows, D), FL),
            ((1, D), FL),
        ],
        [spread],
        follows=(x0[1], n0[1]) if usual else (),
    )

    border2 = passed_along(normed2[rows - WIN :], "seq", 1)
    *heads2, table2 = window_project(2, normed2, vectors, near_table, w_in, False)
    mixed2, edge_normed2, border2, weights2 = window_attention(
        2, False, info, heads2, border2, vectors, w_in, table2
    )
    x1, n2 = swapped(pack1), swapped(jnp.concatenate([edge_normed2, normed2], axis=0))
    middle2, slope2, pack2, output, squares2, _ = window_feed(
        2, mixed2, inputs2, vectors, ff_weights, BF, x1[1:] if usual else ()
    )

    share = D // seq_count
    shapes = [
        (3, share, 4 * D),
        (3, share, D),
        (3, share, 4 * D),
        (3, 4 * share, D),
        (3 * share, D),
        (share, 3 * D),
    ]

    every = {}

    def feed_pieces(x, dy, layer):
        pieces = [
            plain_piece(x, D, D, dy, 0, 2 * D),
            plain_piece(x, 2 * D, 4 * D, dy, 2 * D, D // 2),
            plain_piece(x, 0, D, dy, 2 * D + D // 2, D // 2),
        ]
        targets = [
            (2, layer, 0, 4 * D, share),
            (3, layer, 0, D, 4 * share),
            (1, layer, 0, D, share),
        ]
        return pieces, targets

    def project_targets(layer):
        return [(0, layer, index * D, D, share) for index in range(4)]

    feed2 = feed_pieces("x2", "a2", 2)
    project2 = [window_piece("n2", "b2", "near")], project_targets(2)
    up = [upsample_piece("x1", 6 * D, "u2")], [(5, None, 0, 3 * D, share)]
    feed1 = feed_pieces("x1", "a1", 1)
    project1 = [pooled_piece("n1", "b1", "far")], project_targets(1)
    pool = [plain_piece("x1", 7 * D, 3 * D, "p1", 0, D // 2)], [(4, None, 0, D, 3 * share)]
    feed0 = feed_pieces("x0", "a0", 0)
    project0 = [window_piece("n0", "b0", "near")], project_targets(0)

    def gradients(names, follows, *parts, natural=False):
        if not usual:
            return ()
        pieces = sum((part[0] for part in parts), [])
        sources = {name: every[name] for name in names}
        return tuple(pair_gradients(7, place, sources, pieces, follows, natural))

    def step(function, values, *options):
        return tuple(function(*values, *options)) if usual else ()

    back_weights = [w_contract, w_expand, w_out]
    x2 = swapped(pack2)
    every["near"], every["far"] = (near_table,), (far_table,)
    every["x0"], every["x1"], every["x2"] = x0, x1, x2
    every["n0"], every["n1"], every["n2"] = n0, (normed1_all,), n2

    middle_grad2, mixed_grad2, own_a2, other_a2, small_a2 = feed_back(
        partial(feed_backward_kernel, 2),
        2,
        place,
        [cotangent[0], slope2, middle2, vectors],
        rows,
        back_weights,
    )
    every["a2"] = swapped_halves(own_a2, other_a2)
    bias2, leaving2, *grads2 = window_attention_back(
        2, place, heads2, border2, w_in, table2, weights2, mixed_grad2, (x2[1], n2[1]) if usual else ()
    )
    returned2 = passed_along(leaving2, "seq", -1)
    every["b2"] = swapped_halves(*grads2)
    sent2 = gradients(
        ("a2", "x2", "b2", "n2", "near"), (bias2,), feed2, project2, natural=True
    )
    joined, short_grad, own_u2, other_u2, small_b2 = whole(
        6,
        last_project_backward_kernel,
        [place],
        [first_lanes(grads2, REACH, 3 * D // 2), returned2, inputs2, middle_grad2, vectors],
        [(w_in, 2), (upsample_weight, None)],
        [
            ((rows, D), FL),
            ((pooled_rows, D), FL),
            ((rows, D // 2), BF),
            ((rows, D // 2), BF),
            ((8, D), FL),
        ],
        [spread],
        follows=sent2[:1],
    )
    every["u2"] = swapped_halves(own_u2, other_u2)

    middle_grad1, mixed_grad1, own_a1, other_a1, small_a1 = feed_back(
        partial(feed_backward_kernel, 1),
        1,
        place,
        [short_grad, slope1, middle1, vectors],
        pooled_rows,
        back_weights,
    )
    every["a1"] = swapped_halves(own_a1, other_a1)
    if usual:
        share2 = sent2[0].reshape(4 * LANES, -1)
        share2 = lax.psum_scatter(
            share2, "seq", scatter_dimension=0, tiled=True, axis_index_groups=cores
        )
        follows0 = (share2,)
        share2 = lax.psum(share2, "dp")
    else:
        follows0 = ()
    heads1 = (content1, position1, keys1, values1)
    bias1, even, odd, *grads1 = pooled_attention_back(
        order, place, heads1, w_in, table1, weights1, mixed_grad1, ()
    )
    every["b1"] = swapped_halves(*grads1)

    def group1_gradients(total):
        return gradients(("a1", "x1", "u2"), (total,), up, feed1)

    if usual:
        normed_grad1, group1 = scatter_pooled(even, odd, group1_gradients)
    else:
        group1 = ()
        split = (seq_count // 2, 1, LANES, D)
        summed = jnp.concatenate([even.reshape(split), odd.reshape(split)], axis=1)
        summed = summed.reshape(seq_count * LANES, D)
        normed_grad1 = lax.psum_scatter(summed, "seq", scatter_dimension=0, tiled=True).astype(FL)
    (normed_grad1,), group1 = together((normed_grad1,), group1)
    group1 = step(first_step, group1)
    shifted_grad, first_rows, own_p1, other_p1, small_b1 = whole(
        5,
        pooled_project_backward_kernel,
        [info, place],
        [first_lanes(grads1, LANES, D // 2), normed_grad1, inputs1, middle_grad1, vectors],
        [(w_in, 1), (pool_weight, None)],
        [
            ((rows, D), FL),
            ((EDGE, D), FL),
            ((pooled_rows, D // 2), BF),
            ((pooled_rows, D // 2), BF),
            ((8, D), FL),
        ],
        [spread],
        follows=follows0,
    )
    every["p1"] = swapped_halves(own_p1, other_p1)
    came_back = passed_along(first_rows, "seq", -1)
    group1b = gradients(("p1", "x1", "b1", "n1", "far"), (small_b1,), pool, project1)
    (came_back,), group1b = together((came_back,), group1b)
    group1b = step(first_step, group1b)
    middle_grad0, mixed_grad0, own_a0, other_a0, small_a0 = feed_back(
        first_feed_backward_kernel,
        0,
        place,
        [joined, shifted_grad, came_back, slope0, middle0, vectors],
        rows,
        back_weights,
        [((rows + 8, D), FL)],
    )
    every["a0"] = swapped_halves(own_a0, other_a0)
    (mixed_grad0,), group1, group1b = together((mixed_grad0,), group1, group1b)
    group1 = step(first_sums, (group1, group1b))
    (mixed_grad0,), group1 = together((mixed_grad0,), group1)
    group1 = step(second_step, group1)
    bias0, leaving0, *grads0 = window_attention_back(
        0, place, heads0, border0, w_in, table0, weights0, mixed_grad0
    )
    every["b0"] = swapped_halves(*grads0)
    returned0 = passed_along(leaving0, "seq", -1)

    follows = ()
    if usual:
        group0 = gradients(("a0", "x0"), (bias0,), feed0)
        last = gradients(("b0", "n0", "near"), group0[:1], project0)
        last_sent = last[0]
        group0 = step(first_step, group0)
        last = step(first_step, last)
        group1 = step(second_sums, group1)
        group1 = step(depth_halves, group1, depth)
        group1 = step(depth_quarters, group1)
        follows = (last_sent, share2, group1[0])
    tokens_grad, small_b0 = whole(
        5,
        first_project_backward_kernel,
        [place],
        [first_lanes(grads0, REACH, 3 * D // 2), returned0, inputs, middle_grad0, vectors],
        [(w_in, 0)],
        [((rows, D), BF), ((8, D), FL)],
        follows=follows,
    )
    small = jnp.concatenate(
        [
            small_b0[:2],
            small_b1[:3],
            small_b2[:5],
            small_a0[:7],
            small_a1[:7],
            small_a2[:7],
            bias0,
            bias1,
            bias2,
            squares0,
            squares1,
            squares2,
        ],
        axis=0,
    )
    if usual:
        clock = (small_b0,)
        small = small + crossed(small, "seq", 1)
        clock, (small,), group0 = together(clock, (small,), group0)
        group0 = step(first_sums, (group0,))
        group0 = step(second_step, group0)
        small = small + crossed(small, "seq", 2)
        clock, (small,), last = together(clock, (small,), last)
        last = step(first_sums, (last,))
        last = step(second_step, last)
        small = small + crossed(small, "seq", 4)
        clock, (small,), group0, group1 = together(clock, (small,), group0, group1)
        group0 = step(second_sums, group0)
        group0 = step(depth_halves, group0, depth)
        group1 = step(depth_back, group1)
        clock, last = together(clock, last)
        last = step(second_sums, last)
        last = step(depth_halves, last, depth)
        clock, group0 = together(clock, group0)
        group0 = step(depth_quarters, group0)
        clock, last, group1 = together(clock, last, group1)
        last = step(depth_quarters, last)
        small = small + crossed(small, "dp", 1)
        clock, (small,), group0 = together(clock, (small,), group0)
        group0 = step(depth_back, group0)
        clock, last = together(clock, last)
        last = step(depth_back, last)
        small = small + crossed(small, "dp", 2)
        plan = [feed2[1] + project2[1], up[1] + feed1[1] + pool[1] + project1[1]]
        plan += [feed0[1], project0[1]]
        shares = [share2] + [depth_share(*group, depth) for group in (group1, group0, last)]
        buffers = [core_rows(share, core) for share in shares]
        sums = final_outputs(place, plan, buffers, shapes)
    else:
        small = summed_everywhere(small)
        sums = plain_sums(
            shapes,
            core,
            (pack0, pack1, pack2),
            (every["n0"], normed1, every["n2"]),
            (every["n0"], normed1_all, every["n2"]),
            (every["a0"], every["a1"], every["a2"]),
            (grads0, grads1, grads2),
            every["p1"],
            every["u2"],
            (near_table, far_table),
        )
    in_grad, out_grad, expand_grad, contract_grad = [by_layer(total) for total in sums[:4]]

    gain, shift, expand_sum, contract_sum = [], [], [], []
    for layer, b in enumerate((0, 2, 5)):
        a = 10 + 7 * layer
        gain.append(jnp.stack([small[b], small[a + 1]]))
        shift.append(jnp.stack([small[b + 1], small[a + 2]]))
        contract_sum.append(small[a])
        expand_sum.append(small[a + 3 : a + 7].reshape(4 * D))
    bias_sum = small[31:37].reshape(3, 2, D)
    whole_rows = lax.axis_size("dp") * seq_count * rows * D
    counts = jnp.array([whole_rows, whole_rows // 3, whole_rows], FL)
    rms = jnp.sqrt(jnp.sum(small[37:40], axis=1) / counts)
    return (
        output[None],
        tokens_grad[None],
        jnp.stack(gain),
        jnp.stack(shift),
        bias_sum,
        in_grad,
        out_grad,
        expand_grad,
        jnp.stack(expand_sum),
        contract_grad,
        jnp.stack(contract_sum),
        sums[4],
        small[4],
        sums[5],
        small[7:10].reshape(3 * D),
        rms,
    )


def plain_sums(
    shapes, core, packs, normed, normed_all, a_pairs, grads, pool_pair, up_pair, tables
):
    def full(pair, start, half):
        own, other = (array[:, start : start + half] for array in pair)
        return jnp.concatenate(both(own, other, core), axis=1)

    def summed(features, grad):
        total = outer_float(features, grad).astype(BF)
        total = lax.psum_scatter(total, "seq", scatter_dimension=0, tiled=True)
        return lax.psum(total, "dp").astype(FL)

    into, out, expand, contract = [], [], [], []
    for layer in range(3):
        x, a, b = packs[layer], a_pairs[layer], grads[layer]
        table, near, every = tables[layer % 2], normed[layer], normed_all[layer]
        own = x.shape[0]
        near = near[near.shape[0] - own :]
        columns = [
            summed(near, full(b, 0, D // 2)[:own]),
            summed(every, full(b, D // 2, D // 2)[: every.shape[0]]),
            summed(every, full(b, D, D // 2)[: every.shape[0]]),
            summed(table, full(b, 3 * D // 2, D // 2)[: table.shape[0]]),
        ]
        into.append(jnp.concatenate(columns, axis=1))
        out.append(summed(x[:, :D], full(a, 2 * D + D // 2, D // 2)))
        expand.append(summed(x[:, D : 2 * D], full(a, 0, 2 * D)))
        contract.append(summed(x[:, 2 * D : 6 * D], full(a, 2 * D, D // 2)))
    pool = summed(packs[1][:, 7 * D :], full(pool_pair, 0, D // 2))
    sides = []
    for array in up_pair:
        parts = [array[index * LANES : (index + 1) * LANES] for index in range(3)]
        sides.append(jnp.concatenate(parts, axis=1))
    up = summed(packs[1][:, 6 * D : 7 * D], jnp.concatenate(both(*sides, core), axis=1))
    stacks = [jnp.stack(parts) for parts in (into, out, expand, contract)]
    return stacks + [pool, up]


def solution(mesh):
    rows = P("dp", "seq", None)
    in_specs = (rows, P("dp", None), rows) + (P(),) * 13
    split = P("seq", None, None)
    flat = P("seq", None)
    out_specs = (rows, rows, P(), P(), P(), split, split, split, P(), split, P())
    out_specs += (flat, P(), flat, P(), P())
    return jax.shard_map(
        per_device, mesh=mesh, in_specs=in_specs, out_specs=out_specs, check_vma=False
    )
```

```python
import math
from functools import partial

import jax
import jax.numpy as jnp
from jax import lax
from jax.experimental import pallas as pl
from jax.experimental.pallas import tpu as pltpu
from jax.sharding import PartitionSpec as P

D = 512
HEADS = 8
HD = 64
WIN = 256
QBLK = 384
DOCS = 8
EDGE = 16
epsilon = 1e-05
GAIN, SHIFT, BIAS, CONTRACT, EXPAND, POOL, UP = 0, 6, 12, 18, 21, 33, 34

VMEM = pl.BlockSpec(memory_space=pltpu.VMEM)
SMEM = pl.BlockSpec(memory_space=pltpu.SMEM)
HBM = pl.BlockSpec(memory_space=pltpu.HBM)
ANY = pl.BlockSpec(memory_space=pl.ANY)


LANES = 128
PAIR = 2 * HD
MASKED = -1e30
PARTS = QBLK // LANES
SEEN = LANES + WIN
REACH = QBLK + WIN


def nt(first, second):
    return lax.dot_general(
        first, second, (((1,), (1,)), ((), ())), preferred_element_type=jnp.float32
    )


def nn(first, second):
    return lax.dot_general(
        first, second, (((1,), (0,)), ((), ())), preferred_element_type=jnp.float32
    )


def tn(first, second):
    return lax.dot_general(
        first, second, (((0,), (0,)), ((), ())), preferred_element_type=jnp.float32
    )


def document(places, info):
    total = jnp.zeros(places.shape, jnp.int32)
    for index in range(DOCS):
        total = total + (places >= info[1 + index]).astype(jnp.int32)
    return total


def lanes_and_rows():
    lane = lax.broadcasted_iota(jnp.int32, (LANES, LANES), 1)
    row = lax.broadcasted_iota(jnp.int32, (LANES, LANES), 0)
    return lane, row


def turned(values, index):
    return [
        jnp.take_along_axis(values[:, m * LANES : (m + 1) * LANES], index, axis=1)
        for m in range(values.shape[1] // LANES)
    ]


def skew_window(table):
    lane, row = lanes_and_rows()
    blocks = turned(table, (lane - row + LANES) % LANES)
    out = [blocks[0]] + [
        jnp.where(lane >= row, here, before) for before, here in zip(blocks, blocks[1:])
    ]
    return jnp.concatenate(out, axis=1)


def unskew_window(scores):
    lane, row = lanes_and_rows()
    blocks = turned(scores, (lane + row) % LANES)
    blocks.append(jnp.zeros_like(blocks[0]))
    out = [
        jnp.where(lane + row < LANES, here, after) for here, after in zip(blocks, blocks[1:])
    ]
    return jnp.concatenate(out, axis=1)


def unskew_pooled(scores):
    lane, row = lanes_and_rows()
    (block,) = turned(scores, (lane + row + 1) % LANES)
    zero = jnp.zeros_like(block)
    first = lane + row >= LANES - 1
    return jnp.concatenate([jnp.where(first, block, zero), jnp.where(first, zero, block)], axis=1)


def stacked(rows):
    head = lax.broadcasted_iota(jnp.int32, rows.shape, 1) // HD
    zero = jnp.zeros_like(rows)
    return jnp.concatenate([jnp.where(head == 0, rows, zero), jnp.where(head == 1, rows, zero)], axis=0)


def unstacked(rows):
    count = rows.shape[0] // 2
    head = lax.broadcasted_iota(jnp.int32, (count, PAIR), 1) // HD
    return jnp.where(head == 0, rows[:count], rows[count:])


def softmax_rows(scores):
    highest = jnp.max(scores, axis=1, keepdims=True)
    powers = jnp.exp(scores - highest)
    return powers * (1.0 / jnp.sum(powers, axis=1, keepdims=True))


def window_mask(info, part):
    place = info[0] + part * LANES
    row = lax.broadcasted_iota(jnp.int32, (LANES, SEEN), 0)
    column = lax.broadcasted_iota(jnp.int32, (LANES, SEEN), 1)
    behind = row + WIN - column
    query = place + lax.broadcasted_iota(jnp.int32, (LANES, 1), 0)
    key = place - WIN + lax.broadcasted_iota(jnp.int32, (1, SEEN), 1)
    same = document(query, info) == document(key, info)
    return (behind >= 0) & (behind <= WIN) & same & (key >= 0)


def pooled_mask(info, start):
    query = info[0] + lax.broadcasted_iota(jnp.int32, (LANES, 1), 0)
    key = start + lax.broadcasted_iota(jnp.int32, (1, LANES), 1)
    return (key <= query) & (document(3 * query, info) == document(3 * key, info))


def column_sums(first, second):
    return jnp.concatenate(
        [jnp.sum(first, axis=0, keepdims=True), jnp.sum(second, axis=0, keepdims=True)], axis=0
    )


def backward_scores(weights, grad_weights):
    delta = jnp.sum(weights * grad_weights, axis=1, keepdims=True)
    return weights * (grad_weights - delta)


def window_forward_kernel(
    raw,
    info,
    content,
    position,
    keys,
    values,
    border,
    gain,
    shift,
    key_weight,
    value_weight,
    table,
    mixed_ref,
    normed_ref,
    border_ref,
    weights_ref,
    bias,
    normed,
    places,
):
    pair = pl.program_id(0)

    @pl.when(pair == 0)
    def _():
        if raw is None:
            normed[...] = border[...]
        else:
            hat, _ = normalised(border[...].astype(jnp.float32))
            scale = gain[raw].astype(jnp.float32)[0:1, :]
            normed[...] = (hat * scale + shift[raw].astype(jnp.float32)[0:1, :]).astype(jnp.bfloat16)
        normed_ref[...] = normed[...]
        for part in range(PARTS):
            bias[part] = jnp.where(window_mask(info, part), 0.0, MASKED)

    border_keys = nn(normed[...], key_weight[...]).astype(jnp.bfloat16)
    border_values = nn(normed[...], value_weight[...]).astype(jnp.bfloat16)
    border_ref[0] = border_keys
    border_ref[1] = border_values
    all_keys = jnp.concatenate([border_keys, keys[...]], axis=0)
    all_values = jnp.concatenate([border_values, values[...]], axis=0)
    scale = jnp.asarray(HD**-0.5, jnp.bfloat16)
    order = [
        stacked(position[part * LANES : (part + 1) * LANES, :] * scale) for part in range(PARTS)
    ]
    places[...] = nt(jnp.concatenate(order, axis=0), table[...])
    for part in range(PARTS):
        rows = slice(part * LANES, (part + 1) * LANES)
        seen = slice(part * LANES, part * LANES + SEEN)
        scores = nt(stacked(content[rows, :] * scale), all_keys[seen])
        weights = []
        for index in range(2):
            start = (2 * part + index) * LANES
            score = scores[index * LANES : (index + 1) * LANES]
            score = score + skew_window(places[start : start + LANES, :]) + bias[part]
            weights.append(softmax_rows(score).astype(jnp.bfloat16))
            weights_ref[index, part] = weights[index]
        mixed = nn(jnp.concatenate(weights, axis=0), all_values[seen])
        mixed_ref[rows, :] = unstacked(mixed).astype(jnp.bfloat16)


def window_backward_kernel(
    place,
    content,
    position,
    keys,
    values,
    border,
    key_weight,
    value_weight,
    table,
    weights,
    grad,
    bias_ref,
    returned_ref,
    own_pack,
    other_pack,
    dk_sum,
    dv_sum,
    returned,
    places,
    dq_out,
    dk_out,
    dv_out,
    dt_out,
    sems,
):
    pair = pl.program_id(0)
    all_keys = jnp.concatenate([border[0], keys[...]], axis=0)
    all_values = jnp.concatenate([border[1], values[...]], axis=0)
    scale = HD**-0.5
    low_scale = jnp.asarray(scale, jnp.bfloat16)
    dk_sum[...] = jnp.zeros_like(dk_sum)
    dv_sum[...] = jnp.zeros_like(dv_sum)
    contents = []
    for part in range(PARTS):
        rows = slice(part * LANES, (part + 1) * LANES)
        seen = slice(part * LANES, part * LANES + SEEN)
        grads = stacked(grad[rows, :])
        grad_weights = nt(grads, all_values[seen])
        scores, lows = [], []
        for index in range(2):
            low = weights[index, part]
            score = backward_scores(
                low.astype(jnp.float32), grad_weights[index * LANES : (index + 1) * LANES]
            ).astype(jnp.bfloat16)
            start = (2 * part + index) * LANES
            places[start : start + LANES, :] = unskew_window(score.astype(jnp.float32)).astype(
                jnp.bfloat16
            )
            scores.append(score)
            lows.append(low)
        scores = jnp.concatenate(scores, axis=0)
        contents.append(unstacked(nn(scores, all_keys[seen])) * scale)
        dk_sum[seen, :] += tn(scores, stacked(content[rows, :] * low_scale))
        dv_sum[seen, :] += tn(jnp.concatenate(lows, axis=0), grads)
    order = [
        stacked(position[part * LANES : (part + 1) * LANES, :] * low_scale)
        for part in range(PARTS)
    ]
    to_position = nn(places[...], table[...]) * scale
    positions = [
        unstacked(to_position[2 * part * LANES : 2 * (part + 1) * LANES]) for part in range(PARTS)
    ]
    grad_content = jnp.concatenate(contents, axis=0)
    grad_position = jnp.concatenate(positions, axis=0)
    bias_ref[...] = column_sums(grad_content, grad_position)
    slot = pair % 2
    grad_keys = dk_sum[...].astype(jnp.bfloat16)
    grad_values = dv_sum[...].astype(jnp.bfloat16)
    dq_out[slot] = (grad_content + grad_position).astype(jnp.bfloat16)
    dk_out[slot] = grad_keys
    dv_out[slot] = grad_values
    dt_out[slot] = tn(places[...], jnp.concatenate(order, axis=0)).astype(jnp.bfloat16)
    outs = (dq_out, dk_out, dv_out, dt_out)
    send_pack(place, pair, (own_pack, other_pack), outs, sems)
    back = nt(grad_keys[:WIN], key_weight[...]) + nt(grad_values[:WIN], value_weight[...])

    @pl.when(pair == 0)
    def _():
        returned[...] = back

    @pl.when(pair != 0)
    def _():
        returned[...] += back

    @pl.when(pair == HEADS // 2 - 1)
    def _():
        returned_ref[...] = returned[...].astype(jnp.bfloat16)


def pack_copies(place, pair, packs, outs, sems, act):
    for slot, pack in enumerate(packs):

        @pl.when((pair // 2) ^ place[1] == slot)
        def _(pack=pack):
            for index, out in enumerate(outs):
                lane = pl.multiple_of(index * D // 2 + pair % 2 * PAIR, PAIR)
                source = out.at[pair % 2]
                target = pack.at[pl.ds(0, source.shape[0]), pl.ds(lane, PAIR)]
                act(pltpu.make_async_copy(source, target, sems.at[pair % 2, index]))


def send_pack(place, pair, packs, outs, sems):
    def start(copy):
        copy.start()

    def wait(copy):
        copy.wait()

    pack_copies(place, pair, packs, outs, sems, start)

    @pl.when(pair > 0)
    def _():
        pack_copies(place, pair - 1, packs, outs, sems, wait)

    @pl.when(pair == HEADS // 2 - 1)
    def _():
        pack_copies(place, pair, packs, outs, sems, wait)


def table_rows(order, block, count):
    start = jnp.minimum(order[block] + count - 1 - order[count], count - 1)
    return pl.ds(pl.multiple_of(LANES * start, LANES), 2 * LANES)


def table_lanes(order, block, count, offset):
    start = jnp.minimum(order[block] + count - 1 - order[count], count - 1) + offset
    return pl.ds(pl.multiple_of(LANES * start, LANES), LANES)


def pooled_forward_kernel(
    info,
    order,
    content,
    position,
    normed,
    key_weight,
    value_weight,
    table,
    mixed_ref,
    keys_ref,
    values_ref,
    weights_ref,
    bias,
    places,
):
    count = normed.shape[0] // LANES

    @pl.when(pl.program_id(0) == 0)
    def _():
        for block in range(count):
            visible = pooled_mask(info, LANES * order[block])
            bias[block] = jnp.where(visible, 0.0, MASKED)

    scale = jnp.asarray(HD**-0.5, jnp.bfloat16)
    keys_ref[...] = nn(normed[...], key_weight[...]).astype(jnp.bfloat16)
    values_ref[...] = nn(normed[...], value_weight[...]).astype(jnp.bfloat16)
    scores = nt(stacked(content[...] * scale), keys_ref[...])
    lane, row = lanes_and_rows()
    place = nt(stacked(position[...] * scale), table[...])
    turn = (lane + LANES - 1 - row) % LANES
    rows = [[], []]
    for index in range(2):
        half = slice(index * LANES, (index + 1) * LANES)
        places[half, :] = jnp.concatenate(turned(place[half], turn), axis=1)
        for block in range(count):
            here = places[half, table_lanes(order, block, count, 0)]
            there = places[half, table_lanes(order, block, count, 1)]
            score = scores[half, block * LANES : (block + 1) * LANES]
            rows[index].append(score + jnp.where(lane <= row, here, there) + bias[block])
    weights = []
    for index in range(2):
        weight = softmax_rows(jnp.concatenate(rows[index], axis=1)).astype(jnp.bfloat16)
        weights_ref[index] = weight
        weights.append(weight)
    mixed = nn(jnp.concatenate(weights, axis=0), values_ref[...])
    mixed_ref[...] = unstacked(mixed).astype(jnp.bfloat16)


def pooled_backward_kernel(
    order,
    place,
    content,
    position,
    keys,
    values,
    key_weight,
    value_weight,
    table,
    weights,
    grad,
    bias_ref,
    even_ref,
    odd_ref,
    own_pack,
    other_pack,
    table_sum,
    total,
    dq_out,
    dk_out,
    dv_out,
    dt_out,
    sems,
):
    pair = pl.program_id(0)
    count = keys.shape[0] // LANES
    scale = HD**-0.5
    low_scale = jnp.asarray(scale, jnp.bfloat16)
    table_sum[...] = jnp.zeros_like(table_sum)
    grads = stacked(grad[...])
    grad_weights = nt(grads, values[...])
    lows = jnp.concatenate([weights[0], weights[1]], axis=0)
    scores = backward_scores(lows.astype(jnp.float32), grad_weights)
    low_scores = scores.astype(jnp.bfloat16)
    grad_content = unstacked(nn(low_scores, keys[...])) * scale
    positions = stacked(position[...] * low_scale)
    to_position = jnp.zeros((2 * LANES, PAIR), jnp.float32)
    for block in range(count):
        rows = table_rows(order, block, count)
        lanes = slice(block * LANES, (block + 1) * LANES)
        parts = []
        for index in range(2):
            half = low_scores[index * LANES : (index + 1) * LANES, lanes]
            parts.append(unskew_pooled(half.astype(jnp.float32)).astype(jnp.bfloat16))
        parts = jnp.concatenate(parts, axis=0)
        to_position = to_position + nn(parts, table[rows, :])
        table_sum[rows, :] += tn(parts, positions)
    grad_position = unstacked(to_position) * scale
    bias_ref[...] = column_sums(grad_content, grad_position)
    slot = pair % 2
    grad_keys = tn(low_scores, stacked(content[...] * low_scale)).astype(jnp.bfloat16)
    grad_values = tn(lows, grads).astype(jnp.bfloat16)
    dq_out[slot] = (grad_content + grad_position).astype(jnp.bfloat16)
    dk_out[slot] = grad_keys
    dv_out[slot] = grad_values
    dt_out[slot] = table_sum[...].astype(jnp.bfloat16)
    outs = (dq_out, dk_out, dv_out, dt_out)
    send_pack(place, pair, (own_pack, other_pack), outs, sems)
    back = nt(grad_keys, key_weight[...]) + nt(grad_values, value_weight[...])

    @pl.when(pair == 0)
    def _():
        total[...] = back

    @pl.when(pair != 0)
    def _():
        total[...] += back

    @pl.when(pair == HEADS // 2 - 1)
    def _():
        for block in range(count):
            target = (even_ref, odd_ref)[block % 2]
            start = block // 2 * LANES
            rows = total[block * LANES : (block + 1) * LANES, :]
            target[start : start + LANES, :] = rows.astype(jnp.bfloat16)


def by_pair(shape, first=0):
    front = tuple(shape[:-1])
    zeros = (0,) * len(front)
    return pl.BlockSpec(front + (PAIR,), lambda pair: zeros + (first + pair,))


def entire(shape):
    zeros = (0,) * len(shape)
    return pl.BlockSpec(tuple(shape), lambda pair: zeros)


def of_layer(shape, layer, first):
    return pl.BlockSpec((None, shape[1], PAIR), lambda pair: (layer, 0, first + pair))


def weights_block(shape):
    return pl.BlockSpec((2,) + tuple(shape[1:]), lambda pair: (pair,) + (0,) * (len(shape) - 1))


def attention_call(micros, kernel, scalars, operands, outs, scratch, mib, follows=()):
    first = len(scalars) + len(operands)

    def run(*refs):
        kernel(*refs[:first], *refs[first + len(follows) :])

    return pl.pallas_call(
        run,
        grid=(HEADS // 2,),
        in_specs=[SMEM] * len(scalars) + [spec for _, spec in operands] + [HBM] * len(follows),
        out_specs=[HBM if spec is None else spec for _, _, spec in outs],
        out_shape=[pltpu.HBM(shape, kind) for shape, kind, _ in outs],
        scratch_shapes=scratch,
        compiler_params=pltpu.CompilerParams(vmem_limit_bytes=mib * 2**20),
        cost_estimate=lasting(micros),
    )(*scalars, *[in_hbm(array) for array, _ in operands], *[in_hbm(a) for a in follows])


def vector(vectors, row):
    gain, shift, bias, contract, expand, pool, up = vectors
    for start, ref in ((GAIN, gain), (SHIFT, shift), (BIAS, bias)):
        if start <= row < start + 6:
            layer, index = divmod(row - start, 2)
            return ref[layer].astype(jnp.float32)[index : index + 1, :]
    if row < EXPAND:
        return contract[...].astype(jnp.float32)[row - CONTRACT : row - CONTRACT + 1, :]
    if row < POOL:
        layer, part = divmod(row - EXPAND, 4)
        lanes = slice(part * D, (part + 1) * D)
        return expand[:, lanes].astype(jnp.float32)[layer : layer + 1, :]
    if row < UP:
        return pool[...].astype(jnp.float32)
    part = row - UP
    return up[:, part * D : (part + 1) * D].astype(jnp.float32)


def normalised(values):
    centre = values - jnp.mean(values, axis=1, keepdims=True)
    spread = jnp.mean(centre * centre, axis=1, keepdims=True)
    rate = lax.rsqrt(spread + epsilon)
    return centre * rate, rate


def norm_forward(values, vectors, layer, index):
    hat, _ = normalised(values)
    gain = vector(vectors, GAIN + 2 * layer + index)
    return (hat * gain + vector(vectors, SHIFT + 2 * layer + index)).astype(jnp.bfloat16)


def norm_backward(values, vectors, layer, index, grad):
    hat, rate = normalised(values)
    scaled = grad * vector(vectors, GAIN + 2 * layer + index)
    mean = jnp.mean(scaled, axis=1, keepdims=True)
    along = jnp.mean(scaled * hat, axis=1, keepdims=True)
    result = rate * (scaled - mean - hat * along)
    return result, jnp.sum(grad * hat, axis=0, keepdims=True), jnp.sum(grad, axis=0, keepdims=True)


class Copies:
    def __init__(self, sems):
        self.sems, self.used, self.open = sems, 0, []

    def start(self, source, target):
        copy = pltpu.make_async_copy(source, target, self.sems.at[self.used])
        self.used += 1
        copy.start()
        return copy

    def send(self, source, target):
        self.open.append(self.start(source, target))

    def finish(self):
        for copy in self.open:
            copy.wait()


class Output:
    def __init__(self, buffer, target, copies):
        self.buffer, self.target, self.copies, self.sent = buffer, target, copies, False
        self.shape, self.dtype = buffer.shape, buffer.dtype

    def __setitem__(self, index, value):
        self.buffer[index] = value

    def __getitem__(self, index):
        return self.buffer[index]

    def send(self, lanes=None):
        self.sent = True
        if lanes is None:
            self.copies.send(self.buffer, self.target)
        else:
            self.copies.send(self.buffer.at[:, lanes], self.target.at[:, lanes])


def write_table(frequency, first, out):
    step = 32
    count = out.shape[0]

    def waves(start, change, rows):
        distance = start + change * lax.broadcasted_iota(jnp.int32, (rows, 1), 0)
        angle = distance.astype(jnp.float32) * frequency[...]
        return jnp.sin(angle), jnp.cos(angle)

    high_sin, high_cos = waves(first, -step, count // step)
    low_sin, low_cos = waves(0, -1, step)
    for index in range(count // step):
        rows = slice(index * step, (index + 1) * step)
        sine, cosine = high_sin[index : index + 1], high_cos[index : index + 1]
        out[rows, : D // 2] = (sine * low_cos + cosine * low_sin).astype(jnp.bfloat16)
        out[rows, D // 2 :] = (cosine * low_cos - sine * low_sin).astype(jnp.bfloat16)
    out.send()


def queries(layer, normed, vectors, weight, content, position):
    value = nn(normed, weight[:, :D])
    content[...] = (value + vector(vectors, BIAS + 2 * layer)).astype(jnp.bfloat16)
    position[...] = (value + vector(vectors, BIAS + 2 * layer + 1)).astype(jnp.bfloat16)
    content.send()
    position.send()


def window_project_kernel(
    layer, inputs, vectors, embedded, w_in, content, position, keys, values, table, *more
):
    weight, copy = w_in
    rows = inputs[...]
    if more:
        normed, waves = more
        rows = norm_forward(rows.astype(jnp.float32), vectors, layer, 0)
        normed[...] = rows
        normed.send()
        write_table(embedded, WIN, waves)
        embedded = waves
    copy.wait()
    queries(layer, rows, vectors, weight, content, position)
    for index, out in ((1, keys), (2, values)):
        out[...] = nn(rows, weight[:, index * D : (index + 1) * D]).astype(jnp.bfloat16)
        out.send()
    table[...] = nn(embedded[...], weight[:, 3 * D :]).astype(jnp.bfloat16)


def third_rows(ref, start):
    rows = pl.ds(start, LANES, stride=3)
    return jnp.concatenate([ref[index, rows, :] for index in range(D // LANES)], axis=1)


def put_third_rows(ref, start, values):
    for index in range(D // LANES):
        lanes = slice(index * LANES, (index + 1) * LANES)
        ref[index, pl.ds(start, LANES, stride=3), :] = values[:, lanes]


def put_rows(ref, start, values):
    for index in range(D // LANES):
        lanes = slice(index * LANES, (index + 1) * LANES)
        ref[index, start : start + values.shape[0], :] = values[:, lanes]


def all_rows(ref):
    return jnp.concatenate([ref[index] for index in range(D // LANES)], axis=1)


def kept(info, offset):
    count = LANES
    place = info[0] + 3 * lax.broadcasted_iota(jnp.int32, (count, 1), 0) + offset
    return (place >= 2) & (document(place - 2, info) == document(place, info))


def pool_kernel(info, full, edge, vectors, w_pool, normed, inputs, grouped, moved):
    pool_weight, pool_copy = w_pool
    put_rows(moved, 8, full[...])
    put_rows(moved, 6, edge[-2:, :].astype(jnp.float32))
    parts = []
    for offset in range(3):
        rows = third_rows(moved, offset + 6)
        parts.append(jnp.where(kept(info, offset), rows, 0.0).astype(jnp.bfloat16))
        grouped[:, offset * D : (offset + 1) * D] = parts[offset]
    pool_copy.wait()
    total = vector(vectors, POOL)
    for offset in range(3):
        total = total + nn(parts[offset], pool_weight[offset * D : (offset + 1) * D, :])
    normed[...] = norm_forward(total, vectors, 1, 0)
    normed.send()
    inputs[...] = total


def pooled_project_kernel(normed, vectors, frequency, w_in, content, position, table, waves):
    weight, copy = w_in
    write_table(frequency, waves.shape[0] - LANES - 1, waves)
    copy.wait()
    queries(1, normed[...], vectors, weight, content, position)
    table[...] = nn(waves[...], weight[:, 3 * D :]).astype(jnp.bfloat16)


def feed(layer, mixed, inputs, vectors, weights, middle_ref, slope, pack):
    w_out, w_expand, w_contract = [buffer for buffer, _ in weights]
    copies = [copy for _, copy in weights]
    pack[:, :D] = mixed[...]
    copies[0].wait()
    middle = inputs[...].astype(jnp.float32) + nn(mixed[...], w_out[...])
    middle_ref[...] = middle
    middle_ref.send()
    normed_two = norm_forward(middle, vectors, layer, 1)
    pack[:, D : 2 * D] = normed_two
    pack.send(slice(0, 2 * D))
    copies[1].wait()
    copies[2].wait()
    total = middle + vector(vectors, CONTRACT + layer)
    for part in range(4):
        lanes = slice(part * D, (part + 1) * D)
        value = nn(normed_two, w_expand[:, lanes]) + vector(vectors, EXPAND + 4 * layer + part)
        below = 0.5 + 0.5 * lax.erf(value * 0.5**0.5)
        density = jnp.exp(value * value * -0.5) * (0.5 / math.pi) ** 0.5
        slope[:, lanes] = (below + value * density).astype(jnp.bfloat16)
        active = (value * below).astype(jnp.bfloat16)
        pack[:, (2 + part) * D : (3 + part) * D] = active
        slope.send(lanes)
        pack.send(slice((2 + part) * D, (3 + part) * D))
        total = total + nn(active, w_contract[lanes, :])
    return total


def window_feed_kernel(
    layer,
    mixed,
    inputs,
    vectors,
    w_out,
    w_expand,
    w_contract,
    middle,
    slope,
    pack,
    result,
    squares,
    edge,
):
    weights = (w_out, w_expand, w_contract)
    total = feed(layer, mixed, inputs, vectors, weights, middle, slope, pack)
    result[...] = total.astype(result.dtype)
    edge[...] = total[-EDGE:].astype(jnp.bfloat16)
    squares[...] = jnp.sum(total * total, axis=0, keepdims=True)


def pooled_feed_kernel(
    mixed,
    inputs,
    grouped,
    full,
    vectors,
    w_out,
    w_expand,
    w_contract,
    w_up,
    middle,
    slope,
    pack,
    next_normed,
    result,
    squares,
    spread,
):
    weights = (w_out, w_expand, w_contract)
    total = feed(1, mixed, inputs, vectors, weights, middle, slope, pack)
    squares[...] = jnp.sum(total * total, axis=0, keepdims=True)
    low = total.astype(jnp.bfloat16)
    pack[:, 6 * D : 7 * D] = low
    pack[:, 7 * D :] = grouped[...]
    pack.send(slice(6 * D, 10 * D))
    up_buffer, copy = w_up
    copy.wait()
    for offset in range(3):
        raised = nn(low, up_buffer[:, offset * D : (offset + 1) * D])
        put_third_rows(spread, offset, raised + vector(vectors, UP + offset))
    raised = full[...] + all_rows(spread)
    next_normed[...] = norm_forward(raised, vectors, 2, 0)
    next_normed.send()
    result[...] = raised


def store_halves(core, own, other, offset, values):
    half = values.shape[1] // 2
    low = values[:, :half].astype(jnp.bfloat16)
    high = values[:, half:].astype(jnp.bfloat16)
    rows = values.shape[0]

    @pl.when(core == 0)
    def _():
        own[:rows, offset : offset + half] = low
        other[:rows, offset : offset + half] = high

    @pl.when(core != 0)
    def _():
        own[:rows, offset : offset + half] = high
        other[:rows, offset : offset + half] = low


def feed_backward(
    layer,
    place,
    grad,
    slope,
    middle,
    vectors,
    w_contract,
    w_expand,
    w_out,
    middle_grad,
    mixed_grad,
    own,
    other,
    small,
):
    contract, expand, out = [weight[0] for weight in (w_contract, w_expand, w_out)]
    copies = [weight[1] for weight in (w_contract, w_expand, w_out)]
    core = place[1]
    branch = grad.astype(jnp.bfloat16)
    small[...] = jnp.zeros_like(small)
    small[0:1, :] = jnp.sum(branch.astype(jnp.float32), axis=0, keepdims=True)
    store_halves(core, own, other, 2 * D, branch)
    copies[0].wait()
    copies[1].wait()
    normed_grad = jnp.zeros(grad.shape, jnp.float32)
    changes = []
    for part in range(4):
        lanes = slice(part * D, (part + 1) * D)
        change = nt(branch, contract[lanes, :]) * slope[:, lanes].astype(jnp.float32)
        change = change.astype(jnp.bfloat16)
        changes.append(change)
        small[3 + part : 4 + part, :] = jnp.sum(
            change.astype(jnp.float32), axis=0, keepdims=True
        )
        normed_grad = normed_grad + nt(change, expand[:, lanes])
    store_halves(core, own, other, 0, jnp.concatenate(changes, axis=1))
    norm, gain, shift = norm_backward(middle[...], vectors, layer, 1, normed_grad)
    small[1:2, :] = gain
    small[2:3, :] = shift
    total = grad + norm
    middle_grad[...] = total
    attend = total.astype(jnp.bfloat16)
    store_halves(core, own, other, 2 * D + D // 2, attend)
    other.send()
    copies[2].wait()
    mixed_grad[...] = nt(attend, out[...]).astype(jnp.bfloat16)


def feed_backward_kernel(layer, place, grad, *refs):
    feed_backward(layer, place, grad[...].astype(jnp.float32), *refs)


def first_feed_backward_kernel(place, joined, shifted, came_back, *refs):
    moved = refs[-1]
    rows = shifted.shape[0]
    moved[:rows, :] = shifted[...]
    moved[rows : rows + 2, :] = came_back[:2, :]
    feed_backward(0, place, joined[...] + moved[2 : rows + 2, :], *refs[:-1])


def project_backward(layer, core, packs, rows, weight, extra, inputs, middle_grad, vectors, small):
    small[...] = jnp.zeros_like(small)
    normed_grad = extra
    for index, chosen in enumerate(rows):
        for slot in range(2):
            half = slot ^ core
            begin = pl.multiple_of(index * D + half * (D // 2), D // 2)
            grad = packs[slot][chosen, index * D // 2 : (index + 1) * D // 2]
            normed_grad = normed_grad + nt(grad, weight[:, pl.ds(begin, D // 2)])
    norm, gain, shift = norm_backward(inputs, vectors, layer, 0, normed_grad)
    small[0:1, :] = gain
    small[1:2, :] = shift
    return middle_grad[...] + norm


def window_project_backward(layer, core, packs, returned, weight, *rest):
    extra = jnp.concatenate(
        [jnp.zeros((QBLK - WIN, D), jnp.float32), returned[...].astype(jnp.float32)], axis=0
    )
    rows = (slice(0, QBLK), slice(WIN, REACH), slice(WIN, REACH))
    return project_backward(layer, core, packs, rows, weight, extra, *rest)


def first_project_backward_kernel(
    place, packs, returned, inputs, middle_grad, vectors, w_in, inputs_grad, small
):
    weight, copy = w_in
    copy.wait()
    rows = inputs[...].astype(jnp.float32)
    total = window_project_backward(
        0, place[1], packs, returned, weight, rows, middle_grad, vectors, small
    )
    inputs_grad[...] = total.astype(inputs_grad.dtype)


def last_project_backward_kernel(
    place,
    packs,
    returned,
    inputs,
    middle_grad,
    vectors,
    w_in,
    w_up,
    inputs_grad,
    short_grad,
    own,
    other,
    small,
    spread,
):
    (weight, copy), (up_weight, up_copy) = w_in, w_up
    copy.wait()
    total = window_project_backward(
        2, place[1], packs, returned, weight, inputs[...], middle_grad, vectors, small
    )
    inputs_grad[...] = total
    inputs_grad.send()
    put_rows(spread, 0, total)
    parts = [third_rows(spread, offset).astype(jnp.bfloat16) for offset in range(3)]
    up_copy.wait()
    result = jnp.zeros((LANES, D), jnp.float32)
    for offset in range(3):
        small[2 + offset : 3 + offset, :] = jnp.sum(
            parts[offset].astype(jnp.float32), axis=0, keepdims=True
        )
        result = result + nt(parts[offset], up_weight[:, offset * D : (offset + 1) * D])
    short_grad[...] = result
    joined = jnp.concatenate(parts, axis=1)
    half = 3 * D // 2
    quarter = half // 3

    def place_parts(target, values):
        for index in range(3):
            target[index * LANES : (index + 1) * LANES, :] = values[
                :, index * quarter : (index + 1) * quarter
            ]

    @pl.when(place[1] == 0)
    def _():
        place_parts(own, joined[:, :half])
        place_parts(other, joined[:, half:])

    @pl.when(place[1] != 0)
    def _():
        place_parts(own, joined[:, half:])
        place_parts(other, joined[:, :half])


def pooled_project_backward_kernel(
    info,
    place,
    packs,
    normed_grad,
    inputs,
    middle_grad,
    vectors,
    w_in,
    w_pool,
    shifted_grad,
    first_rows,
    own,
    other,
    small,
    spread,
):
    (weight, copy), (pool_weight, pool_copy) = w_in, w_pool
    copy.wait()
    total = project_backward(
        1,
        place[1],
        packs,
        (slice(0, LANES),),
        weight,
        normed_grad[...],
        inputs[...],
        middle_grad,
        vectors,
        small,
    )
    low = total.astype(jnp.bfloat16)
    small[2:3, :] = jnp.sum(low.astype(jnp.float32), axis=0, keepdims=True)
    store_halves(place[1], own, other, 0, low)
    pool_copy.wait()
    for offset in range(3):
        rows = nt(low, pool_weight[offset * D : (offset + 1) * D, :])
        put_third_rows(spread, offset, jnp.where(kept(info, offset), rows, 0.0))
    shifted_grad[...] = all_rows(spread)
    first_rows[...] = shifted_grad[:EDGE, :]


def lasting(micros):
    return pl.CostEstimate(
        flops=int(micros * 4e9), bytes_accessed=int(micros * 1.2e7), transcendentals=0
    )


class Part:
    def __init__(self, array, shape=None, place=None):
        self.array, self.place = array, place
        self.shape = tuple(shape or (array.shape if place is None else array.shape[1:]))

    def of(self, ref):
        if self.place is not None:
            return ref.at[self.place]
        if self.shape == self.array.shape:
            return ref
        return ref.at[tuple(slice(0, size) for size in self.shape)]


def whole(micros, kernel, scalars, arrays, weights, outs, scratch=(), mib=24, follows=()):
    flat, groups, parts = [], [], []
    for array in arrays:
        groups.append(len(array) if isinstance(array, tuple) else 0)
        for item in array if isinstance(array, tuple) else (array,):
            part = item if isinstance(item, Part) else Part(item, item.shape)
            flat.append(part.array)
            parts.append(part)
    shapes = [(part.shape, part.array.dtype) for part in parts]
    shapes += [(w.shape if layer is None else w.shape[1:], w.dtype) for w, layer in weights]
    shapes += list(outs) + list(scratch)
    scalar_count, flat_count, weight_count = len(scalars), len(flat), len(weights)
    sem_count = 64

    def run(*refs):
        copies = Copies(refs[-1])
        refs = list(refs[:-1])

        def take(count):
            taken, refs[:count] = refs[:count], []
            return taken

        taken = take(scalar_count)
        sources, weight_sources = take(flat_count), take(weight_count)
        take(len(follows))
        targets = take(len(outs))
        buffers, weight_buffers, out_buffers = take(flat_count), take(weight_count), take(len(outs))
        loads = [copies.start(p.of(s), b) for p, s, b in zip(parts, sources, buffers)]
        loaded = []
        for (_, layer), source, buffer in zip(weights, weight_sources, weight_buffers):
            source = source if layer is None else source.at[layer]
            loaded.append((buffer, copies.start(source, buffer)))
        for copy in loads:
            copy.wait()
        position = 0
        for size in groups:
            taken.append(buffers[position : position + size] if size else buffers[position])
            position += size or 1
        results = [Output(b, t, copies) for b, t in zip(out_buffers, targets)]
        kernel(*taken, *loaded, *results, *refs)
        for result in results:
            if not result.sent:
                result.send()
        copies.finish()

    return pl.pallas_call(
        run,
        in_specs=[SMEM] * scalar_count + [HBM] * (flat_count + weight_count + len(follows)),
        out_specs=[HBM] * len(outs),
        out_shape=[pltpu.HBM(shape, kind) for shape, kind in outs],
        scratch_shapes=[pltpu.VMEM(*item) for item in shapes]
        + [pltpu.SemaphoreType.DMA((sem_count,))],
        compiler_params=pltpu.CompilerParams(vmem_limit_bytes=mib * 2**20),
        cost_estimate=lasting(micros),
    )(*scalars, *[in_hbm(a) for a in flat + [w for w, _ in weights] + list(follows)])


def in_hbm(array):
    return pltpu.with_memory_space_constraint(array, pltpu.HBM)


def crossed(block, axis, bit):
    count = lax.axis_size(axis)
    return lax.ppermute(block, axis, [(index, index ^ bit) for index in range(count)])


def passed_along(block, axis, distance):
    devices = range(lax.axis_size(axis))
    route = [(i - distance, i) for i in devices if i - distance in devices]
    return lax.ppermute(block, axis, route)


def both(low, high, bit):
    return jnp.where(bit, high, low), jnp.where(bit, low, high)


def rounded_sum(*terms):
    return sum(term.astype(jnp.float32) for term in terms).astype(jnp.bfloat16)


def gather_pooled(rows):
    half = rows.shape[0] // 2
    from_x = crossed(rows, "seq", 2)
    from_y = crossed(rows, "seq", 4)
    from_core = crossed(rows, "seq", 1)
    first = crossed(from_x[:half], "seq", 4)
    second = crossed(from_y[half:], "seq", 2)
    core_x = crossed(from_x, "seq", 1)
    core_y = crossed(from_y, "seq", 1)
    opposite = jnp.concatenate([first, second], axis=0)
    core_opposite = crossed(opposite, "seq", 1)
    return jnp.concatenate(
        [rows, from_core, from_x, core_x, from_y, core_y, opposite, core_opposite], axis=0
    )


def scatter_pooled(even, odd, meanwhile):
    arrived = crossed(odd, "seq", 1)
    total = rounded_sum(even, arrived).reshape(4, LANES, D)
    made = meanwhile(total)
    left, right = total[:, :, : D // 2], total[:, :, D // 2 :]
    left_arrived = crossed(jnp.stack([left[1], left[3]]), "seq", 2)
    right_arrived = crossed(right[2:], "seq", 4)
    (left_arrived, right_arrived), _ = together((left_arrived, right_arrived), made)
    left_next = crossed(rounded_sum(left[2], left_arrived[1]), "seq", 4)
    right_next = crossed(rounded_sum(right[1], right_arrived[1]), "seq", 2)

    def added(*terms):
        return sum(term.astype(jnp.float32) for term in terms)

    total = jnp.concatenate(
        [
            added(left[0], left_arrived[0], left_next),
            added(right[0], right_arrived[0], right_next),
        ],
        axis=1,
    )
    return total, made


class Piece:
    def __init__(self, features, halves, reads, compute):
        self.height, self.halves, self.reads, self.compute = features // 4, halves, reads, compute
        self.lanes = sum(features // D * half // 2 for half in halves)


def plain_piece(x, first, features, dy, start, half):
    def compute(refs, chosen):
        return [sum(tn(a[:, chosen], b[...]) for a, b in zip(refs[x], refs[dy]))]

    return Piece(features, [half], {x: (first, features), dy: (start, half)}, compute)


def table_part(embedded, grads, chosen):
    rows = embedded.shape[0]
    lanes = slice(3 * D // 2, 2 * D)
    summed = sum(grad[:rows, lanes].astype(jnp.float32) for grad in grads)
    return tn(embedded[:, chosen], summed.astype(jnp.bfloat16))


def window_piece(normed, grads, table):
    def compute(refs, chosen):
        totals = []
        for index, (rows, grad_rows) in enumerate(
            ((slice(WIN, REACH), slice(0, QBLK)),) + ((slice(0, REACH),) * 2,) * 2
        ):
            lanes = slice(index * D // 2, (index + 1) * D // 2)
            totals.append(
                sum(
                    tn(features[rows, chosen], grad[grad_rows, lanes])
                    for features, grad in zip(refs[normed], refs[grads])
                )
            )
        return totals + [table_part(refs[table][0], refs[grads], chosen)]

    return Piece(D, [D // 2] * 4, {normed: (0, D), grads: (0, 2 * D), table: (0, D)}, compute)


def pooled_piece(normed, grads, table):
    def compute(refs, chosen):
        (features,) = refs[normed]
        own, pair = refs[grads]
        count = features.shape[0] // LANES
        lanes = slice(0, D // 2)
        query = sum(
            tn(features[index * LANES : (index + 1) * LANES, chosen], grad[:LANES, lanes])
            for index, grad in enumerate((own, pair))
        )
        totals = [query]
        for index in (1, 2):
            lanes = slice(index * D // 2, (index + 1) * D // 2)
            parts = []
            for block in range(count):
                near, far = block * LANES, (block ^ 1) * LANES
                parts.append(
                    rounded_sum(own[near : near + LANES, lanes], pair[far : far + LANES, lanes])
                )
            totals.append(tn(features[:, chosen], jnp.concatenate(parts, axis=0)))
        return totals + [table_part(refs[table][0], refs[grads], chosen)]

    return Piece(D, [D // 2] * 4, {normed: (0, D), grads: (0, 2 * D), table: (0, D)}, compute)


def upsample_piece(x, first, dy):
    def compute(refs, chosen):
        parts = []
        for index in range(3):
            rows = slice(index * LANES, (index + 1) * LANES)
            parts.append(sum(tn(a[:, chosen], b[rows, :]) for a, b in zip(refs[x], refs[dy])))
        return [jnp.concatenate(parts, axis=1)]

    return Piece(D, [3 * D // 2], {x: (first, D), dy: (0, D // 2)}, compute)


def pair_gradients(micros, place, sources, pieces, follows, natural=False):
    lanes = sum(piece.lanes for piece in pieces)
    flat, first = [], {}
    for name, arrays in sources.items():
        first[name] = len(flat)
        flat.extend(arrays)
    buffers = []
    for piece in pieces:
        for name, (_, width) in piece.reads.items():
            for array in sources[name]:
                buffers.append(pltpu.VMEM((array.shape[-2], width), array.dtype))
    count = len(flat)
    out = (2, LANES, lanes)
    shapes = [(4, LANES, 2 * lanes)] if natural else [out] * 4
    total_outs = len(shapes)

    def kernel(place, *refs):
        arrays = refs[:count]
        refs = refs[count + len(follows) :]
        targets, spaces, sems = refs[:total_outs], list(refs[total_outs : -1 - total_outs]), refs[-1]
        copies = Copies(sems)
        results = refs[-1 - total_outs : -1]
        ready = []
        for piece in pieces:
            inputs, loads = {}, []
            for name, (start, width) in piece.reads.items():
                inputs[name] = []
                for index in range(len(sources[name])):
                    source = arrays[first[name] + index]
                    space = spaces.pop(0)
                    if len(source.shape) == 3:
                        source = source.at[0]
                    if width != source.shape[1]:
                        source = source.at[:, start : start + width]
                    loads.append(copies.start(source, space))
                    inputs[name].append(space)
            ready.append((inputs, loads))
        offset = 0
        for piece, (inputs, loads) in zip(pieces, ready):
            for load in loads:
                load.wait()
            groups = piece.height // LANES
            for block in range(4):
                chip = block if natural else place[0] ^ block
                begin = chip * piece.height
                if not natural:
                    begin = pl.multiple_of(begin, LANES)
                totals = piece.compute(inputs, pl.ds(begin, piece.height))
                position = offset
                for total in totals:
                    total = total.astype(jnp.bfloat16)
                    quarter = total.shape[1] // 2
                    halves = (total[:, :quarter], total[:, quarter:])
                    for index, part in enumerate(halves):
                        if natural:
                            space, slot, lane = results[0], block, position + index * lanes
                        else:
                            which = (block % 2, block // 2)[index]
                            space, slot, lane = results[2 * index + which], block // 2, position
                            if index == 1:
                                slot = block % 2
                        if groups == 1:
                            space[slot, :, lane : lane + quarter] = part
                            continue
                        for group in range(groups):
                            start = lane + quarter * group
                            low = HD * group
                            high = piece.height // 2 + low
                            space[slot, :HD, start : start + quarter] = part[low : low + HD]
                            space[slot, HD:, start : start + quarter] = part[high : high + HD]
                    position += quarter * groups
            for begin in (offset, offset + lanes) if natural else (offset,):
                done = slice(begin, begin + piece.lanes)
                for space, target in zip(results, targets):
                    copies.send(space.at[:, :, done], target.at[:, :, done])
            offset += piece.lanes
        copies.finish()

    return pl.pallas_call(
        kernel,
        in_specs=[SMEM] + [ANY] * count + [HBM] * len(follows),
        out_specs=[HBM] * total_outs,
        out_shape=[pltpu.HBM(shape, jnp.bfloat16) for shape in shapes],
        scratch_shapes=buffers
        + [pltpu.VMEM(shape, jnp.bfloat16) for shape in shapes]
        + [pltpu.SemaphoreType.DMA((64,))],
        compiler_params=pltpu.CompilerParams(vmem_limit_bytes=32 * 2**20),
        cost_estimate=lasting(micros),
    )(place, *flat, *[in_hbm(a) for a in follows])


def first_step(keep_one, send_one, keep_two, send_two):
    return keep_one, crossed(send_one, "seq", 2), keep_two, crossed(send_two, "seq", 4)


def first_sums(*groups):
    parts = [[], [], [], []]
    for keep_one, one, keep_two, two in groups:
        for index in range(2):
            parts[index].append(rounded_sum(keep_one[index], one[index]))
            parts[2 + index].append(rounded_sum(keep_two[index], two[index]))
    return tuple(jnp.concatenate(part, axis=1) for part in parts)


def second_step(one, send_one, two, send_two):
    return one, crossed(send_one, "seq", 4), two, crossed(send_two, "seq", 2)


def second_sums(one, add_one, two, add_two):
    return rounded_sum(one, add_one), rounded_sum(two, add_two)


def depth_halves(first, second, depth):
    keep, send = both(first, second, depth)
    return keep, crossed(send, "dp", 1)


def depth_quarters(keep, arrived):
    keep = rounded_sum(keep, arrived)
    return keep, crossed(keep, "dp", 2)


def depth_back(keep, arrived):
    keep = rounded_sum(keep, arrived)
    return keep, crossed(keep, "dp", 1)


def depth_share(keep, other, depth):
    return jnp.concatenate(both(keep, other, depth), axis=1)


def core_rows(share, core):
    keep, send = both(share[:HD], share[HD:], core)
    return keep, crossed(send, "seq", 1)


def together(*groups):
    return lax.optimization_barrier(tuple(tuple(group) for group in groups))


def final_kernel(plan, place, *refs):
    groups = len(plan)
    buffers, outs = refs[: 2 * groups], refs[2 * groups :]
    for index, pieces in enumerate(plan):
        mine, other = buffers[2 * index : 2 * index + 2]
        lanes = mine.shape[1] // 2
        offset = 0
        for out_index, layer, first_column, columns, height in pieces:
            out = outs[out_index]
            quarter = columns // 4
            for group in range(height // HD):
                rows = slice(HD * group, HD * (group + 1))
                for part in range(4):
                    start = (part % 2) * lanes + offset
                    chosen = slice(start, start + quarter)
                    value = jnp.where(place[1] == part // 2, mine[:, chosen], other[:, chosen])
                    begin = first_column + part * quarter
                    where = (rows, slice(begin, begin + quarter))
                    out[where if layer is None else (layer, *where)] = value.astype(jnp.float32)
                offset += quarter


def final_outputs(place, plan, buffers, shapes):
    flat = [array for pair in buffers for array in pair]
    outs = [(shape, jnp.float32) for shape in shapes]
    return whole(3, partial(final_kernel, plan), [place], flat, [], outs, mib=32)


def summed_everywhere(flat):
    for axis in ("seq", "dp"):
        for bit in range(lax.axis_size(axis).bit_length() - 1):
            flat = flat + crossed(flat, axis, 1 << bit)
    return flat


def outer_float(first_matrix, second_matrix):
    return jnp.einsum("rc,re->ce", first_matrix, second_matrix, preferred_element_type=jnp.float32)


BF, FL = jnp.bfloat16, jnp.float32


def window_project(layer, inputs, vectors, embedded, w_in, first):
    one = (inputs.shape, BF)
    outs = [one, one, one, one, ((QBLK, D), BF)] + [one, ((QBLK, D), BF)] * first
    return whole(
        4,
        partial(window_project_kernel, layer),
        [],
        [inputs, vectors, embedded],
        [(w_in, layer)],
        outs,
    )


def window_attention(layer, raw, info, heads, border, vectors, w_in, table):
    rows = heads[0].shape[0]
    operands = [(a, by_pair(a.shape)) for a in heads]
    operands += [(a, entire(a.shape)) for a in (border, vectors[0], vectors[1])]
    operands += [(w_in, of_layer(w_in.shape, layer, first)) for first in (4, 8)]
    operands.append((table, by_pair(table.shape)))
    weights = (HEADS, PARTS, LANES, SEEN)
    pair_border = (2, WIN, D)
    outs = [
        ((rows, D), BF, by_pair((rows, D))),
        (border.shape, BF, entire(border.shape)),
        (pair_border, BF, by_pair(pair_border)),
        (weights, BF, weights_block(weights)),
    ]
    scratch = [
        pltpu.VMEM((PARTS, LANES, SEEN), FL),
        pltpu.VMEM(border.shape, BF),
        pltpu.VMEM((2 * rows, SEEN), FL),
    ]
    kernel = partial(window_forward_kernel, layer if raw else None)
    return attention_call(11, kernel, [info], operands, outs, scratch, 20)


def window_attention_back(
    layer, place, heads, border, w_in, table, weights, grad, follows=()
):
    rows = heads[0].shape[0]
    operands = [(a, by_pair(a.shape)) for a in (*heads, border)]
    operands += [(w_in, of_layer(w_in.shape, layer, first)) for first in (4, 8)]
    operands += [(table, by_pair(table.shape)), (weights, weights_block(weights.shape))]
    operands.append((grad, by_pair(grad.shape)))
    outs = [
        ((2, D), FL, by_pair((2, D))),
        ((WIN, D), BF, entire((WIN, D))),
        ((REACH, 2 * D), BF, None),
        ((REACH, 2 * D), BF, None),
    ]
    scratch = [pltpu.VMEM((REACH, PAIR), FL)] * 2
    scratch += [pltpu.VMEM((WIN, D), FL), pltpu.VMEM((2 * rows, SEEN), BF)]
    scratch += [pltpu.VMEM((2, size, PAIR), BF) for size in (rows, REACH, REACH, table.shape[0])]
    scratch.append(pltpu.SemaphoreType.DMA((2, 4)))
    return attention_call(
        13, window_backward_kernel, [place], operands, outs, scratch, 20, follows
    )


def pooled_attention(info, order, content, position, normed, w_in, table):
    rows, total = content.shape[0], normed.shape[0]
    operands = [(a, by_pair(a.shape)) for a in (content, position)]
    operands.append((normed, entire(normed.shape)))
    operands += [(w_in, of_layer(w_in.shape, 1, first)) for first in (4, 8)]
    operands.append((table, by_pair(table.shape)))
    weights = (HEADS, LANES, total)
    outs = [
        ((rows, D), BF, by_pair((rows, D))),
        ((total, D), BF, by_pair((total, D))),
        ((total, D), BF, by_pair((total, D))),
        (weights, BF, weights_block(weights)),
    ]
    scratch = [
        pltpu.VMEM((total // LANES, LANES, LANES), FL),
        pltpu.VMEM((2 * rows, table.shape[0]), FL),
    ]
    mib = 10 + total // LANES * 3 // 2
    return attention_call(13, pooled_forward_kernel, [info, order], operands, outs, scratch, mib)


def pooled_attention_back(order, place, heads, w_in, table, weights, grad, follows):
    rows, total = heads[0].shape[0], heads[2].shape[0]
    operands = [(a, by_pair(a.shape)) for a in heads]
    operands += [(w_in, of_layer(w_in.shape, 1, first)) for first in (4, 8)]
    operands += [(table, by_pair(table.shape)), (weights, weights_block(weights.shape))]
    operands.append((grad, by_pair(grad.shape)))
    half = ((total // LANES + 1) // 2 * LANES, D)
    outs = [
        ((2, D), FL, by_pair((2, D))),
        (half, BF, entire(half)),
        (half, BF, entire(half)),
        ((table.shape[0], 2 * D), BF, None),
        ((table.shape[0], 2 * D), BF, None),
    ]
    scratch = [pltpu.VMEM((table.shape[0], PAIR), FL), pltpu.VMEM((total, D), FL)]
    scratch += [pltpu.VMEM((2, size, PAIR), BF) for size in (rows, total, total, table.shape[0])]
    scratch.append(pltpu.SemaphoreType.DMA((2, 4)))
    mib = 10 + total // LANES * 3 // 2
    return attention_call(
        13, pooled_backward_kernel, [order, place], operands, outs, scratch, mib, follows
    )


def window_feed(layer, mixed, inputs, vectors, weights, kind, follows=()):
    rows = mixed.shape[0]
    outs = [
        ((rows, D), FL),
        ((rows, 4 * D), BF),
        ((rows, 6 * D), BF),
        ((rows, D), kind),
        ((1, D), FL),
        ((EDGE, D), BF),
    ]
    return whole(
        7,
        partial(window_feed_kernel, layer),
        [],
        [mixed, inputs, vectors],
        [(w, layer) for w in weights],
        outs,
        follows=follows,
    )


def feed_back(kernel, layer, place, arrays, rows, weights, extra=(), follows=()):
    outs = [((rows, D), FL), ((rows, D), BF), ((rows, 3 * D), BF), ((rows, 3 * D), BF)]
    outs.append(((8, D), FL))
    return whole(
        8, kernel, [place], arrays, [(w, layer) for w in weights], outs, extra, follows=follows
    )


def first_lanes(arrays, rows, lanes):
    return tuple(Part(array, (rows, lanes)) for array in arrays)


def per_device(
    tokens,
    doc_lengths,
    cotangent,
    norm_gain,
    norm_shift,
    relative_bias,
    attention_in,
    attention_out,
    expand_weight,
    expand_bias,
    contract_weight,
    contract_bias,
    pool_weight,
    pool_bias,
    upsample_weight,
    upsample_bias,
):
    def by_layer(weight):
        return jnp.transpose(weight, (1, 0, 2))

    w_in, w_out = by_layer(attention_in), by_layer(attention_out)
    w_expand, w_contract = by_layer(expand_weight), by_layer(contract_weight)
    ff_weights = [w_out, w_expand, w_contract]
    vectors = (norm_gain, norm_shift, relative_bias, contract_bias, expand_bias)
    vectors += (pool_bias[None], upsample_bias[None])

    inputs = tokens[0]
    rows = inputs.shape[0]
    pooled_rows = rows // 3
    device = lax.axis_index("seq").astype(jnp.int32)
    seq_count = lax.axis_size("seq")
    usual = seq_count == 8 and lax.axis_size("dp") == 4
    core_index = device % 2
    core = core_index == 1
    depth = lax.axis_index("dp") % 2 == 1
    place = jnp.stack([device // 2, core_index])
    cores = [[core + chip for chip in range(0, seq_count, 2)] for core in range(2)]
    document = jnp.arange(DOCS)
    ends = jnp.sum(jnp.where(document[None] <= document[:, None], doc_lengths, 0), axis=1)
    info = jnp.concatenate([(device * rows)[None], ends]).astype(jnp.int32)
    pooled_info = jnp.concatenate([(device * pooled_rows)[None], ends]).astype(jnp.int32)
    order = jnp.arange(seq_count, dtype=jnp.int32)
    if usual:
        order = order ^ device
    order = jnp.concatenate([order, device[None]])
    frequency = jnp.power(10000.0, -2.0 * jnp.arange(D // 2, dtype=FL) / D)[None]

    def swapped(array):
        return (array, crossed(array, "seq", 1)) if usual else array

    def swapped_halves(own, other):
        return (own, crossed(other, "seq", 1)) if usual else (own, other)

    border0 = passed_along(inputs[rows - WIN :], "seq", 1)
    *heads0, table0, normed0, near_table = window_project(
        0, inputs, vectors, frequency, w_in, True
    )
    mixed0, edge_normed0, border0, weights0 = window_attention(
        0, True, info, heads0, border0, vectors, w_in, table0
    )
    middle0, slope0, pack0, full0, squares0, edge = window_feed(
        0, mixed0, inputs, vectors, ff_weights, FL
    )
    edge = passed_along(edge, "seq", 1)
    x0, n0 = swapped(pack0), swapped(jnp.concatenate([edge_normed0, normed0], axis=0))

    one = ((pooled_rows, D), BF)
    spread = ((D // LANES, rows, LANES), FL)
    normed1, inputs1, grouped = whole(
        4,
        pool_kernel,
        [info],
        [full0, edge, vectors],
        [(pool_weight, None)],
        [one, ((pooled_rows, D), FL), ((pooled_rows, 3 * D), BF)],
        [((D // LANES, rows + 8, LANES), FL)],
    )
    far_shape = (((seq_count + 1) * pooled_rows, D), BF)
    if usual:
        normed1_all = gather_pooled(normed1)
    else:
        normed1_all = lax.all_gather(normed1, "seq", axis=0, tiled=True)
    content1, position1, table1, far_table = whole(
        4,
        pooled_project_kernel,
        [],
        [normed1, vectors, frequency],
        [(w_in, 1)],
        [one, one, far_shape, far_shape],
    )
    mixed1, keys1, values1, weights1 = pooled_attention(
        pooled_info, order, content1, position1, normed1_all, w_in, table1
    )
    middle1, slope1, pack1, normed2, inputs2, squares1 = whole(
        7,
        pooled_feed_kernel,
        [],
        [mixed1, inputs1, grouped, full0, vectors],
        [(w, 1) for w in ff_weights] + [(upsample_weight, None)],
        [
            ((pooled_rows, D), FL),
            ((pooled_rows, 4 * D), BF),
            ((pooled_rows, 10 * D), BF),
            ((rows, D), BF),
            ((rows, D), FL),
            ((1, D), FL),
        ],
        [spread],
        follows=(x0[1], n0[1]) if usual else (),
    )

    border2 = passed_along(normed2[rows - WIN :], "seq", 1)
    *heads2, table2 = window_project(2, normed2, vectors, near_table, w_in, False)
    mixed2, edge_normed2, border2, weights2 = window_attention(
        2, False, info, heads2, border2, vectors, w_in, table2
    )
    x1, n2 = swapped(pack1), swapped(jnp.concatenate([edge_normed2, normed2], axis=0))
    middle2, slope2, pack2, output, squares2, _ = window_feed(
        2, mixed2, inputs2, vectors, ff_weights, BF, x1[1:] if usual else ()
    )

    share = D // seq_count
    shapes = [
        (3, share, 4 * D),
        (3, share, D),
        (3, share, 4 * D),
        (3, 4 * share, D),
        (3 * share, D),
        (share, 3 * D),
    ]

    every = {}

    def feed_pieces(x, dy, layer):
        pieces = [
            plain_piece(x, D, D, dy, 0, 2 * D),
            plain_piece(x, 2 * D, 4 * D, dy, 2 * D, D // 2),
            plain_piece(x, 0, D, dy, 2 * D + D // 2, D // 2),
        ]
        targets = [
            (2, layer, 0, 4 * D, share),
            (3, layer, 0, D, 4 * share),
            (1, layer, 0, D, share),
        ]
        return pieces, targets

    def project_targets(layer):
        return [(0, layer, index * D, D, share) for index in range(4)]

    feed2 = feed_pieces("x2", "a2", 2)
    project2 = [window_piece("n2", "b2", "near")], project_targets(2)
    up = [upsample_piece("x1", 6 * D, "u2")], [(5, None, 0, 3 * D, share)]
    feed1 = feed_pieces("x1", "a1", 1)
    project1 = [pooled_piece("n1", "b1", "far")], project_targets(1)
    pool = [plain_piece("x1", 7 * D, 3 * D, "p1", 0, D // 2)], [(4, None, 0, D, 3 * share)]
    feed0 = feed_pieces("x0", "a0", 0)
    project0 = [window_piece("n0", "b0", "near")], project_targets(0)

    def gradients(names, follows, *parts, natural=False):
        if not usual:
            return ()
        pieces = sum((part[0] for part in parts), [])
        sources = {name: every[name] for name in names}
        return tuple(pair_gradients(7, place, sources, pieces, follows, natural))

    def step(function, values, *options):
        return tuple(function(*values, *options)) if usual else ()

    back_weights = [w_contract, w_expand, w_out]
    x2 = swapped(pack2)
    every["near"], every["far"] = (near_table,), (far_table,)
    every["x0"], every["x1"], every["x2"] = x0, x1, x2
    every["n0"], every["n1"], every["n2"] = n0, (normed1_all,), n2

    middle_grad2, mixed_grad2, own_a2, other_a2, small_a2 = feed_back(
        partial(feed_backward_kernel, 2),
        2,
        place,
        [cotangent[0], slope2, middle2, vectors],
        rows,
        back_weights,
    )
    every["a2"] = swapped_halves(own_a2, other_a2)
    bias2, leaving2, *grads2 = window_attention_back(
        2, place, heads2, border2, w_in, table2, weights2, mixed_grad2, (x2[1], n2[1]) if usual else ()
    )
    returned2 = passed_along(leaving2, "seq", -1)
    every["b2"] = swapped_halves(*grads2)
    sent2 = gradients(
        ("a2", "x2", "b2", "n2", "near"), (bias2,), feed2, project2, natural=True
    )
    joined, short_grad, own_u2, other_u2, small_b2 = whole(
        6,
        last_project_backward_kernel,
        [place],
        [first_lanes(grads2, REACH, 3 * D // 2), returned2, inputs2, middle_grad2, vectors],
        [(w_in, 2), (upsample_weight, None)],
        [
            ((rows, D), FL),
            ((pooled_rows, D), FL),
            ((rows, D // 2), BF),
            ((rows, D // 2), BF),
            ((8, D), FL),
        ],
        [spread],
        follows=sent2[:1],
    )
    every["u2"] = swapped_halves(own_u2, other_u2)

    middle_grad1, mixed_grad1, own_a1, other_a1, small_a1 = feed_back(
        partial(feed_backward_kernel, 1),
        1,
        place,
        [short_grad, slope1, middle1, vectors],
        pooled_rows,
        back_weights,
    )
    every["a1"] = swapped_halves(own_a1, other_a1)
    if usual:
        share2 = sent2[0].reshape(4 * LANES, -1)
        share2 = lax.psum_scatter(
            share2, "seq", scatter_dimension=0, tiled=True, axis_index_groups=cores
        )
        follows0 = (share2,)
        share2 = lax.psum(share2, "dp")
    else:
        follows0 = ()
    heads1 = (content1, position1, keys1, values1)
    bias1, even, odd, *grads1 = pooled_attention_back(
        order, place, heads1, w_in, table1, weights1, mixed_grad1, ()
    )
    every["b1"] = swapped_halves(*grads1)

    def group1_gradients(total):
        return gradients(("a1", "x1", "u2"), (total,), up, feed1)

    if usual:
        normed_grad1, group1 = scatter_pooled(even, odd, group1_gradients)
    else:
        group1 = ()
        split = (seq_count // 2, 1, LANES, D)
        summed = jnp.concatenate([even.reshape(split), odd.reshape(split)], axis=1)
        summed = summed.reshape(seq_count * LANES, D)
        normed_grad1 = lax.psum_scatter(summed, "seq", scatter_dimension=0, tiled=True).astype(FL)
    (normed_grad1,), group1 = together((normed_grad1,), group1)
    group1 = step(first_step, group1)
    shifted_grad, first_rows, own_p1, other_p1, small_b1 = whole(
        5,
        pooled_project_backward_kernel,
        [info, place],
        [first_lanes(grads1, LANES, D // 2), normed_grad1, inputs1, middle_grad1, vectors],
        [(w_in, 1), (pool_weight, None)],
        [
            ((rows, D), FL),
            ((EDGE, D), FL),
            ((pooled_rows, D // 2), BF),
            ((pooled_rows, D // 2), BF),
            ((8, D), FL),
        ],
        [spread],
        follows=follows0,
    )
    every["p1"] = swapped_halves(own_p1, other_p1)
    came_back = passed_along(first_rows, "seq", -1)
    group1b = gradients(("p1", "x1", "b1", "n1", "far"), (small_b1,), pool, project1)
    (came_back,), group1b = together((came_back,), group1b)
    group1b = step(first_step, group1b)
    middle_grad0, mixed_grad0, own_a0, other_a0, small_a0 = feed_back(
        first_feed_backward_kernel,
        0,
        place,
        [joined, shifted_grad, came_back, slope0, middle0, vectors],
        rows,
        back_weights,
        [((rows + 8, D), FL)],
    )
    every["a0"] = swapped_halves(own_a0, other_a0)
    (mixed_grad0,), group1, group1b = together((mixed_grad0,), group1, group1b)
    group1 = step(first_sums, (group1, group1b))
    (mixed_grad0,), group1 = together((mixed_grad0,), group1)
    group1 = step(second_step, group1)
    bias0, leaving0, *grads0 = window_attention_back(
        0, place, heads0, border0, w_in, table0, weights0, mixed_grad0
    )
    every["b0"] = swapped_halves(*grads0)
    returned0 = passed_along(leaving0, "seq", -1)

    follows = ()
    if usual:
        group0 = gradients(("a0", "x0"), (bias0,), feed0)
        last = gradients(("b0", "n0", "near"), group0[:1], project0)
        last_sent = last[0]
        group0 = step(first_step, group0)
        last = step(first_step, last)
        group1 = step(second_sums, group1)
        group1 = step(depth_halves, group1, depth)
        group1 = step(depth_quarters, group1)
        follows = (last_sent, share2, group1[0])
    tokens_grad, small_b0 = whole(
        5,
        first_project_backward_kernel,
        [place],
        [first_lanes(grads0, REACH, 3 * D // 2), returned0, inputs, middle_grad0, vectors],
        [(w_in, 0)],
        [((rows, D), BF), ((8, D), FL)],
        follows=follows,
    )
    small = jnp.concatenate(
        [
            small_b0[:2],
            small_b1[:3],
            small_b2[:5],
            small_a0[:7],
            small_a1[:7],
            small_a2[:7],
            bias0,
            bias1,
            bias2,
            squares0,
            squares1,
            squares2,
        ],
        axis=0,
    )
    if usual:
        clock = (small_b0,)
        small = small + crossed(small, "seq", 1)
        clock, (small,), group0 = together(clock, (small,), group0)
        group0 = step(first_sums, (group0,))
        group0 = step(second_step, group0)
        small = small + crossed(small, "seq", 2)
        clock, (small,), last = together(clock, (small,), last)
        last = step(first_sums, (last,))
        last = step(second_step, last)
        small = small + crossed(small, "seq", 4)
        clock, (small,), group0, group1 = together(clock, (small,), group0, group1)
        group0 = step(second_sums, group0)
        group0 = step(depth_halves, group0, depth)
        group1 = step(depth_back, group1)
        clock, last = together(clock, last)
        last = step(second_sums, last)
        last = step(depth_halves, last, depth)
        clock, group0 = together(clock, group0)
        group0 = step(depth_quarters, group0)
        clock, last, group1 = together(clock, last, group1)
        last = step(depth_quarters, last)
        small = small + crossed(small, "dp", 1)
        clock, (small,), group0 = together(clock, (small,), group0)
        group0 = step(depth_back, group0)
        clock, last = together(clock, last)
        last = step(depth_back, last)
        small = small + crossed(small, "dp", 2)
        plan = [feed2[1] + project2[1], up[1] + feed1[1] + pool[1] + project1[1]]
        plan += [feed0[1], project0[1]]
        shares = [share2] + [depth_share(*group, depth) for group in (group1, group0, last)]
        buffers = [core_rows(share, core) for share in shares]
        sums = final_outputs(place, plan, buffers, shapes)
    else:
        small = summed_everywhere(small)
        sums = plain_sums(
            shapes,
            core,
            (pack0, pack1, pack2),
            (every["n0"], normed1, every["n2"]),
            (every["n0"], normed1_all, every["n2"]),
            (every["a0"], every["a1"], every["a2"]),
            (grads0, grads1, grads2),
            every["p1"],
            every["u2"],
            (near_table, far_table),
        )
    in_grad, out_grad, expand_grad, contract_grad = [by_layer(total) for total in sums[:4]]

    gain, shift, expand_sum, contract_sum = [], [], [], []
    for layer, b in enumerate((0, 2, 5)):
        a = 10 + 7 * layer
        gain.append(jnp.stack([small[b], small[a + 1]]))
        shift.append(jnp.stack([small[b + 1], small[a + 2]]))
        contract_sum.append(small[a])
        expand_sum.append(small[a + 3 : a + 7].reshape(4 * D))
    bias_sum = small[31:37].reshape(3, 2, D)
    whole_rows = lax.axis_size("dp") * seq_count * rows * D
    counts = jnp.array([whole_rows, whole_rows // 3, whole_rows], FL)
    rms = jnp.sqrt(jnp.sum(small[37:40], axis=1) / counts)
    return (
        output[None],
        tokens_grad[None],
        jnp.stack(gain),
        jnp.stack(shift),
        bias_sum,
        in_grad,
        out_grad,
        expand_grad,
        jnp.stack(expand_sum),
        contract_grad,
        jnp.stack(contract_sum),
        sums[4],
        small[4],
        sums[5],
        small[7:10].reshape(3 * D),
        rms,
    )


def plain_sums(
    shapes, core, packs, normed, normed_all, a_pairs, grads, pool_pair, up_pair, tables
):
    def full(pair, start, half):
        own, other = (array[:, start : start + half] for array in pair)
        return jnp.concatenate(both(own, other, core), axis=1)

    def summed(features, grad):
        total = outer_float(features, grad).astype(BF)
        total = lax.psum_scatter(total, "seq", scatter_dimension=0, tiled=True)
        return lax.psum(total, "dp").astype(FL)

    into, out, expand, contract = [], [], [], []
    for layer in range(3):
        x, a, b = packs[layer], a_pairs[layer], grads[layer]
        table, near, every = tables[layer % 2], normed[layer], normed_all[layer]
        own = x.shape[0]
        near = near[near.shape[0] - own :]
        columns = [
            summed(near, full(b, 0, D // 2)[:own]),
            summed(every, full(b, D // 2, D // 2)[: every.shape[0]]),
            summed(every, full(b, D, D // 2)[: every.shape[0]]),
            summed(table, full(b, 3 * D // 2, D // 2)[: table.shape[0]]),
        ]
        into.append(jnp.concatenate(columns, axis=1))
        out.append(summed(x[:, :D], full(a, 2 * D + D // 2, D // 2)))
        expand.append(summed(x[:, D : 2 * D], full(a, 0, 2 * D)))
        contract.append(summed(x[:, 2 * D : 6 * D], full(a, 2 * D, D // 2)))
    pool = summed(packs[1][:, 7 * D :], full(pool_pair, 0, D // 2))
    sides = []
    for array in up_pair:
        parts = [array[index * LANES : (index + 1) * LANES] for index in range(3)]
        sides.append(jnp.concatenate(parts, axis=1))
    up = summed(packs[1][:, 6 * D : 7 * D], jnp.concatenate(both(*sides, core), axis=1))
    stacks = [jnp.stack(parts) for parts in (into, out, expand, contract)]
    return stacks + [pool, up]


def solution(mesh):
    rows = P("dp", "seq", None)
    in_specs = (rows, P("dp", None), rows) + (P(),) * 13
    split = P("seq", None, None)
    flat = P("seq", None)
    out_specs = (rows, rows, P(), P(), P(), split, split, split, P(), split, P())
    out_specs += (flat, P(), flat, P(), P())
    return jax.shard_map(
        per_device, mesh=mesh, in_specs=in_specs, out_specs=out_specs, check_vma=False
    )
```
